256 devices in a mesh: patch: 16 (over y, x), span: 8 (over z), wall: 2 (over core).
Axes of the slice: x: 4, y: 4, z: 8, core: 2. Of those that a mesh axis runs over, the one named last changes fastest.
Arguments:
- rhs: float32 [32, 16, 5, 16384], P('span', 'wall', None, 'patch'), may hold values from -24 to 24
- jac: float32 [32, 16, 5, 5, 16384], P('span', 'wall', None, None, 'patch'), may hold values from -2 to 24
- jac_inv: float32 [32, 16, 5, 5, 16384], P('span', 'wall', None, None, 'patch'), may hold values from -0.04 to 0.13
- wall_coupling: float32 [5, 5], replicated, may hold values from -1.2 to 1.2
- span_coupling: float32 [5, 5], replicated, may hold values from -1.2 to 1.2
- block_owner: int32 [32, 16, 128], P('span', 'wall', 'patch'), may hold values from 0 to 15, as said below
- block_slot: int32 [32, 16, 128], P('span', 'wall', 'patch'), may hold values from 0 to 3
- coarse_inv: float32 [8, 2, 5, 10, 64], P('span', 'wall', None, None, 'patch'), may hold values from -0.045 to 0.045
Outputs:
- solution: float32 [32, 16, 5, 16384], P('span', 'wall', None, 'patch')
The draws below stay inside these ranges and needn't reach their ends.
Inputs may be any that keep to these rules, and one draw needn't show every extreme that they name: `block_owner`: A device's blocks are those of its 4 spanwise cells, 8 wall-normal cells and 1024 lines. Of one device's 256 blocks at most 32 name one owner; in every span and wall group one owner receives exactly 32 blocks from each of the 16 devices along the patch axis.
All inputs are finite; a program needn't handle non-finite values.
Results may differ from the reference program's by a relative error of at most 0.000094.
Values sent between devices are 32-bit elements; how exact they have to be, the bound alone decides.
No kernel may reach another device: no remote copies, remote signals or barrier semaphores. Data moves between devices by JAX's collectives and lax.ppermute only.
A program may use at most 64 MiB of HBM per device.

```python
import jax
import jax.numpy as jnp
from jax import lax

EQUATIONS = 5
BLOCK = 128
S_DEV = 4
W_DEV = 8
L_DEV = 1024
AGG_DEV = 4
NS = 32
NW = 16
NL = 16384
NQ = 128
BLK_DEV = 256
SPAN_GROUPS = 8
WALL_GROUPS = 2
AGGS = 64


def jacobian_pair(key):
    diag_key, off_key = jax.random.split(jax.random.fold_in(key, 7))
    diagonal = jnp.exp(jax.random.uniform(diag_key, (NS, NW, EQUATIONS, NL), jnp.float32, jnp.log(8.0), jnp.log(24.0)))
    offdiag = jax.random.uniform(off_key, (NS, NW, EQUATIONS, EQUATIONS, NL), jnp.float32, -2.0, 2.0)
    identity = jnp.eye(EQUATIONS, dtype=jnp.float32)[None, None, :, :, None]
    jac = identity * diagonal[:, :, :, None, :] + (1.0 - identity) * offdiag
    row_diag = diagonal[:, :, :, None, :]
    col_diag = diagonal[:, :, None, :, :]
    approx = identity / row_diag - (1.0 - identity) * jnp.swapaxes(offdiag, 2, 3) / (row_diag * col_diag)
    return (jac, approx)


def draw_jac(key, part):
    return jacobian_pair(key)[0]


def draw_jac_inv(key, part):
    return jacobian_pair(key)[1]


def draw_block_owner(key, part):
    busy_key, label_key = jax.random.split(jax.random.fold_in(key, 11))
    span_count = NS // S_DEV
    wall_count = NW // W_DEV
    patch_count = NL // L_DEV
    per_line = L_DEV // BLOCK
    block_total = S_DEV * W_DEV * per_line
    capacity = max(2, 2 * block_total // patch_count)
    busy = jax.random.randint(busy_key, (span_count, wall_count, 1, 1), 0, patch_count)
    pattern = jnp.arange(block_total, dtype=jnp.int32)
    pattern = jnp.where(pattern < capacity, 0, 1 + (pattern - capacity) % (patch_count - 1))

    def device_labels(device_key):
        perm_key, order_key = jax.random.split(device_key)
        permuted = jax.random.permutation(perm_key, patch_count - 1).astype(jnp.int32)
        order = jax.random.permutation(order_key, block_total)
        labels = jnp.where(pattern == 0, 0, 1 + permuted[jnp.maximum(pattern - 1, 0)])
        return labels[order]
    devices = span_count * wall_count * patch_count
    labels = jax.vmap(device_labels)(jax.random.split(label_key, devices))
    labels = labels.reshape(span_count, wall_count, patch_count, block_total)
    owners = (busy + labels) % patch_count
    owners = owners.reshape(span_count, wall_count, patch_count, S_DEV, W_DEV, per_line)
    owners = owners.transpose(0, 3, 1, 4, 2, 5).reshape(NS, NW, NQ)
    return owners.astype(jnp.int32)


def with_ends(values, own_key, low, largest):
    index_at = [jax.random.randint(jax.random.fold_in(own_key, axis), (), 0, length) for axis, length in enumerate(values.shape)]
    longest = values.shape.index(max(values.shape))
    next_to = index_at[:longest] + [(index_at[longest] + 1) % values.shape[longest]] + index_at[longest + 1:]
    return values.at[tuple(index_at)].set(low).at[tuple(next_to)].set(largest)


def shard_levels(key, dims, cuts, least, top_value):
    gain = 1.0
    for position, blocks in cuts:
        steps = jax.random.uniform(jax.random.fold_in(jax.random.fold_in(key, 6), position), (blocks,), jnp.float32, least / len(cuts), top_value / len(cuts))
        gain = gain * jnp.repeat(jnp.exp(steps), dims[position] // blocks).reshape((-1,) + (1,) * (len(dims) - 1 - position))
    return gain


def scatter_about(stream_key, shape, spread, most, shards=(), kind=jnp.bfloat16):
    result = jax.random.normal(stream_key, shape, jnp.float32) * spread
    if len(shards) > 0:
        result = shard_levels(stream_key, shape, shards, -0.22, 0.18) * result
    return jnp.clip(result, min=-most, max=most).astype(kind)


def setup_inputs(seed: int = 0) -> dict:
    key_list = jax.random.split(jax.random.key(seed), 9)
    rhs = scatter_about(key_list[0], (NS, NW, EQUATIONS, NL), 4.0, 24.0, ((0, 8), (1, 2), (3, 16)), jnp.float32)
    jac = draw_jac(jax.random.fold_in(key_list[8], 71), 0)
    jac_inv = draw_jac_inv(jax.random.fold_in(key_list[8], 71), 0)
    wall_coupling = scatter_about(key_list[3], (EQUATIONS, EQUATIONS), 0.3, 1.2, (), jnp.float32)
    span_coupling = scatter_about(key_list[4], (EQUATIONS, EQUATIONS), 0.3, 1.2, (), jnp.float32)
    block_owner = draw_block_owner(jax.random.fold_in(key_list[8], 71), 0)
    block_slot = with_ends(jax.random.randint(key_list[6], (NS, NW, NQ), 0, AGG_DEV), jax.random.fold_in(key_list[6], 1), 0, AGG_DEV - 1).astype(jnp.int32)
    coarse_inv = scatter_about(key_list[7], (SPAN_GROUPS, WALL_GROUPS, EQUATIONS, EQUATIONS * WALL_GROUPS, AGGS), (0.06 * (AGG_DEV / BLK_DEV) ** 0.5), 0.045, ((0, 8), (1, 2), (4, 16)), jnp.float32)
    return dict(rhs=rhs, jac=jac, jac_inv=jac_inv, wall_coupling=wall_coupling, span_coupling=span_coupling, block_owner=block_owner, block_slot=block_slot, coarse_inv=coarse_inv)


def apply_adjoint(field, jac, wall_coupling, span_coupling):
    highest = lax.Precision.HIGHEST
    own_term = jnp.sum(jac * field[:, :, :, None, :], axis=2)
    pad_wall = jnp.pad(field, ((0, 0), (1, 1), (0, 0), (0, 0)))
    pad_span = jnp.pad(field, ((1, 1), (0, 0), (0, 0), (0, 0)))
    near_wall = pad_wall[:, 2:] + pad_wall[:, :-2]
    near_span = pad_span[2:] + pad_span[:-2]
    wall_term = jnp.einsum('ki,swkl->swil', wall_coupling, near_wall, precision=highest)
    span_term = jnp.einsum('ki,swkl->swil', span_coupling, near_span, precision=highest)
    return own_term - wall_term - span_term


def precondition(defect, jac_inv):
    return jnp.sum(jac_inv * defect[:, :, None, :, :], axis=3)


def reference(rhs, jac, jac_inv, wall_coupling, span_coupling, block_owner, block_slot, coarse_inv):
    highest = lax.Precision.HIGHEST
    first_pass = precondition(rhs, jac_inv)
    second = first_pass + precondition(rhs - apply_adjoint(first_pass, jac, wall_coupling, span_coupling), jac_inv)
    defect = rhs - apply_adjoint(second, jac, wall_coupling, span_coupling)
    defect_blocks = defect.reshape(SPAN_GROUPS, S_DEV, WALL_GROUPS, W_DEV, EQUATIONS, NQ, BLOCK)
    agg_index = block_owner * AGG_DEV + block_slot
    onehot = (agg_index[..., None] == jnp.arange(AGGS, dtype=jnp.int32)).astype(jnp.float32)
    onehot = onehot.reshape(SPAN_GROUPS, S_DEV, WALL_GROUPS, W_DEV, NQ, AGGS)
    coarse_res = jnp.einsum('asbwkqj,asbwqg->abgkj', defect_blocks, onehot, precision=highest)
    line_inv = coarse_inv.reshape(SPAN_GROUPS, WALL_GROUPS, EQUATIONS, WALL_GROUPS, EQUATIONS, AGGS)
    coarse_fix = jnp.einsum('abiBkg,aBgkj->abgij', line_inv, coarse_res, precision=highest)
    correction = jnp.einsum('asbwqg,abgij->asbwiqj', onehot, coarse_fix, precision=highest)
    third_pass = second + correction.reshape(NS, NW, EQUATIONS, NL)
    return third_pass + precondition(rhs - apply_adjoint(third_pass, jac, wall_coupling, span_coupling), jac_inv)
```

```python
import functools

import jax
import jax.numpy as jnp
from jax import lax
from jax.experimental import pallas as pl
from jax.experimental.pallas import tpu as pltpu
from jax.sharding import PartitionSpec as P

LANES = 128
VMEM = pl.BlockSpec(memory_space=pltpu.VMEM)
SMEM = pl.BlockSpec(memory_space=pltpu.SMEM)
HIGHEST = lax.Precision.HIGHEST


def call(kernel, outs, n_smem, *args):
    size = 4 * sum(a.size for a in (*args, *outs))
    return pl.pallas_call(
        kernel,
        out_shape=outs,
        in_specs=[SMEM] * n_smem + [VMEM] * (len(args) - n_smem),
        out_specs=[VMEM] * len(outs),
        cost_estimate=pl.CostEstimate(flops=size, bytes_accessed=size, transcendentals=0),
        compiler_params=pltpu.CompilerParams(vmem_limit_bytes=20 * 2**20),
    )(*args)


def mix(coupling, values):
    n = len(values)
    return [
        functools.reduce(lambda a, b: a + b, [coupling[k, i] * values[k] for k in range(n)])
        for i in range(n)
    ]


def sweep(jinv, s, lanes, values):
    n = len(values)
    return [
        functools.reduce(lambda a, b: a + b, [jinv[s, i, k, :, lanes] * values[k] for k in range(n)])
        for i in range(n)
    ]


def wall_edges(flags, planes, out):
    row = jnp.where(flags[1] == 0, 7, 0)
    for s, plane in enumerate(planes):
        for k in range(5):
            out[s * 5 + k, :] = plane(k, row)


def for_lanes(body, length):
    @pl.loop(0, length // LANES)
    def _(q):
        body(pl.ds(pl.multiple_of(q * LANES, LANES), LANES), q)


def first_kernel(flags, rhs, jinv, first, edge_a, edge_b, edge_w):
    even = flags[0] == 1

    def body(lanes, q):
        ends = {}
        for s in range(4):
            ends[s] = sweep(jinv, s, lanes, [rhs[s, k, :, lanes] for k in range(5)])
            for k in range(5):
                first[s, k, :, lanes] = ends[s][k]
        for k in range(5):
            edge_a[k, :, lanes] = jnp.where(even, ends[3][k], ends[0][k])
            edge_b[k, :, lanes] = jnp.where(even, ends[0][k], ends[3][k])

    for_lanes(body, rhs.shape[-1])
    wall_edges(flags, [functools.partial(lambda s, k, r: first[s, k, r, :], s) for s in range(4)], edge_w)


def local_apply(flags, wall, span, planes, halo_w, jac, lanes, s):
    own = planes[s]
    rows = lax.broadcasted_iota(jnp.int32, own[0].shape, 0)
    other_side = rows == jnp.where(flags[1] == 0, 7, 0)
    near_wall, near_span = [], []
    for k in range(5):
        up = jnp.where(rows == 7, 0.0, pltpu.roll(own[k], 7, 0))
        down = jnp.where(rows == 0, 0.0, pltpu.roll(own[k], 1, 0))
        beyond = jnp.where(other_side, halo_w[s * 5 + k, lanes][None, :], 0.0)
        near_wall.append(up + down + beyond)
        around = [planes[n][k] for n in (s - 1, s + 1) if 0 <= n < 4]
        near_span.append(functools.reduce(lambda a, b: a + b, around))
    from_wall, from_span = mix(wall, near_wall), mix(span, near_span)
    return [
        functools.reduce(lambda a, b: a + b, [jac[s, k, i, :, lanes] * own[k] for k in range(5)])
        - from_wall[i] - from_span[i]
        for i in range(5)
    ]


def second_local_kernel(flags, wall, span, first, halo_w, rhs, jac, jinv, out):
    def body(lanes, q):
        planes = [[first[s, k, :, lanes] for k in range(5)] for s in range(4)]
        for s in range(4):
            applied = local_apply(flags, wall, span, planes, halo_w, jac, lanes, s)
            swept = sweep(jinv, s, lanes, [rhs[s, k, :, lanes] - applied[k] for k in range(5)])
            for k in range(5):
                out[s, k, :, lanes] = planes[s][k] + swept[k]

    for_lanes(body, rhs.shape[-1])


def second_edge_kernel(flags, span, inner, halo_a, halo_b, jinv, edge_a, edge_b, edge_w):
    even = flags[0] == 1
    plane_a = jnp.where(even, 3, 0)
    plane_b = 3 - plane_a

    def body(lanes, q):
        for plane, halo, edge in ((plane_a, halo_a, edge_a), (plane_b, halo_b, edge_b)):
            beyond = mix(span, [halo[k, :, lanes] for k in range(5)])
            swept = sweep(jinv, plane, lanes, beyond)
            for k in range(5):
                edge[k, :, lanes] = inner[plane, k, :, lanes] + swept[k]

    for_lanes(body, inner.shape[-1])
    row = jnp.where(flags[1] == 0, 7, 0)
    for k in range(5):
        for s in (1, 2):
            edge_w[s * 5 + k, :] = inner[s, k, row, :]
        a, b = edge_a[k, row, :], edge_b[k, row, :]
        edge_w[k, :] = jnp.where(even, b, a)
        edge_w[15 + k, :] = jnp.where(even, a, b)


def planes_of(flags, inner, edge_a, edge_b, lanes):
    even = flags[0] == 1
    a = [edge_a[k, :, lanes] for k in range(5)]
    b = [edge_b[k, :, lanes] for k in range(5)]
    return [
        [jnp.where(even, b[k], a[k]) for k in range(5)],
        [inner[1, k, :, lanes] for k in range(5)],
        [inner[2, k, :, lanes] for k in range(5)],
        [jnp.where(even, a[k], b[k]) for k in range(5)],
    ]


def defect_local_kernel(flags, wall, span, inner, edge_a, edge_b, halo_w, rhs, jac, second, defect):
    def body(lanes, q):
        planes = planes_of(flags, inner, edge_a, edge_b, lanes)
        for s in range(4):
            applied = local_apply(flags, wall, span, planes, halo_w, jac, lanes, s)
            for k in range(5):
                second[s, k, :, lanes] = planes[s][k]
                defect[s, k, :, lanes] = rhs[s, k, :, lanes] - applied[k]

    for_lanes(body, rhs.shape[-1])


def restrict_kernel(flags, span, defect_in, halo_a, halo_b, onehot_t, defect, partial):
    even = flags[0] == 1
    plane_a = jnp.where(even, 3, 0)
    plane_b = 3 - plane_a

    def body(lanes, q):
        for s in (1, 2):
            for k in range(5):
                defect[s, k, :, lanes] = defect_in[s, k, :, lanes]
        for plane, halo in ((plane_a, halo_a), (plane_b, halo_b)):
            beyond = mix(span, [halo[k, :, lanes] for k in range(5)])
            for k in range(5):
                defect[plane, k, :, lanes] = defect_in[plane, k, :, lanes] + beyond[k]

    for_lanes(body, defect.shape[-1])
    tiles = defect.shape[-1] // LANES
    for k in range(5):
        rows = jnp.concatenate(
            [defect[s, k, :, q * LANES : (q + 1) * LANES] for s in range(4) for q in range(tiles)], axis=0
        )
        partial[:, k * LANES : (k + 1) * LANES] = jnp.dot(
            onehot_t[...], rows, precision=HIGHEST, preferred_element_type=jnp.float32
        )


def smooth_kernel(second, defect, jinv, base):
    def body(lanes, q):
        for s in range(4):
            swept = sweep(jinv, s, lanes, [defect[s, k, :, lanes] for k in range(5)])
            for k in range(5):
                base[s, k, :, lanes] = second[s, k, :, lanes] + swept[k]

    for_lanes(body, base.shape[-1])


def sum_kernel(received, total):
    sums = functools.reduce(lambda a, b: a + b, [received[8 * i : 8 * i + 8, :] for i in range(received.shape[0] // 8)])
    total[...] = sums[:4] + sums[4:]


def coarse_kernel(own_inv, other_inv, own, other, out):
    columns = own.shape[1]
    for i in range(5):
        terms = []
        for k in range(5):
            lanes = slice(k * LANES, (k + 1) * LANES)
            terms.append(own_inv[i * 5 + k] * own[:, lanes])
            terms.append(other_inv[i * 5 + k] * other[:, lanes])
        fix = functools.reduce(lambda a, b: a + b, terms)
        for p in range(out.shape[0]):
            out[p, :, i * LANES : (i + 1) * LANES] = fix
    del columns


def prolong_kernel(flags, onehot, fix, out, edge_a, edge_b, edge_w):
    even = flags[0] == 1
    tiles = out.shape[-1] // LANES
    for k in range(5):
        rows = jnp.dot(
            onehot[...], fix[:, k * LANES : (k + 1) * LANES], precision=HIGHEST, preferred_element_type=jnp.float32
        )
        for q in range(tiles):
            lanes = slice(q * LANES, (q + 1) * LANES)
            tile = [rows[(s * tiles + q) * 8 : (s * tiles + q) * 8 + 8] for s in range(4)]
            for s in range(4):
                out[s, k, :, lanes] = tile[s]
            edge_a[k, :, lanes] = jnp.where(even, tile[3], tile[0])
            edge_b[k, :, lanes] = jnp.where(even, tile[0], tile[3])
    wall_edges(flags, [functools.partial(lambda s, k, r: out[s, k, r, :], s) for s in range(4)], edge_w)


def final_local_kernel(flags, wall, span, base, fix, halo_w, jac, jinv, out):
    def body(lanes, q):
        planes = [[fix[s, k, :, lanes] for k in range(5)] for s in range(4)]
        for s in range(4):
            applied = local_apply(flags, wall, span, planes, halo_w, jac, lanes, s)
            swept = sweep(jinv, s, lanes, applied)
            for k in range(5):
                out[s, k, :, lanes] = base[s, k, :, lanes] + (planes[s][k] - swept[k])

    for_lanes(body, base.shape[-1])


def final_edge_kernel(flags, span, inner, halo_a, halo_b, jinv, out):
    plane_a = jnp.where(flags[0] == 1, 3, 0)
    plane_b = 3 - plane_a

    def body(lanes, q):
        for s in (1, 2):
            for k in range(5):
                out[s, k, :, lanes] = inner[s, k, :, lanes]
        for plane, halo in ((plane_a, halo_a), (plane_b, halo_b)):
            beyond = mix(span, [halo[k, :, lanes] for k in range(5)])
            swept = sweep(jinv, plane, lanes, beyond)
            for k in range(5):
                out[plane, k, :, lanes] = inner[plane, k, :, lanes] + swept[k]

    for_lanes(body, inner.shape[-1])


def exchange(edge_a, edge_b, edge_w):
    size = lax.axis_size("span")
    pairs = [(i, i + 1) for i in range(size - 1)]
    even = [p for i, j in pairs[0::2] for p in ((i, j), (j, i))]
    odd = [p for i, j in pairs[1::2] for p in ((i, j), (j, i))]
    return (
        lax.ppermute(edge_a, "span", even),
        lax.ppermute(edge_b, "span", odd),
        lax.ppermute(edge_w, "wall", [(0, 1), (1, 0)]),
    )


def local(rhs, jac, jac_inv, wall_coupling, span_coupling, block_owner, block_slot, coarse_inv):
    f32 = jnp.float32
    rhs = rhs.transpose(0, 2, 1, 3)
    jac = jac.transpose(0, 2, 3, 1, 4)
    jinv = jac_inv.transpose(0, 2, 3, 1, 4)
    field = jax.ShapeDtypeStruct(rhs.shape, f32)
    plane = jax.ShapeDtypeStruct(rhs.shape[1:], f32)
    edge = jax.ShapeDtypeStruct((20, rhs.shape[-1]), f32)
    span_at, wall_at = lax.axis_index("span"), lax.axis_index("wall")
    flags = jnp.stack([1 - span_at % 2, wall_at]).astype(jnp.int32)
    owners, slots = lax.axis_size("patch"), coarse_inv.shape[-1]
    aggregates = owners * slots
    named = (block_owner * slots + block_slot).transpose(0, 2, 1).reshape(-1)
    ids = jnp.arange(aggregates, dtype=jnp.int32)
    onehot = (named[:, None] == ids[None, :]).astype(f32)
    onehot_t = (named[None, :] == ids[:, None]).astype(f32)
    inv = coarse_inv.reshape(5, 2, 5, slots)
    own_inv = lax.dynamic_index_in_dim(inv, wall_at, 1, keepdims=False).reshape(25, slots, 1)
    other_inv = lax.dynamic_index_in_dim(inv, 1 - wall_at, 1, keepdims=False).reshape(25, slots, 1)
    own_inv = jnp.broadcast_to(own_inv, (25, slots, LANES))
    other_inv = jnp.broadcast_to(other_inv, (25, slots, LANES))

    first, a, b, w = call(first_kernel, [field, plane, plane, edge], 1, flags, rhs, jinv)
    halo_a, halo_b, halo_w = exchange(a, b, w)
    [inner] = call(second_local_kernel, [field], 3, flags, wall_coupling, span_coupling, first, halo_w, rhs, jac, jinv)
    a, b, w = call(second_edge_kernel, [plane, plane, edge], 2, flags, span_coupling, inner, halo_a, halo_b, jinv)
    halo_a, halo_b, halo_w = exchange(a, b, w)
    second, defect = call(
        defect_local_kernel, [field, field], 3, flags, wall_coupling, span_coupling, inner, a, b, halo_w, rhs, jac
    )
    part = jax.ShapeDtypeStruct((aggregates, 5 * LANES), f32)
    defect, partial = call(
        restrict_kernel, [field, part], 2, flags, span_coupling, defect, halo_a, halo_b, onehot_t
    )
    received = lax.all_to_all(partial, "patch", split_axis=0, concat_axis=0, tiled=True)
    [base] = call(smooth_kernel, [field], 0, second, defect, jinv)
    [mine] = call(sum_kernel, [jax.ShapeDtypeStruct((slots, 5 * LANES), f32)], 0, received)
    theirs = lax.ppermute(mine, "wall", [(0, 1), (1, 0)])
    [reply] = call(
        coarse_kernel, [jax.ShapeDtypeStruct((owners, slots, 5 * LANES), f32)], 0, own_inv, other_inv, mine, theirs
    )
    fixes = lax.all_to_all(reply, "patch", split_axis=0, concat_axis=0, tiled=True)
    fixes = fixes.reshape(aggregates, 5 * LANES)
    fix, a, b, w = call(prolong_kernel, [field, plane, plane, edge], 1, flags, onehot, fixes)
    halo_a, halo_b, halo_w = exchange(a, b, w)
    [inner] = call(
        final_local_kernel, [field], 3, flags, wall_coupling, span_coupling, base, fix, halo_w, jac, jinv
    )
    [out] = call(final_edge_kernel, [field], 2, flags, span_coupling, inner, halo_a, halo_b, jinv)
    return out.transpose(0, 2, 1, 3)


def solution(mesh):
    return jax.shard_map(
        local,
        mesh=mesh,
        in_specs=(
            P("span", "wall", None, "patch"),
            P("span", "wall", None, None, "patch"),
            P("span", "wall", None, None, "patch"),
            P(),
            P(),
            P("span", "wall", "patch"),
            P("span", "wall", "patch"),
            P("span", "wall", None, None, "patch"),
        ),
        out_specs=P("span", "wall", None, "patch"),
        check_vma=False,
    )
```

```python
import functools
import math

import jax
import jax.numpy as jnp
from jax import lax
from jax.experimental import pallas as pl
from jax.experimental.pallas import tpu as pltpu
from jax.sharding import PartitionSpec as P

LANES = 128
VMEM = pl.BlockSpec(memory_space=pltpu.VMEM)
SMEM = pl.BlockSpec(memory_space=pltpu.SMEM)
HBM = pl.BlockSpec(memory_space=pltpu.HBM)
HIGHEST = lax.Precision.HIGHEST
F32 = jnp.float32


def shaped(*shape):
    return jax.ShapeDtypeStruct(shape, F32)


def in_hbm(array):
    return pltpu.with_memory_space_constraint(array, pltpu.HBM)


def call(kernel, outs, args, places=None, out_places=None, scratch=(), aliases=None):
    size = 2 * sum(math.prod(a.shape) for a in (*args, *outs))
    return pl.pallas_call(
        kernel,
        out_shape=outs,
        in_specs=places or [VMEM] * len(args),
        out_specs=out_places or [VMEM] * len(outs),
        scratch_shapes=scratch,
        input_output_aliases=aliases or {},
        cost_estimate=pl.CostEstimate(flops=size, bytes_accessed=size, transcendentals=0),
        compiler_params=pltpu.CompilerParams(vmem_limit_bytes=8 * 2**20),
    )(*args)


def total(terms):
    return functools.reduce(lambda a, b: a + b, terms)


def position():
    span_at, wall_at = lax.axis_index("span"), lax.axis_index("wall")
    odd = lax.rem(span_at, 2)
    plane_a = 3 - 3 * odd
    return odd == 0, plane_a, 3 - plane_a, 7 - 7 * wall_at


def inside():
    at, size = lax.axis_index("span"), lax.axis_size("span")
    return jnp.logical_and(at > 0, at < size - 1)


def mix(splat, which, values):
    return [total([splat[which, k, i] * values[k] for k in range(5)]) for i in range(5)]


def sweep(jinv, s, lanes, values):
    return [total([jinv[s, i, k, :, lanes] * values[k] for k in range(5)]) for i in range(5)]


def beyond_span(splat, halo, lanes, real=None):
    values = [halo[k, :, lanes] for k in range(5)]
    if real is not None:
        values = [jnp.where(real, v, 0.0) for v in values]
    return mix(splat, 1, values)


def for_lanes(body, length):
    @pl.loop(0, length // LANES)
    def _(q):
        body(pl.ds(pl.multiple_of(q * LANES, LANES), LANES))


def first_kernel(wall, span, rhs_in, jinv_in, rhs, jinv, splat, first, edge_a, edge_b, edge_w, sems):
    copies = [pltpu.make_async_copy(rhs_in, rhs, sems.at[4])]
    copies += [pltpu.make_async_copy(jinv_in.at[s], jinv.at[s], sems.at[s]) for s in range(4)]
    for copy in copies:
        copy.start()
    for which, coupling in enumerate((wall, span)):
        for k in range(5):
            for i in range(5):
                splat[which, k, i] = jnp.full((8, LANES), coupling[k, i], F32)
    even, plane_a, plane_b, row = position()
    copies[0].wait()
    for s in range(4):
        copies[1 + s].wait()

        def body(lanes, s=s):
            swept = sweep(jinv, s, lanes, [rhs[s, k, :, lanes] for k in range(5)])
            for k in range(5):
                first[s, k, :, lanes] = swept[k]

        for_lanes(body, rhs.shape[-1])
        for k in range(5):
            edge_w[s * 5 + k, :] = first[s, k, row, :]
    for k in range(5):
        edge_a[k] = first[plane_a, k]
        edge_b[k] = first[plane_b, k]


def local_apply(splat, row, planes, halo_w, jac, lanes, s):
    own = planes[s]
    rows = lax.broadcasted_iota(jnp.int32, own[0].shape, 0)
    other_side = rows == row
    near_wall, near_span = [], []
    for k in range(5):
        up = jnp.where(rows == 7, 0.0, pltpu.roll(own[k], 7, 0))
        down = jnp.where(rows == 0, 0.0, pltpu.roll(own[k], 1, 0))
        beyond = jnp.where(other_side, halo_w[s * 5 + k, lanes][None, :], 0.0)
        near_wall.append(up + down + beyond)
        near_span.append(total([planes[n][k] for n in (s - 1, s + 1) if 0 <= n < 4]))
    from_wall, from_span = mix(splat, 0, near_wall), mix(splat, 1, near_span)
    return [
        total([jac[s, k, i, :, lanes] * own[k] for k in range(5)]) - (from_wall[i] + from_span[i])
        for i in range(5)
    ]


def hot_rows(owner, slot, tiles):
    ids = lax.broadcasted_iota(jnp.int32, (8, LANES), 1)
    hot = []
    for s in range(4):
        named = owner[s] * 4 + slot[s]
        hot += [jnp.where(named[:, q : q + 1] == ids, 1.0, 0.0) for q in range(tiles)]
    return jnp.concatenate(hot, axis=0)


def second_local_kernel(splat, first, halo_w, rhs, jinv, owner, slot, jac_in, inner, jac, onehot_t, sems):
    copies = [pltpu.make_async_copy(jac_in.at[s], jac.at[s], sems.at[s]) for s in range(4)]
    for copy in copies:
        copy.start()
    row = position()[3]
    onehot_t[...] = hot_rows(owner, slot, rhs.shape[-1] // LANES).T[: onehot_t.shape[0]]
    for s in range(4):
        copies[s].wait()

        def body(lanes, s=s):
            planes = [[first[n, k, :, lanes] for k in range(5)] if abs(n - s) < 2 else None for n in range(4)]
            applied = local_apply(splat, row, planes, halo_w, jac, lanes, s)
            swept = sweep(jinv, s, lanes, [rhs[s, k, :, lanes] - applied[k] for k in range(5)])
            for k in range(5):
                inner[s, k, :, lanes] = planes[s][k] + swept[k]

        for_lanes(body, rhs.shape[-1])


def second_edge_kernel(splat, inner, halo_a, halo_b, jinv, edge_a, edge_b, edge_w):
    even, plane_a, plane_b, row = position()
    real = inside()

    def body(lanes):
        for plane, halo, edge, there in ((plane_a, halo_a, edge_a, None), (plane_b, halo_b, edge_b, real)):
            swept = sweep(jinv, plane, lanes, beyond_span(splat, halo, lanes, there))
            for k in range(5):
                edge[k, :, lanes] = inner[plane, k, :, lanes] + swept[k]

    for_lanes(body, inner.shape[-1])
    for k in range(5):
        for s in (1, 2):
            edge_w[s * 5 + k, :] = inner[s, k, row, :]
        a, b = edge_a[k, row, :], edge_b[k, row, :]
        edge_w[k, :] = jnp.where(even, b, a)
        edge_w[15 + k, :] = jnp.where(even, a, b)


def planes_of(even, inner, edge_a, edge_b, lanes):
    a = [edge_a[k, :, lanes] for k in range(5)]
    b = [edge_b[k, :, lanes] for k in range(5)]
    return [
        [jnp.where(even, b[k], a[k]) for k in range(5)],
        [inner[1, k, :, lanes] for k in range(5)],
        [inner[2, k, :, lanes] for k in range(5)],
        [jnp.where(even, a[k], b[k]) for k in range(5)],
    ]


def defect_local_kernel(splat, inner, edge_a, edge_b, halo_w, rhs, jac, jinv, onehot_t, base, partial, defect):
    even, _, _, row = position()

    def body(lanes):
        planes = planes_of(even, inner, edge_a, edge_b, lanes)
        for s in range(4):
            applied = local_apply(splat, row, planes, halo_w, jac, lanes, s)
            rest = [rhs[s, k, :, lanes] - applied[k] for k in range(5)]
            swept = sweep(jinv, s, lanes, rest)
            for k in range(5):
                base[s, k, :, lanes] = planes[s][k] + swept[k]
                defect[s, k, :, lanes] = rest[k]

    for_lanes(body, rhs.shape[-1])
    tiles = defect.shape[-1] // LANES
    for k in range(5):
        rows = jnp.concatenate(
            [defect[s, k, :, q * LANES : (q + 1) * LANES] for s in range(4) for q in range(tiles)], axis=0
        )
        partial[:, k * LANES : (k + 1) * LANES] = jnp.dot(
            onehot_t[...], rows, precision=HIGHEST, preferred_element_type=F32
        )


def restrict_kernel(splat, inner, base, halo_a, halo_b, onehot_t, jinv, partial, base_out, edges, sems):
    even, plane_a, plane_b, _ = position()
    real = inside()
    copies = [pltpu.make_async_copy(base.at[pl.ds(1, 2)], base_out.at[pl.ds(1, 2)], sems.at[2])]
    copies[0].start()
    tiles = halo_a.shape[-1] // LANES
    parts = []
    for n, (plane, halo, there) in enumerate(((plane_a, halo_a, None), (plane_b, halo_b, real))):
        for q in range(tiles):
            lanes = slice(q * LANES, (q + 1) * LANES)
            beyond = beyond_span(splat, halo, lanes, there)
            parts.append(beyond)
            swept = sweep(jinv, plane, lanes, beyond)
            for k in range(5):
                edges[n, k, :, lanes] = base[plane, k, :, lanes] + swept[k]
        copies.append(pltpu.make_async_copy(edges.at[n], base_out.at[plane], sems.at[n]))
        copies[-1].start()
    width = 8 * tiles
    low, high = onehot_t[:, :width], onehot_t[:, 3 * width :]
    hot = jnp.concatenate([jnp.where(even, high, low), jnp.where(even, low, high)], axis=1)
    slots = partial.shape[1]
    for k in range(5):
        rows = jnp.concatenate([part[k] for part in parts], axis=0)
        sums = inner[:, k * LANES : (k + 1) * LANES] + jnp.dot(
            hot, rows, precision=HIGHEST, preferred_element_type=F32
        )
        for p in range(partial.shape[0]):
            partial[p, :, k * LANES : (k + 1) * LANES] = sums[p * slots : (p + 1) * slots]
    for copy in copies:
        copy.wait()


def sum_kernel(received, sums):
    sums[...] = total([received[p] for p in range(received.shape[0])])


def coarse_kernel(inv, own, other, out):
    first_group = lax.axis_index("wall") == 0
    groups = [
        [jnp.where(first_group, x[:, k * LANES : (k + 1) * LANES], y[:, k * LANES : (k + 1) * LANES]) for k in range(5)]
        for x, y in ((own, other), (other, own))
    ]
    for i in range(5):
        rows = inv[i]
        fix = total([rows[:, c * 5 + k : c * 5 + k + 1] * groups[c][k] for c in range(2) for k in range(5)])
        for p in range(out.shape[0]):
            out[p, :, i * LANES : (i + 1) * LANES] = fix


def prolong_kernel(owner, slot, fixes, out, edge_a, edge_b, edge_w, fix):
    _, plane_a, plane_b, row = position()
    tiles = out.shape[-1] // LANES
    owners, slots, _ = fixes.shape
    for p in range(owners):
        fix[p * slots : (p + 1) * slots, :] = fixes[p]
    hot = hot_rows(owner, slot, tiles)[:, : owners * slots]
    for k in range(5):
        rows = jnp.dot(hot, fix[:, k * LANES : (k + 1) * LANES], precision=HIGHEST, preferred_element_type=F32)
        for s in range(4):
            for q in range(tiles):
                at = (s * tiles + q) * 8
                out[s, k, :, q * LANES : (q + 1) * LANES] = rows[at : at + 8]
    for k in range(5):
        edge_a[k] = out[plane_a, k]
        edge_b[k] = out[plane_b, k]
        for s in range(4):
            edge_w[s * 5 + k, :] = out[s, k, row, :]


def final_local_kernel(splat, fix, halo_w, base_in, jac_in, jinv_in, out, inner, jinv, base, jac, sems):
    row = position()[3]
    loads = []
    for s in range(4):
        loads += [
            pltpu.make_async_copy(source.at[s], here.at[s], sems.at[n, s])
            for n, (source, here) in enumerate(((jac_in, jac), (jinv_in, jinv), (base_in, base)))
        ]
    for load in loads:
        load.start()
    stores = []
    for s in range(4):
        for load in loads[3 * s : 3 * s + 3]:
            load.wait()

        def body(lanes, s=s):
            planes = [[fix[n, k, :, lanes] for k in range(5)] if abs(n - s) < 2 else None for n in range(4)]
            applied = local_apply(splat, row, planes, halo_w, jac, lanes, s)
            swept = sweep(jinv, s, lanes, applied)
            for k in range(5):
                inner[s, k, :, lanes] = base[s, k, :, lanes] + (planes[s][k] - swept[k])

        for_lanes(body, fix.shape[-1])
        if s in (1, 2):
            stores.append(pltpu.make_async_copy(inner.at[s], out.at[s], sems.at[3, s]))
            stores[-1].start()
    for store in stores:
        store.wait()


def final_edge_kernel(splat, inner, halo_a, halo_b, jinv, out_in, out, edges, sems):
    del out_in
    _, plane_a, plane_b, _ = position()
    real = inside()
    stores = []
    for n, (plane, halo, there) in enumerate(((plane_a, halo_a, None), (plane_b, halo_b, real))):

        def body(lanes, n=n, plane=plane, halo=halo, there=there):
            swept = sweep(jinv, plane, lanes, beyond_span(splat, halo, lanes, there))
            for k in range(5):
                edges[n, k, :, lanes] = inner[plane, k, :, lanes] + swept[k]

        for_lanes(body, inner.shape[-1])
        stores.append(pltpu.make_async_copy(edges.at[n], out.at[plane], sems.at[n]))
        stores[-1].start()
    for store in stores:
        store.wait()


def exchange(edge_a, edge_b, edge_w):
    size = lax.axis_size("span")
    even = [p for i in range(0, size, 2) for p in ((i, i + 1), (i + 1, i))]
    odd = [((i + 1) % size, (j + 1) % size) for i, j in even]
    return (
        lax.ppermute(edge_a, "span", even),
        lax.ppermute(edge_b, "span", odd),
        lax.ppermute(edge_w, "wall", [(0, 1), (1, 0)]),
    )


def local(rhs, jac, jac_inv, wall_coupling, span_coupling, block_owner, block_slot, coarse_inv):
    rhs = in_hbm(rhs.transpose(0, 2, 1, 3))
    jac_in = in_hbm(jac.transpose(0, 2, 3, 1, 4))
    jinv_in = in_hbm(jac_inv.transpose(0, 2, 3, 1, 4))
    inv = coarse_inv[0, 0].transpose(0, 2, 1)
    field, plane, edge = shaped(*rhs.shape), shaped(*rhs.shape[1:]), shaped(20, rhs.shape[-1])
    field_out = pltpu.HBM(rhs.shape, F32)
    matrices = shaped(*jac_in.shape)
    outer = pltpu.VMEM((2, *rhs.shape[1:]), F32)
    owners, slots = lax.axis_size("patch"), coarse_inv.shape[-1]
    aggregates, columns = owners * slots, 5 * LANES
    chunks = shaped(owners, slots, columns)

    rhs, jinv, splat, first, a, b, w = call(
        first_kernel,
        [field, matrices, shaped(2, 5, 5, 8, LANES), field, plane, plane, edge],
        [wall_coupling, span_coupling, rhs, jinv_in],
        places=[SMEM, SMEM, HBM, HBM],
        scratch=[pltpu.SemaphoreType.DMA((5,))],
    )
    halo_a, halo_b, halo_w = exchange(a, b, w)
    inner, jac, onehot_t = call(
        second_local_kernel,
        [field, matrices, shaped(aggregates, block_owner.size)],
        [splat, first, halo_w, rhs, jinv, block_owner, block_slot, jac_in],
        places=[VMEM] * 7 + [HBM],
        scratch=[pltpu.SemaphoreType.DMA((4,))],
    )
    a, b, w = call(second_edge_kernel, [plane, plane, edge], [splat, inner, halo_a, halo_b, jinv])
    halo_a, halo_b, halo_w = exchange(a, b, w)
    base, partial = call(
        defect_local_kernel,
        [field, shaped(aggregates, columns)],
        [splat, inner, a, b, halo_w, rhs, jac, jinv, onehot_t],
        scratch=[pltpu.VMEM(rhs.shape, F32)],
    )
    partial, base = call(
        restrict_kernel,
        [chunks, field_out],
        [splat, partial, base, halo_a, halo_b, onehot_t, jinv],
        out_places=[VMEM, HBM],
        scratch=[outer, pltpu.SemaphoreType.DMA((3,))],
    )
    received = lax.all_to_all(partial, "patch", split_axis=0, concat_axis=0, tiled=True)
    [mine] = call(sum_kernel, [shaped(slots, columns)], [received])
    theirs = lax.ppermute(mine, "wall", [(0, 1), (1, 0)])
    [reply] = call(coarse_kernel, [chunks], [inv, mine, theirs])
    fixes = lax.all_to_all(reply, "patch", split_axis=0, concat_axis=0, tiled=True)
    fix, a, b, w = call(
        prolong_kernel,
        [field, plane, plane, edge],
        [block_owner, block_slot, fixes],
        scratch=[pltpu.VMEM((aggregates, columns), F32)],
    )
    halo_a, halo_b, halo_w = exchange(a, b, w)
    out, inner, jinv = call(
        final_local_kernel,
        [field_out, field, matrices],
        [splat, fix, halo_w, in_hbm(base), jac_in, jinv_in],
        places=[VMEM] * 3 + [HBM] * 3,
        out_places=[HBM, VMEM, VMEM],
        scratch=[pltpu.VMEM(rhs.shape, F32), pltpu.VMEM(jac_in.shape, F32), pltpu.SemaphoreType.DMA((4, 4))],
    )
    [out] = call(
        final_edge_kernel,
        [field_out],
        [splat, inner, halo_a, halo_b, jinv, in_hbm(out)],
        places=[VMEM] * 5 + [HBM],
        out_places=[HBM],
        scratch=[outer, pltpu.SemaphoreType.DMA((2,))],
        aliases={5: 0},
    )
    return out.transpose(0, 2, 1, 3)


def solution(mesh):
    return jax.shard_map(
        local,
        mesh=mesh,
        in_specs=(
            P("span", "wall", None, "patch"),
            P("span", "wall", None, None, "patch"),
            P("span", "wall", None, None, "patch"),
            P(),
            P(),
            P("span", "wall", "patch"),
            P("span", "wall", "patch"),
            P("span", "wall", None, None, "patch"),
        ),
        out_specs=P("span", "wall", None, "patch"),
        check_vma=False,
    )
```

```python
import functools
import math

import jax
import jax.numpy as jnp
from jax import lax
from jax.experimental import pallas as pl
from jax.experimental.pallas import tpu as pltpu
from jax.sharding import PartitionSpec as P

LANES = 128
VMEM = pl.BlockSpec(memory_space=pltpu.VMEM)
SMEM = pl.BlockSpec(memory_space=pltpu.SMEM)
HBM = pl.BlockSpec(memory_space=pltpu.HBM)
F32 = jnp.float32


def shaped(*shape):
    return jax.ShapeDtypeStruct(shape, F32)


def in_hbm(array):
    return pltpu.with_memory_space_constraint(array, pltpu.HBM)


def call(kernel, outs, args, places=None, out_places=None, scratch=(), aliases=None):
    size = 2 * sum(math.prod(a.shape) for a in (*args, *outs))
    return pl.pallas_call(
        kernel,
        out_shape=outs,
        in_specs=places or [VMEM] * len(args),
        out_specs=out_places or [VMEM] * len(outs),
        scratch_shapes=scratch,
        input_output_aliases=aliases or {},
        cost_estimate=pl.CostEstimate(flops=size, bytes_accessed=size, transcendentals=0),
        compiler_params=pltpu.CompilerParams(vmem_limit_bytes=8 * 2**20),
    )(*args)


def total(terms):
    return functools.reduce(lambda a, b: a + b, terms)


def position():
    span_at, wall_at = lax.axis_index("span"), lax.axis_index("wall")
    odd = lax.rem(span_at, 2)
    plane_a = 3 - 3 * odd
    return odd == 0, plane_a, 3 - plane_a, 7 - 7 * wall_at


def inside():
    at, size = lax.axis_index("span"), lax.axis_size("span")
    return jnp.logical_and(at > 0, at < size - 1)


def mix(splat, which, values):
    return [total([splat[which, k, i] * values[k] for k in range(5)]) for i in range(5)]


def sweep(jinv, s, lanes, values):
    return [total([jinv[s, i, k, :, lanes] * values[k] for k in range(5)]) for i in range(5)]


def beyond_span(splat, halo, lanes, real=None):
    values = [halo[k, :, lanes] for k in range(5)]
    if real is not None:
        values = [jnp.where(real, v, 0.0) for v in values]
    return mix(splat, 1, values)


def for_lanes(body, length):
    @pl.loop(0, length // LANES)
    def _(q):
        body(pl.ds(pl.multiple_of(q * LANES, LANES), LANES))


def picked_sums(hot, rows):
    hot = hot.astype(jnp.bfloat16)
    high = rows.astype(jnp.bfloat16)
    rest = rows - high.astype(F32)
    middle = rest.astype(jnp.bfloat16)
    low = (rest - middle.astype(F32)).astype(jnp.bfloat16)
    return total([jnp.dot(hot, part, preferred_element_type=F32) for part in (low, middle, high)])


def hot_rows(owner, slot, tiles):
    ids = lax.broadcasted_iota(jnp.int32, (8, LANES), 1)
    hot = []
    for s in range(4):
        named = owner[s] * 4 + slot[s]
        hot += [jnp.where(named[:, q : q + 1] == ids, 1.0, 0.0) for q in range(tiles)]
    return jnp.concatenate(hot, axis=0)


def first_kernel(
    wall_in, span_in, owner_in, slot_in, rhs_in, jinv_in, jac_in,
    rhs, jinv, jac, splat, onehot_t, first, edge_a, edge_b, edge_w,
    wall, span, owner, slot, small_sems, sems,
):
    small = [
        pltpu.make_async_copy(source, here, small_sems.at[n])
        for n, (source, here) in enumerate(
            ((wall_in, wall), (span_in, span), (owner_in, owner), (slot_in, slot), (rhs_in, rhs))
        )
    ]
    slabs = [pltpu.make_async_copy(jinv_in.at[s], jinv.at[s], sems.at[0, s]) for s in range(4)]
    later = [pltpu.make_async_copy(jac_in.at[s], jac.at[s], sems.at[1, s]) for s in range(4)]
    for copy in small + slabs + later:
        copy.start()
    small[0].wait()
    small[1].wait()
    for which, coupling in enumerate((wall, span)):
        for k in range(5):
            for i in range(5):
                splat[which, k, i] = jnp.full((8, LANES), coupling[k, i], F32)
    small[2].wait()
    small[3].wait()
    onehot_t[...] = hot_rows(owner, slot, rhs.shape[-1] // LANES).T[: onehot_t.shape[0]]
    _, plane_a, plane_b, row = position()
    small[4].wait()
    for s in range(4):
        slabs[s].wait()

        def body(lanes, s=s):
            swept = sweep(jinv, s, lanes, [rhs[s, k, :, lanes] for k in range(5)])
            for k in range(5):
                first[s, k, :, lanes] = swept[k]

        for_lanes(body, rhs.shape[-1])
        for k in range(5):
            edge_w[s * 5 + k, :] = first[s, k, row, :]
    for k in range(5):
        edge_a[k] = first[plane_a, k]
        edge_b[k] = first[plane_b, k]
    for copy in later:
        copy.wait()


def local_apply(splat, row, planes, halo_w, jac, lanes, s):
    own = planes[s]
    rows = lax.broadcasted_iota(jnp.int32, own[0].shape, 0)
    other_side = rows == row
    near_wall, near_span = [], []
    for k in range(5):
        up = jnp.where(rows == 7, 0.0, pltpu.roll(own[k], 7, 0))
        down = jnp.where(rows == 0, 0.0, pltpu.roll(own[k], 1, 0))
        beyond = jnp.where(other_side, halo_w[s * 5 + k, lanes][None, :], 0.0)
        near_wall.append(up + down + beyond)
        near_span.append(total([planes[n][k] for n in (s - 1, s + 1) if 0 <= n < 4]))
    from_wall, from_span = mix(splat, 0, near_wall), mix(splat, 1, near_span)
    return [
        total([jac[s, k, i, :, lanes] * own[k] for k in range(5)]) - (from_wall[i] + from_span[i])
        for i in range(5)
    ]


def second_local_kernel(splat, first, halo_w, rhs, jac, jinv, inner):
    row = position()[3]

    def body(lanes):
        planes = [[first[n, k, :, lanes] for k in range(5)] for n in range(4)]
        for s in range(4):
            applied = local_apply(splat, row, planes, halo_w, jac, lanes, s)
            swept = sweep(jinv, s, lanes, [rhs[s, k, :, lanes] - applied[k] for k in range(5)])
            for k in range(5):
                inner[s, k, :, lanes] = planes[s][k] + swept[k]

    for_lanes(body, rhs.shape[-1])


def second_edge_kernel(splat, inner, halo_a, halo_b, jinv, edge_a, edge_b, edge_w):
    even, plane_a, plane_b, row = position()
    real = inside()

    def body(lanes):
        for plane, halo, edge, there in ((plane_a, halo_a, edge_a, None), (plane_b, halo_b, edge_b, real)):
            swept = sweep(jinv, plane, lanes, beyond_span(splat, halo, lanes, there))
            for k in range(5):
                edge[k, :, lanes] = inner[plane, k, :, lanes] + swept[k]

    for_lanes(body, inner.shape[-1])
    for k in range(5):
        for s in (1, 2):
            edge_w[s * 5 + k, :] = inner[s, k, row, :]
        a, b = edge_a[k, row, :], edge_b[k, row, :]
        edge_w[k, :] = jnp.where(even, b, a)
        edge_w[15 + k, :] = jnp.where(even, a, b)


def planes_of(even, inner, edge_a, edge_b, lanes):
    a = [edge_a[k, :, lanes] for k in range(5)]
    b = [edge_b[k, :, lanes] for k in range(5)]
    return [
        [jnp.where(even, b[k], a[k]) for k in range(5)],
        [inner[1, k, :, lanes] for k in range(5)],
        [inner[2, k, :, lanes] for k in range(5)],
        [jnp.where(even, a[k], b[k]) for k in range(5)],
    ]


def defect_local_kernel(splat, inner, edge_a, edge_b, halo_w, rhs, jac, jinv, onehot_t, base, partial, defect):
    even, _, _, row = position()

    def body(lanes):
        planes = planes_of(even, inner, edge_a, edge_b, lanes)
        for s in range(4):
            applied = local_apply(splat, row, planes, halo_w, jac, lanes, s)
            rest = [rhs[s, k, :, lanes] - applied[k] for k in range(5)]
            swept = sweep(jinv, s, lanes, rest)
            for k in range(5):
                base[s, k, :, lanes] = planes[s][k] + swept[k]
                defect[s, k, :, lanes] = rest[k]

    for_lanes(body, rhs.shape[-1])
    tiles = defect.shape[-1] // LANES
    for k in range(5):
        rows = jnp.concatenate(
            [defect[s, k, :, q * LANES : (q + 1) * LANES] for s in range(4) for q in range(tiles)], axis=0
        )
        partial[:, k * LANES : (k + 1) * LANES] = picked_sums(onehot_t[...], rows)


def restrict_kernel(splat, inner, base, halo_a, halo_b, onehot_t, jinv, partial, base_out, edges, sems):
    even, plane_a, plane_b, _ = position()
    real = inside()
    copies = [pltpu.make_async_copy(base.at[pl.ds(1, 2)], base_out.at[pl.ds(1, 2)], sems.at[2])]
    copies[0].start()
    tiles = halo_a.shape[-1] // LANES
    parts = []
    for n, (plane, halo, there) in enumerate(((plane_a, halo_a, None), (plane_b, halo_b, real))):
        for q in range(tiles):
            lanes = slice(q * LANES, (q + 1) * LANES)
            beyond = beyond_span(splat, halo, lanes, there)
            parts.append(beyond)
            swept = sweep(jinv, plane, lanes, beyond)
            for k in range(5):
                edges[n, k, :, lanes] = base[plane, k, :, lanes] + swept[k]
        copies.append(pltpu.make_async_copy(edges.at[n], base_out.at[plane], sems.at[n]))
        copies[-1].start()
    width = 8 * tiles
    low, high = onehot_t[:, :width], onehot_t[:, 3 * width :]
    hot = jnp.concatenate([jnp.where(even, high, low), jnp.where(even, low, high)], axis=1)
    slots = partial.shape[1]
    rows = jnp.concatenate([jnp.concatenate(part, axis=1) for part in parts], axis=0)
    sums = inner[...] + picked_sums(hot, rows)
    for p in range(partial.shape[0]):
        partial[p] = sums[p * slots : (p + 1) * slots]
    for copy in copies:
        copy.wait()


def sum_kernel(received, sums):
    sums[...] = total([received[p] for p in range(received.shape[0])])


def coarse_kernel(inv, own, other, out):
    first_group = lax.axis_index("wall") == 0
    groups = [
        [jnp.where(first_group, x[:, k * LANES : (k + 1) * LANES], y[:, k * LANES : (k + 1) * LANES]) for k in range(5)]
        for x, y in ((own, other), (other, own))
    ]
    for i in range(5):
        rows = inv[i]
        fix = total([rows[:, c * 5 + k : c * 5 + k + 1] * groups[c][k] for c in range(2) for k in range(5)])
        for p in range(out.shape[0]):
            out[p, :, i * LANES : (i + 1) * LANES] = fix


def prolong_kernel(owner, slot, fixes, out, edge_a, edge_b, edge_w, fix):
    _, plane_a, plane_b, row = position()
    tiles = out.shape[-1] // LANES
    owners, slots, _ = fixes.shape
    for p in range(owners):
        fix[p * slots : (p + 1) * slots, :] = fixes[p]
    hot = hot_rows(owner, slot, tiles)[:, : owners * slots]
    for k in range(5):
        rows = picked_sums(hot, fix[:, k * LANES : (k + 1) * LANES])
        for s in range(4):
            for q in range(tiles):
                at = (s * tiles + q) * 8
                out[s, k, :, q * LANES : (q + 1) * LANES] = rows[at : at + 8]
    for k in range(5):
        edge_a[k] = out[plane_a, k]
        edge_b[k] = out[plane_b, k]
        for s in range(4):
            edge_w[s * 5 + k, :] = out[s, k, row, :]


def final_local_kernel(splat, fix, halo_w, jac, jinv, base_in, out, inner, base, sems):
    row = position()[3]
    load = pltpu.make_async_copy(base_in, base, sems.at[4])
    load.start()
    stores = []
    for s in range(4):

        def body(lanes, s=s):
            planes = [[fix[n, k, :, lanes] for k in range(5)] if abs(n - s) < 2 else None for n in range(4)]
            applied = local_apply(splat, row, planes, halo_w, jac, lanes, s)
            swept = sweep(jinv, s, lanes, applied)
            for k in range(5):
                inner[s, k, :, lanes] = base[s, k, :, lanes] + (planes[s][k] - swept[k])

        if s == 0:
            load.wait()
        for_lanes(body, fix.shape[-1])
        if s in (1, 2):
            stores.append(pltpu.make_async_copy(inner.at[s], out.at[s], sems.at[s]))
            stores[-1].start()
    for store in stores:
        store.wait()


def final_edge_kernel(splat, inner, halo_a, halo_b, jinv, out_in, out, edges, sems):
    del out_in
    _, plane_a, plane_b, _ = position()
    real = inside()
    stores = []
    for n, (plane, halo, there) in enumerate(((plane_a, halo_a, None), (plane_b, halo_b, real))):

        def body(lanes, n=n, plane=plane, halo=halo, there=there):
            swept = sweep(jinv, plane, lanes, beyond_span(splat, halo, lanes, there))
            for k in range(5):
                edges[n, k, :, lanes] = inner[plane, k, :, lanes] + swept[k]

        for_lanes(body, inner.shape[-1])
        stores.append(pltpu.make_async_copy(edges.at[n], out.at[plane], sems.at[n]))
        stores[-1].start()
    for store in stores:
        store.wait()


def exchange(edge_a, edge_b, edge_w):
    size = lax.axis_size("span")
    even = [p for i in range(0, size, 2) for p in ((i, i + 1), (i + 1, i))]
    odd = [((i + 1) % size, (j + 1) % size) for i, j in even]
    return (
        lax.ppermute(edge_a, "span", even),
        lax.ppermute(edge_b, "span", odd),
        lax.ppermute(edge_w, "wall", [(0, 1), (1, 0)]),
    )


def local(rhs, jac, jac_inv, wall_coupling, span_coupling, block_owner, block_slot, coarse_inv):
    rhs = in_hbm(rhs.transpose(0, 2, 1, 3))
    jac_in = jac.transpose(0, 2, 3, 1, 4)
    jinv_in = jac_inv.transpose(0, 2, 3, 1, 4)
    inv = coarse_inv[0, 0].transpose(0, 2, 1)
    field, plane, edge = shaped(*rhs.shape), shaped(*rhs.shape[1:]), shaped(20, rhs.shape[-1])
    field_out = pltpu.HBM(rhs.shape, F32)
    matrices = shaped(*jac_in.shape)
    outer = pltpu.VMEM((2, *rhs.shape[1:]), F32)
    owners, slots = lax.axis_size("patch"), coarse_inv.shape[-1]
    aggregates, columns = owners * slots, 5 * LANES
    chunks = shaped(owners, slots, columns)

    rhs, jinv, jac, splat, onehot_t, first, a, b, w = call(
        first_kernel,
        [
            field, matrices, matrices, shaped(2, 5, 5, 8, LANES), shaped(aggregates, block_owner.size),
            field, plane, plane, edge,
        ],
        [in_hbm(x) for x in (wall_coupling, span_coupling, block_owner, block_slot, rhs, jinv_in, jac_in)],
        places=[HBM] * 7,
        scratch=[
            pltpu.SMEM(wall_coupling.shape, F32),
            pltpu.SMEM(span_coupling.shape, F32),
            pltpu.VMEM(block_owner.shape, jnp.int32),
            pltpu.VMEM(block_owner.shape, jnp.int32),
            pltpu.SemaphoreType.DMA((5,)),
            pltpu.SemaphoreType.DMA((2, 4)),
        ],
    )
    halo_a, halo_b, halo_w = exchange(a, b, w)
    [inner] = call(second_local_kernel, [field], [splat, first, halo_w, rhs, jac, jinv])
    a, b, w = call(second_edge_kernel, [plane, plane, edge], [splat, inner, halo_a, halo_b, jinv])
    halo_a, halo_b, halo_w = exchange(a, b, w)
    base, partial = call(
        defect_local_kernel,
        [field, shaped(aggregates, columns)],
        [splat, inner, a, b, halo_w, rhs, jac, jinv, onehot_t],
        scratch=[pltpu.VMEM(rhs.shape, F32)],
    )
    partial, base = call(
        restrict_kernel,
        [chunks, field_out],
        [splat, partial, base, halo_a, halo_b, onehot_t, jinv],
        out_places=[VMEM, HBM],
        scratch=[outer, pltpu.SemaphoreType.DMA((3,))],
    )
    received = lax.all_to_all(partial, "patch", split_axis=0, concat_axis=0, tiled=True)
    [mine] = call(sum_kernel, [shaped(slots, columns)], [received])
    theirs = lax.ppermute(mine, "wall", [(0, 1), (1, 0)])
    [reply] = call(coarse_kernel, [chunks], [inv, mine, theirs])
    fixes = lax.all_to_all(reply, "patch", split_axis=0, concat_axis=0, tiled=True)
    fix, a, b, w = call(
        prolong_kernel,
        [field, plane, plane, edge],
        [block_owner, block_slot, fixes],
        scratch=[pltpu.VMEM((aggregates, columns), F32)],
    )
    halo_a, halo_b, halo_w = exchange(a, b, w)
    out, inner = call(
        final_local_kernel,
        [field_out, field],
        [splat, fix, halo_w, jac_in, jinv_in, in_hbm(base)],
        places=[VMEM] * 5 + [HBM],
        out_places=[HBM, VMEM],
        scratch=[pltpu.VMEM(rhs.shape, F32), pltpu.SemaphoreType.DMA((5,))],
    )
    [out] = call(
        final_edge_kernel,
        [field_out],
        [splat, inner, halo_a, halo_b, jinv_in, in_hbm(out)],
        places=[VMEM] * 5 + [HBM],
        out_places=[HBM],
        scratch=[outer, pltpu.SemaphoreType.DMA((2,))],
        aliases={5: 0},
    )
    return out.transpose(0, 2, 1, 3)


def solution(mesh):
    return jax.shard_map(
        local,
        mesh=mesh,
        in_specs=(
            P("span", "wall", None, "patch"),
            P("span", "wall", None, None, "patch"),
            P("span", "wall", None, None, "patch"),
            P(),
            P(),
            P("span", "wall", "patch"),
            P("span", "wall", "patch"),
            P("span", "wall", None, None, "patch"),
        ),
        out_specs=P("span", "wall", None, "patch"),
        check_vma=False,
    )
```

```python
import functools
import math

import jax
import jax.numpy as jnp
from jax import lax
from jax.experimental import pallas as pl
from jax.experimental.pallas import tpu as pltpu
from jax.sharding import PartitionSpec as P

LANES = 128
VMEM = pl.BlockSpec(memory_space=pltpu.VMEM)
SMEM = pl.BlockSpec(memory_space=pltpu.SMEM)
HBM = pl.BlockSpec(memory_space=pltpu.HBM)
F32 = jnp.float32


def shaped(*shape):
    return jax.ShapeDtypeStruct(shape, F32)


def in_hbm(array):
    return pltpu.with_memory_space_constraint(array, pltpu.HBM)


def call(kernel, outs, args, places=None, out_places=None, scratch=(), aliases=None):
    size = 2 * sum(math.prod(a.shape) for a in (*args, *outs))
    return pl.pallas_call(
        kernel,
        out_shape=outs,
        in_specs=places or [VMEM] * len(args),
        out_specs=out_places or [VMEM] * len(outs),
        scratch_shapes=scratch,
        input_output_aliases=aliases or {},
        cost_estimate=pl.CostEstimate(flops=size, bytes_accessed=size, transcendentals=0),
        compiler_params=pltpu.CompilerParams(vmem_limit_bytes=8 * 2**20),
    )(*args)


def total(terms):
    return functools.reduce(lambda a, b: a + b, terms)


def position():
    span_at, wall_at = lax.axis_index("span"), lax.axis_index("wall")
    odd = lax.rem(span_at, 2)
    plane_a = 3 - 3 * odd
    return odd == 0, plane_a, 3 - plane_a, 7 - 7 * wall_at


def inside():
    at, size = lax.axis_index("span"), lax.axis_size("span")
    return jnp.logical_and(at > 0, at < size - 1)


def mix(splat, which, values):
    return [total([splat[which, k, i] * values[k] for k in range(5)]) for i in range(5)]


def sweep(jinv, s, lanes, values):
    return [total([jinv[s, i, k, :, lanes] * values[k] for k in range(5)]) for i in range(5)]


def beyond_span(splat, halo, lanes, real=None):
    values = [halo[k, :, lanes] for k in range(5)]
    if real is not None:
        values = [jnp.where(real, v, 0.0) for v in values]
    return mix(splat, 1, values)


def for_lanes(body, length):
    @pl.loop(0, length // LANES)
    def _(q):
        body(pl.ds(pl.multiple_of(q * LANES, LANES), LANES))


def picked_sums(hot, rows):
    hot = hot.astype(jnp.bfloat16)
    high = rows.astype(jnp.bfloat16)
    rest = rows - high.astype(F32)
    middle = rest.astype(jnp.bfloat16)
    low = (rest - middle.astype(F32)).astype(jnp.bfloat16)
    return total([jnp.dot(hot, part, preferred_element_type=F32) for part in (low, middle, high)])


def hot_rows(owner, slot, tiles):
    ids = lax.broadcasted_iota(jnp.int32, (8, LANES), 1)
    hot = []
    for s in range(4):
        named = owner[s] * 4 + slot[s]
        hot += [jnp.where(named[:, q : q + 1] == ids, 1.0, 0.0) for q in range(tiles)]
    return jnp.concatenate(hot, axis=0)


def first_kernel(
    wall_in, span_in, owner_in, slot_in, rhs_in, jinv_in,
    rhs, jinv, splat, onehot_t, first, edge_a, edge_b, edge_w,
    wall, span, owner, slot, small_sems, sems,
):
    small = [
        pltpu.make_async_copy(source, here, small_sems.at[n])
        for n, (source, here) in enumerate(
            ((wall_in, wall), (span_in, span), (owner_in, owner), (slot_in, slot), (rhs_in, rhs))
        )
    ]
    slabs = [pltpu.make_async_copy(jinv_in.at[s], jinv.at[s], sems.at[s]) for s in range(4)]
    for copy in small + slabs:
        copy.start()
    small[0].wait()
    small[1].wait()
    for which, coupling in enumerate((wall, span)):
        for k in range(5):
            for i in range(5):
                splat[which, k, i] = jnp.full((8, LANES), coupling[k, i], F32)
    small[2].wait()
    small[3].wait()
    onehot_t[...] = hot_rows(owner, slot, rhs.shape[-1] // LANES).T[: onehot_t.shape[0]]
    _, plane_a, plane_b, row = position()
    small[4].wait()
    for s in range(4):
        slabs[s].wait()

        def body(lanes, s=s):
            swept = sweep(jinv, s, lanes, [rhs[s, k, :, lanes] for k in range(5)])
            for k in range(5):
                first[s, k, :, lanes] = swept[k]

        for_lanes(body, rhs.shape[-1])
        for k in range(5):
            edge_w[s * 5 + k, :] = first[s, k, row, :]
    for k in range(5):
        edge_a[k] = first[plane_a, k]
        edge_b[k] = first[plane_b, k]


def local_apply(splat, row, planes, halo_w, jac, lanes, s):
    own = planes[s]
    rows = lax.broadcasted_iota(jnp.int32, own[0].shape, 0)
    other_side = rows == row
    near_wall, near_span = [], []
    for k in range(5):
        up = jnp.where(rows == 7, 0.0, pltpu.roll(own[k], 7, 0))
        down = jnp.where(rows == 0, 0.0, pltpu.roll(own[k], 1, 0))
        beyond = jnp.where(other_side, halo_w[s * 5 + k, lanes][None, :], 0.0)
        near_wall.append(up + down + beyond)
        near_span.append(total([planes[n][k] for n in (s - 1, s + 1) if 0 <= n < 4]))
    from_wall, from_span = mix(splat, 0, near_wall), mix(splat, 1, near_span)
    return [
        total([jac[s, k, i, :, lanes] * own[k] for k in range(5)]) - (from_wall[i] + from_span[i])
        for i in range(5)
    ]


def second_local_kernel(splat, first, halo_w, rhs, jac, jinv, inner):
    row = position()[3]

    def body(lanes):
        planes = [[first[n, k, :, lanes] for k in range(5)] for n in range(4)]
        for s in range(4):
            applied = local_apply(splat, row, planes, halo_w, jac, lanes, s)
            swept = sweep(jinv, s, lanes, [rhs[s, k, :, lanes] - applied[k] for k in range(5)])
            for k in range(5):
                inner[s, k, :, lanes] = planes[s][k] + swept[k]

    for_lanes(body, rhs.shape[-1])


def second_edge_kernel(splat, inner, halo_b, halo_a, jinv, edge_a, edge_b, edge_w):
    even, plane_a, plane_b, row = position()
    real = inside()

    def body(lanes):
        for plane, halo, edge, there in ((plane_a, halo_a, edge_a, None), (plane_b, halo_b, edge_b, real)):
            swept = sweep(jinv, plane, lanes, beyond_span(splat, halo, lanes, there))
            for k in range(5):
                edge[k, :, lanes] = inner[plane, k, :, lanes] + swept[k]

    for_lanes(body, inner.shape[-1])
    for k in range(5):
        for s in (1, 2):
            edge_w[s * 5 + k, :] = inner[s, k, row, :]
        a, b = edge_a[k, row, :], edge_b[k, row, :]
        edge_w[k, :] = jnp.where(even, b, a)
        edge_w[15 + k, :] = jnp.where(even, a, b)


def planes_of(even, inner, edge_a, edge_b, lanes):
    a = [edge_a[k, :, lanes] for k in range(5)]
    b = [edge_b[k, :, lanes] for k in range(5)]
    return [
        [jnp.where(even, b[k], a[k]) for k in range(5)],
        [inner[1, k, :, lanes] for k in range(5)],
        [inner[2, k, :, lanes] for k in range(5)],
        [jnp.where(even, a[k], b[k]) for k in range(5)],
    ]


def defect_local_kernel(splat, inner, edge_b, edge_a, halo_w, rhs, jac, jinv, onehot_t, base, partial, defect):
    even, _, _, row = position()

    def body(lanes):
        planes = planes_of(even, inner, edge_a, edge_b, lanes)
        for s in range(4):
            applied = local_apply(splat, row, planes, halo_w, jac, lanes, s)
            rest = [rhs[s, k, :, lanes] - applied[k] for k in range(5)]
            swept = sweep(jinv, s, lanes, rest)
            for k in range(5):
                base[s, k, :, lanes] = planes[s][k] + swept[k]
                defect[s, k, :, lanes] = rest[k]

    for_lanes(body, rhs.shape[-1])
    tiles = defect.shape[-1] // LANES
    for k in range(5):
        rows = jnp.concatenate(
            [defect[s, k, :, q * LANES : (q + 1) * LANES] for s in range(4) for q in range(tiles)], axis=0
        )
        partial[:, k * LANES : (k + 1) * LANES] = picked_sums(onehot_t[...], rows)


def restrict_kernel(splat, inner, base, halo_b, halo_a, onehot_t, jinv, partial, base_out, edges, sems):
    even, plane_a, plane_b, _ = position()
    real = inside()
    copies = [pltpu.make_async_copy(base.at[pl.ds(1, 2)], base_out.at[pl.ds(1, 2)], sems.at[2])]
    copies[0].start()
    tiles = halo_a.shape[-1] // LANES
    parts = []
    for n, (plane, halo, there) in enumerate(((plane_a, halo_a, None), (plane_b, halo_b, real))):
        for q in range(tiles):
            lanes = slice(q * LANES, (q + 1) * LANES)
            beyond = beyond_span(splat, halo, lanes, there)
            parts.append(beyond)
            swept = sweep(jinv, plane, lanes, beyond)
            for k in range(5):
                edges[n, k, :, lanes] = base[plane, k, :, lanes] + swept[k]
        copies.append(pltpu.make_async_copy(edges.at[n], base_out.at[plane], sems.at[n]))
        copies[-1].start()
    width = 8 * tiles
    low, high = onehot_t[:, :width], onehot_t[:, 3 * width :]
    hot = jnp.concatenate([jnp.where(even, high, low), jnp.where(even, low, high)], axis=1)
    slots = partial.shape[1]
    rows = jnp.concatenate([jnp.concatenate(part, axis=1) for part in parts], axis=0)
    sums = inner[...] + picked_sums(hot, rows)
    for p in range(partial.shape[0]):
        partial[p] = sums[p * slots : (p + 1) * slots]
    for copy in copies:
        copy.wait()


def sum_kernel(received, sums):
    sums[...] = total([received[p] for p in range(received.shape[0])])


def coarse_kernel(inv, own, other, out):
    first_group = lax.axis_index("wall") == 0
    groups = [
        [jnp.where(first_group, x[:, k * LANES : (k + 1) * LANES], y[:, k * LANES : (k + 1) * LANES]) for k in range(5)]
        for x, y in ((own, other), (other, own))
    ]
    for i in range(5):
        rows = inv[i]
        fix = total([rows[:, c * 5 + k : c * 5 + k + 1] * groups[c][k] for c in range(2) for k in range(5)])
        for p in range(out.shape[0]):
            out[p, :, i * LANES : (i + 1) * LANES] = fix


def prolong_kernel(owner, slot, fixes, out, edge_a, edge_b, edge_w, fix):
    _, plane_a, plane_b, row = position()
    tiles = out.shape[-1] // LANES
    owners, slots, _ = fixes.shape
    for p in range(owners):
        fix[p * slots : (p + 1) * slots, :] = fixes[p]
    hot = hot_rows(owner, slot, tiles)[:, : owners * slots]
    for k in range(5):
        rows = picked_sums(hot, fix[:, k * LANES : (k + 1) * LANES])
        for s in range(4):
            for q in range(tiles):
                at = (s * tiles + q) * 8
                out[s, k, :, q * LANES : (q + 1) * LANES] = rows[at : at + 8]
    for k in range(5):
        edge_a[k] = out[plane_a, k]
        edge_b[k] = out[plane_b, k]
        for s in range(4):
            edge_w[s * 5 + k, :] = out[s, k, row, :]


def final_local_kernel(splat, fix, halo_w, jac, jinv, base_in, out, inner, base, sems):
    row = position()[3]
    load = pltpu.make_async_copy(base_in, base, sems.at[0])
    load.start()
    stores = []
    for s in (1, 2, 0, 3):

        def body(lanes, s=s):
            planes = [[fix[n, k, :, lanes] for k in range(5)] if abs(n - s) < 2 else None for n in range(4)]
            applied = local_apply(splat, row, planes, halo_w, jac, lanes, s)
            swept = sweep(jinv, s, lanes, applied)
            for k in range(5):
                change = planes[s][k] - swept[k]
                inner[s, k, :, lanes] = change if s == 1 else base[s, k, :, lanes] + change

        for_lanes(body, fix.shape[-1])
        if s == 1:
            load.wait()
            for k in range(5):
                inner[1, k] += base[1, k]
        if s in (1, 2):
            stores.append(pltpu.make_async_copy(inner.at[s], out.at[s], sems.at[s]))
            stores[-1].start()
    for store in stores:
        store.wait()


def final_edge_kernel(splat, inner, halo_b, halo_a, jinv, out_in, out, edges, sems):
    del out_in
    _, plane_a, plane_b, _ = position()
    real = inside()
    stores = []
    for n, (plane, halo, there) in enumerate(((plane_a, halo_a, None), (plane_b, halo_b, real))):

        def body(lanes, n=n, plane=plane, halo=halo, there=there):
            swept = sweep(jinv, plane, lanes, beyond_span(splat, halo, lanes, there))
            for k in range(5):
                edges[n, k, :, lanes] = inner[plane, k, :, lanes] + swept[k]

        for_lanes(body, inner.shape[-1])
        stores.append(pltpu.make_async_copy(edges.at[n], out.at[plane], sems.at[n]))
        stores[-1].start()
    for store in stores:
        store.wait()


def exchange(edge_a, edge_b, edge_w):
    size = lax.axis_size("span")
    even = [p for i in range(0, size, 2) for p in ((i, i + 1), (i + 1, i))]
    odd = [((i + 1) % size, (j + 1) % size) for i, j in even]
    halo_b = lax.ppermute(edge_b, "span", odd)
    halo_w = lax.ppermute(edge_w, "wall", [(0, 1), (1, 0)])
    halo_a = lax.ppermute(edge_a, "span", even)
    return halo_a, halo_b, halo_w


def local(rhs, jac, jac_inv, wall_coupling, span_coupling, block_owner, block_slot, coarse_inv):
    rhs = in_hbm(rhs.transpose(0, 2, 1, 3))
    jac_in = jac.transpose(0, 2, 3, 1, 4)
    jinv_in = jac_inv.transpose(0, 2, 3, 1, 4)
    inv = coarse_inv[0, 0].transpose(0, 2, 1)
    field, plane, edge = shaped(*rhs.shape), shaped(*rhs.shape[1:]), shaped(20, rhs.shape[-1])
    field_out = pltpu.HBM(rhs.shape, F32)
    matrices = shaped(*jac_in.shape)
    outer = pltpu.VMEM((2, *rhs.shape[1:]), F32)
    owners, slots = lax.axis_size("patch"), coarse_inv.shape[-1]
    aggregates, columns = owners * slots, 5 * LANES
    chunks = shaped(owners, slots, columns)

    rhs, jinv, splat, onehot_t, first, a, b, w = call(
        first_kernel,
        [
            field, matrices, shaped(2, 5, 5, 8, LANES), shaped(aggregates, block_owner.size),
            field, plane, plane, edge,
        ],
        [in_hbm(x) for x in (wall_coupling, span_coupling, block_owner, block_slot, rhs, jinv_in)],
        places=[HBM] * 6,
        scratch=[
            pltpu.SMEM(wall_coupling.shape, F32),
            pltpu.SMEM(span_coupling.shape, F32),
            pltpu.VMEM(block_owner.shape, jnp.int32),
            pltpu.VMEM(block_owner.shape, jnp.int32),
            pltpu.SemaphoreType.DMA((5,)),
            pltpu.SemaphoreType.DMA((4,)),
        ],
    )
    halo_a, halo_b, halo_w = exchange(a, b, w)
    [inner] = call(second_local_kernel, [field], [splat, first, halo_w, rhs, jac_in, jinv])
    a, b, w = call(second_edge_kernel, [plane, plane, edge], [splat, inner, halo_b, halo_a, jinv])
    halo_a, halo_b, halo_w = exchange(a, b, w)
    base, partial = call(
        defect_local_kernel,
        [field, shaped(aggregates, columns)],
        [splat, inner, b, a, halo_w, rhs, jac_in, jinv, onehot_t],
        scratch=[pltpu.VMEM(rhs.shape, F32)],
    )
    partial, base = call(
        restrict_kernel,
        [chunks, field_out],
        [splat, partial, base, halo_b, halo_a, onehot_t, jinv],
        out_places=[VMEM, HBM],
        scratch=[outer, pltpu.SemaphoreType.DMA((3,))],
    )
    received = lax.all_to_all(partial, "patch", split_axis=0, concat_axis=0, tiled=True)
    [mine] = call(sum_kernel, [shaped(slots, columns)], [received])
    theirs = lax.ppermute(mine, "wall", [(0, 1), (1, 0)])
    [reply] = call(coarse_kernel, [chunks], [inv, mine, theirs])
    fixes = lax.all_to_all(reply, "patch", split_axis=0, concat_axis=0, tiled=True)
    fix, a, b, w = call(
        prolong_kernel,
        [field, plane, plane, edge],
        [block_owner, block_slot, fixes],
        scratch=[pltpu.VMEM((aggregates, columns), F32)],
    )
    halo_a, halo_b, halo_w = exchange(a, b, w)
    out, inner = call(
        final_local_kernel,
        [field_out, field],
        [splat, fix, halo_w, jac_in, jinv_in, in_hbm(base)],
        places=[VMEM] * 5 + [HBM],
        out_places=[HBM, VMEM],
        scratch=[pltpu.VMEM(rhs.shape, F32), pltpu.SemaphoreType.DMA((3,))],
    )
    [out] = call(
        final_edge_kernel,
        [field_out],
        [splat, inner, halo_b, halo_a, jinv_in, in_hbm(out)],
        places=[VMEM] * 5 + [HBM],
        out_places=[HBM],
        scratch=[outer, pltpu.SemaphoreType.DMA((2,))],
        aliases={5: 0},
    )
    return out.transpose(0, 2, 1, 3)


def solution(mesh):
    return jax.shard_map(
        local,
        mesh=mesh,
        in_specs=(
            P("span", "wall", None, "patch"),
            P("span", "wall", None, None, "patch"),
            P("span", "wall", None, None, "patch"),
            P(),
            P(),
            P("span", "wall", "patch"),
            P("span", "wall", "patch"),
            P("span", "wall", None, None, "patch"),
        ),
        out_specs=P("span", "wall", None, "patch"),
        check_vma=False,
    )
```

```python
import functools
import math

import jax
import jax.numpy as jnp
from jax import lax
from jax.experimental import pallas as pl
from jax.experimental.pallas import tpu as pltpu
from jax.sharding import PartitionSpec as P

LANES = 128
VMEM = pl.BlockSpec(memory_space=pltpu.VMEM)
SMEM = pl.BlockSpec(memory_space=pltpu.SMEM)
HBM = pl.BlockSpec(memory_space=pltpu.HBM)
F32 = jnp.float32


def shaped(*shape):
    return jax.ShapeDtypeStruct(shape, F32)


def in_hbm(array):
    return pltpu.with_memory_space_constraint(array, pltpu.HBM)


def call(kernel, outs, args, places=None, out_places=None, scratch=(), aliases=None):
    size = 2 * sum(math.prod(a.shape) for a in (*args, *outs))
    return pl.pallas_call(
        kernel,
        out_shape=outs,
        in_specs=places or [VMEM] * len(args),
        out_specs=out_places or [VMEM] * len(outs),
        scratch_shapes=scratch,
        input_output_aliases=aliases or {},
        cost_estimate=pl.CostEstimate(flops=size, bytes_accessed=size, transcendentals=0),
        compiler_params=pltpu.CompilerParams(vmem_limit_bytes=8 * 2**20),
    )(*args)


def total(terms):
    return functools.reduce(lambda a, b: a + b, terms)


def position():
    span_at, wall_at = lax.axis_index("span"), lax.axis_index("wall")
    odd = lax.rem(span_at, 2)
    plane_a = 3 - 3 * odd
    return odd == 0, plane_a, 3 - plane_a, 7 - 7 * wall_at


def inside():
    at, size = lax.axis_index("span"), lax.axis_size("span")
    return jnp.logical_and(at > 0, at < size - 1)


def mix(splat, which, values):
    return [total([splat[which, k, i] * values[k] for k in range(5)]) for i in range(5)]


def sweep(jinv, s, lanes, values):
    return [total([jinv[s, i, k, :, lanes] * values[k] for k in range(5)]) for i in range(5)]


def beyond_span(splat, halo, lanes, real=None):
    values = [halo[k, :, lanes] for k in range(5)]
    if real is not None:
        values = [jnp.where(real, v, 0.0) for v in values]
    return mix(splat, 1, values)


def wall_rows(splat, raw, out):
    for q in range(out.shape[-1] // LANES):
        lanes = slice(q * LANES, (q + 1) * LANES)
        mixed = mix(splat, 0, [raw[k, :, lanes] for k in range(5)])
        for i in range(5):
            out[4 * i : 4 * i + 4, lanes] = mixed[i][:4]


def for_lanes(body, length):
    @pl.loop(0, length // LANES)
    def _(q):
        body(pl.ds(pl.multiple_of(q * LANES, LANES), LANES))


def picked_sums(hot, rows):
    hot = hot.astype(jnp.bfloat16)
    high = rows.astype(jnp.bfloat16)
    rest = rows - high.astype(F32)
    middle = rest.astype(jnp.bfloat16)
    low = (rest - middle.astype(F32)).astype(jnp.bfloat16)
    return total([jnp.dot(hot, part, preferred_element_type=F32) for part in (low, middle, high)])


def hot_rows(owner, slot, tiles):
    ids = lax.broadcasted_iota(jnp.int32, (8, LANES), 1)
    hot = []
    for s in range(4):
        named = owner[s] * 4 + slot[s]
        hot += [jnp.where(named[:, q : q + 1] == ids, 1.0, 0.0) for q in range(tiles)]
    return jnp.concatenate(hot, axis=0)


def first_kernel(
    wall_in, span_in, owner_in, slot_in, rhs_in, jinv_in,
    rhs, jinv, splat, onehot_t, first, edge_a, edge_b, edge_w,
    wall, span, owner, slot, raw, small_sems, sems,
):
    small = [
        pltpu.make_async_copy(source, here, small_sems.at[n])
        for n, (source, here) in enumerate(
            ((wall_in, wall), (span_in, span), (owner_in, owner), (slot_in, slot), (rhs_in, rhs))
        )
    ]
    slabs = [pltpu.make_async_copy(jinv_in.at[s], jinv.at[s], sems.at[s]) for s in range(4)]
    for copy in small + slabs:
        copy.start()
    small[0].wait()
    small[1].wait()
    for which, coupling in enumerate((wall, span)):
        for k in range(5):
            for i in range(5):
                splat[which, k, i] = jnp.full((8, LANES), coupling[k, i], F32)
    small[2].wait()
    small[3].wait()
    onehot_t[...] = hot_rows(owner, slot, rhs.shape[-1] // LANES).T[: onehot_t.shape[0]]
    _, plane_a, plane_b, row = position()
    small[4].wait()
    for s in range(4):
        slabs[s].wait()

        def body(lanes, s=s):
            swept = sweep(jinv, s, lanes, [rhs[s, k, :, lanes] for k in range(5)])
            for k in range(5):
                first[s, k, :, lanes] = swept[k]

        for_lanes(body, rhs.shape[-1])
        for k in range(5):
            raw[k, s, :] = first[s, k, row, :]
    for k in range(5):
        edge_a[k] = first[plane_a, k]
        edge_b[k] = first[plane_b, k]
    wall_rows(splat, raw, edge_w)


def local_apply(splat, planes, jac, lanes, s):
    own = planes[s]
    rows = lax.broadcasted_iota(jnp.int32, own[0].shape, 0)
    near_wall, near_span = [], []
    for k in range(5):
        up = jnp.where(rows == 7, 0.0, pltpu.roll(own[k], 7, 0))
        down = jnp.where(rows == 0, 0.0, pltpu.roll(own[k], 1, 0))
        near_wall.append(up + down)
        near_span.append(total([planes[n][k] for n in (s - 1, s + 1) if 0 <= n < 4]))
    from_wall, from_span = mix(splat, 0, near_wall), mix(splat, 1, near_span)
    return [
        total([jac[s, k, i, :, lanes] * own[k] for k in range(5)]) - (from_wall[i] + from_span[i])
        for i in range(5)
    ]


def with_wall(rest, halo_w, s, lanes, row):
    rows = lax.broadcasted_iota(jnp.int32, (8, LANES), 0)
    return [
        rest[s, i, :, lanes] + jnp.where(rows == row, halo_w[4 * i + s, lanes][None, :], 0.0) for i in range(5)
    ]


def first_residual_kernel(splat, first, rhs, jac, rest):
    def body(lanes):
        planes = [[first[n, k, :, lanes] for k in range(5)] for n in range(4)]
        for s in range(4):
            applied = local_apply(splat, planes, jac, lanes, s)
            for k in range(5):
                rest[s, k, :, lanes] = rhs[s, k, :, lanes] - applied[k]

    for_lanes(body, rhs.shape[-1])


def second_local_kernel(first, rest, halo_w, jinv, inner):
    row = position()[3]

    def body(lanes):
        for s in range(4):
            swept = sweep(jinv, s, lanes, with_wall(rest, halo_w, s, lanes, row))
            for k in range(5):
                inner[s, k, :, lanes] = first[s, k, :, lanes] + swept[k]

    for_lanes(body, rest.shape[-1])


def second_edge_kernel(splat, inner, halo_b, halo_a, jinv, edge_a, edge_b, edge_w, raw):
    even, plane_a, plane_b, row = position()
    real = inside()

    def body(lanes):
        for plane, halo, edge, there in ((plane_a, halo_a, edge_a, None), (plane_b, halo_b, edge_b, real)):
            swept = sweep(jinv, plane, lanes, beyond_span(splat, halo, lanes, there))
            for k in range(5):
                edge[k, :, lanes] = inner[plane, k, :, lanes] + swept[k]

    for_lanes(body, inner.shape[-1])
    for k in range(5):
        for s in (1, 2):
            raw[k, s, :] = inner[s, k, row, :]
        a, b = edge_a[k, row, :], edge_b[k, row, :]
        raw[k, 0, :] = jnp.where(even, b, a)
        raw[k, 3, :] = jnp.where(even, a, b)
    wall_rows(splat, raw, edge_w)


def planes_of(even, inner, edge_a, edge_b, lanes):
    a = [edge_a[k, :, lanes] for k in range(5)]
    b = [edge_b[k, :, lanes] for k in range(5)]
    return [
        [jnp.where(even, b[k], a[k]) for k in range(5)],
        [inner[1, k, :, lanes] for k in range(5)],
        [inner[2, k, :, lanes] for k in range(5)],
        [jnp.where(even, a[k], b[k]) for k in range(5)],
    ]


def second_residual_kernel(splat, inner, edge_b, edge_a, rhs, jac, rest):
    even = position()[0]

    def body(lanes):
        planes = planes_of(even, inner, edge_a, edge_b, lanes)
        for s in range(4):
            applied = local_apply(splat, planes, jac, lanes, s)
            for k in range(5):
                rest[s, k, :, lanes] = rhs[s, k, :, lanes] - applied[k]

    for_lanes(body, rhs.shape[-1])


def defect_local_kernel(inner, edge_b, edge_a, rest, halo_w, jinv, onehot_t, partial, base_out, base, defect, sems):
    even, _, _, row = position()

    def body(lanes):
        planes = planes_of(even, inner, edge_a, edge_b, lanes)
        for s in range(4):
            known = with_wall(rest, halo_w, s, lanes, row)
            swept = sweep(jinv, s, lanes, known)
            for k in range(5):
                base[s, k, :, lanes] = planes[s][k] + swept[k]
                defect[s, k, :, lanes] = known[k]

    for_lanes(body, rest.shape[-1])
    store = pltpu.make_async_copy(base, base_out, sems.at[0])
    store.start()
    tiles = defect.shape[-1] // LANES
    for k in range(5):
        rows = jnp.concatenate(
            [defect[s, k, :, q * LANES : (q + 1) * LANES] for s in range(4) for q in range(tiles)], axis=0
        )
        partial[:, k * LANES : (k + 1) * LANES] = picked_sums(onehot_t[...], rows)
    store.wait()


def restrict_kernel(splat, inner, halo_b, halo_a, onehot_t, partial, late_out, late, sems):
    real = inside()
    at_a = 1 - lax.rem(lax.axis_index("span"), 2)
    tiles = halo_a.shape[-1] // LANES
    stores, parts = [], []
    for n, (halo, there, at) in enumerate(((halo_b, real, 1 - at_a), (halo_a, None, at_a))):
        for q in range(tiles):
            lanes = slice(q * LANES, (q + 1) * LANES)
            beyond = beyond_span(splat, halo, lanes, there)
            parts.append(beyond)
            for k in range(5):
                late[n, k, :, lanes] = beyond[k]
        stores.append(pltpu.make_async_copy(late.at[n], late_out.at[at], sems.at[n]))
        stores[-1].start()
    width = 8 * tiles
    even = at_a == 1
    low, high = onehot_t[:, :width], onehot_t[:, 3 * width :]
    hot = jnp.concatenate([jnp.where(even, low, high), jnp.where(even, high, low)], axis=1)
    slots = partial.shape[1]
    rows = jnp.concatenate([jnp.concatenate(part, axis=1) for part in parts], axis=0)
    sums = inner[...] + picked_sums(hot, rows)
    for p in range(partial.shape[0]):
        partial[p] = sums[p * slots : (p + 1) * slots]
    for store in stores:
        store.wait()


def sum_kernel(received, sums):
    sums[...] = total([received[p] for p in range(received.shape[0])])


def coarse_kernel(inv, own, other, out):
    first_group = lax.axis_index("wall") == 0
    groups = [
        [jnp.where(first_group, x[:, k * LANES : (k + 1) * LANES], y[:, k * LANES : (k + 1) * LANES]) for k in range(5)]
        for x, y in ((own, other), (other, own))
    ]
    for i in range(5):
        rows = inv[i]
        fix = total([rows[:, c * 5 + k : c * 5 + k + 1] * groups[c][k] for c in range(2) for k in range(5)])
        for p in range(out.shape[0]):
            out[p, :, i * LANES : (i + 1) * LANES] = fix


def prolong_kernel(splat, owner, slot, fixes, out, edge_a, edge_b, edge_w, fix, raw):
    _, plane_a, plane_b, row = position()
    tiles = out.shape[-1] // LANES
    owners, slots, _ = fixes.shape
    for p in range(owners):
        fix[p * slots : (p + 1) * slots, :] = fixes[p]
    hot = hot_rows(owner, slot, tiles)[:, : owners * slots]
    for k in range(5):
        rows = picked_sums(hot, fix[:, k * LANES : (k + 1) * LANES])
        for s in range(4):
            for q in range(tiles):
                at = (s * tiles + q) * 8
                out[s, k, :, q * LANES : (q + 1) * LANES] = rows[at : at + 8]
    for k in range(5):
        edge_a[k] = out[plane_a, k]
        edge_b[k] = out[plane_b, k]
        for s in range(4):
            raw[k, s, :] = out[s, k, row, :]
    wall_rows(splat, raw, edge_w)


def final_residual_kernel(splat, fix, jac, rest):
    def body(lanes):
        planes = [[fix[n, k, :, lanes] for k in range(5)] for n in range(4)]
        for s in range(4):
            applied = local_apply(splat, planes, jac, lanes, s)
            for k in range(5):
                rest[s, k, :, lanes] = -applied[k]

    for_lanes(body, fix.shape[-1])


def final_local_kernel(fix, rest, halo_w, jinv, base_in, late_in, out, inner, base, late, sems):
    row = position()[3]
    loads = [
        pltpu.make_async_copy(base_in.at[pl.ds(1, 2)], base.at[pl.ds(1, 2)], sems.at[0]),
        pltpu.make_async_copy(late_in, late, sems.at[1]),
        pltpu.make_async_copy(base_in.at[0], base.at[0], sems.at[2]),
        pltpu.make_async_copy(base_in.at[3], base.at[3], sems.at[3]),
    ]
    for load in loads:
        load.start()
    stores = []
    for s in (1, 2, 0, 3):

        def body(lanes, s=s):
            known = with_wall(rest, halo_w, s, lanes, row)
            if s in (0, 3):
                known = [known[k] + late[s // 3, k, :, lanes] for k in range(5)]
            swept = sweep(jinv, s, lanes, known)
            for k in range(5):
                inner[s, k, :, lanes] = (base[s, k, :, lanes] + fix[s, k, :, lanes]) + swept[k]

        if s == 1:
            loads[0].wait()
        if s == 0:
            for load in loads[1:]:
                load.wait()
        for_lanes(body, fix.shape[-1])
        if s in (1, 2):
            stores.append(pltpu.make_async_copy(inner.at[s], out.at[s], sems.at[3 + s]))
            stores[-1].start()
    for store in stores:
        store.wait()


def final_edge_kernel(splat, inner, halo_b, halo_a, jinv, out_in, out, edges, sems):
    del out_in
    _, plane_a, plane_b, _ = position()
    real = inside()
    stores = []
    for n, (plane, halo, there) in enumerate(((plane_a, halo_a, None), (plane_b, halo_b, real))):

        def body(lanes, n=n, plane=plane, halo=halo, there=there):
            swept = sweep(jinv, plane, lanes, beyond_span(splat, halo, lanes, there))
            for k in range(5):
                edges[n, k, :, lanes] = inner[plane, k, :, lanes] + swept[k]

        for_lanes(body, inner.shape[-1])
        stores.append(pltpu.make_async_copy(edges.at[n], out.at[plane], sems.at[n]))
        stores[-1].start()
    for store in stores:
        store.wait()


def exchange(edge_a, edge_b, edge_w):
    size = lax.axis_size("span")
    even = [p for i in range(0, size, 2) for p in ((i, i + 1), (i + 1, i))]
    odd = [((i + 1) % size, (j + 1) % size) for i, j in even]
    halo_b = lax.ppermute(edge_b, "span", odd)
    halo_w = lax.ppermute(edge_w, "wall", [(0, 1), (1, 0)])
    halo_a = lax.ppermute(edge_a, "span", even)
    return halo_a, halo_b, halo_w


def local(rhs, jac, jac_inv, wall_coupling, span_coupling, block_owner, block_slot, coarse_inv):
    rhs = in_hbm(rhs.transpose(0, 2, 1, 3))
    jac_in = jac.transpose(0, 2, 3, 1, 4)
    jinv_in = jac_inv.transpose(0, 2, 3, 1, 4)
    inv = coarse_inv[0, 0].transpose(0, 2, 1)
    field, plane, edge = shaped(*rhs.shape), shaped(*rhs.shape[1:]), shaped(20, rhs.shape[-1])
    field_out = pltpu.HBM(rhs.shape, F32)
    matrices = shaped(*jac_in.shape)
    outer = pltpu.VMEM((2, *rhs.shape[1:]), F32)
    raw = pltpu.VMEM(rhs.shape[1:], F32)
    owners, slots = lax.axis_size("patch"), coarse_inv.shape[-1]
    aggregates, columns = owners * slots, 5 * LANES
    chunks = shaped(owners, slots, columns)

    rhs, jinv, splat, onehot_t, first, a, b, w = call(
        first_kernel,
        [
            field, matrices, shaped(2, 5, 5, 8, LANES), shaped(aggregates, block_owner.size),
            field, plane, plane, edge,
        ],
        [in_hbm(x) for x in (wall_coupling, span_coupling, block_owner, block_slot, rhs, jinv_in)],
        places=[HBM] * 6,
        scratch=[
            pltpu.SMEM(wall_coupling.shape, F32),
            pltpu.SMEM(span_coupling.shape, F32),
            pltpu.VMEM(block_owner.shape, jnp.int32),
            pltpu.VMEM(block_owner.shape, jnp.int32),
            raw,
            pltpu.SemaphoreType.DMA((5,)),
            pltpu.SemaphoreType.DMA((4,)),
        ],
    )
    jac, b = lax.optimization_barrier((jac_in, b))
    halo_a, halo_b, halo_w = exchange(a, b, w)
    [rest] = call(first_residual_kernel, [field], [splat, first, rhs, jac])
    [inner] = call(second_local_kernel, [field], [first, rest, halo_w, jinv])
    a, b, w = call(
        second_edge_kernel, [plane, plane, edge], [splat, inner, halo_b, halo_a, jinv], scratch=[raw]
    )
    halo_a, halo_b, halo_w = exchange(a, b, w)
    [rest] = call(second_residual_kernel, [field], [splat, inner, b, a, rhs, jac])
    partial, base = call(
        defect_local_kernel,
        [shaped(aggregates, columns), field_out],
        [inner, b, a, rest, halo_w, jinv, onehot_t],
        out_places=[VMEM, HBM],
        scratch=[pltpu.VMEM(rhs.shape, F32), pltpu.VMEM(rhs.shape, F32), pltpu.SemaphoreType.DMA((1,))],
    )
    partial, late = call(
        restrict_kernel,
        [chunks, pltpu.HBM((2, *plane.shape), F32)],
        [splat, partial, halo_b, halo_a, onehot_t],
        out_places=[VMEM, HBM],
        scratch=[outer, pltpu.SemaphoreType.DMA((2,))],
    )
    received = lax.all_to_all(partial, "patch", split_axis=0, concat_axis=0, tiled=True)
    [mine] = call(sum_kernel, [shaped(slots, columns)], [received])
    theirs = lax.ppermute(mine, "wall", [(0, 1), (1, 0)])
    [reply] = call(coarse_kernel, [chunks], [inv, mine, theirs])
    fixes = lax.all_to_all(reply, "patch", split_axis=0, concat_axis=0, tiled=True)
    fix, a, b, w = call(
        prolong_kernel,
        [field, plane, plane, edge],
        [splat, block_owner, block_slot, fixes],
        scratch=[pltpu.VMEM((aggregates, columns), F32), raw],
    )
    halo_a, halo_b, halo_w = exchange(a, b, w)
    [rest] = call(final_residual_kernel, [field], [splat, fix, jac])
    out, inner = call(
        final_local_kernel,
        [field_out, field],
        [fix, rest, halo_w, jinv_in, in_hbm(base), in_hbm(late)],
        places=[VMEM] * 4 + [HBM] * 2,
        out_places=[HBM, VMEM],
        scratch=[pltpu.VMEM(rhs.shape, F32), outer, pltpu.SemaphoreType.DMA((6,))],
    )
    [out] = call(
        final_edge_kernel,
        [field_out],
        [splat, inner, halo_b, halo_a, jinv_in, in_hbm(out)],
        places=[VMEM] * 5 + [HBM],
        out_places=[HBM],
        scratch=[outer, pltpu.SemaphoreType.DMA((2,))],
        aliases={5: 0},
    )
    return out.transpose(0, 2, 1, 3)


def solution(mesh):
    return jax.shard_map(
        local,
        mesh=mesh,
        in_specs=(
            P("span", "wall", None, "patch"),
            P("span", "wall", None, None, "patch"),
            P("span", "wall", None, None, "patch"),
            P(),
            P(),
            P("span", "wall", "patch"),
            P("span", "wall", "patch"),
            P("span", "wall", None, None, "patch"),
        ),
        out_specs=P("span", "wall", None, "patch"),
        check_vma=False,
    )
```

```python
import functools
import math

import jax
import jax.numpy as jnp
from jax import lax
from jax.experimental import pallas as pl
from jax.experimental.pallas import tpu as pltpu
from jax.sharding import PartitionSpec as P

LANES = 128
VMEM = pl.BlockSpec(memory_space=pltpu.VMEM)
SMEM = pl.BlockSpec(memory_space=pltpu.SMEM)
HBM = pl.BlockSpec(memory_space=pltpu.HBM)
F32 = jnp.float32


def shaped(*shape):
    return jax.ShapeDtypeStruct(shape, F32)


def in_hbm(array):
    return pltpu.with_memory_space_constraint(array, pltpu.HBM)


def call(kernel, outs, args, places=None, out_places=None, scratch=()):
    size = 2 * sum(math.prod(a.shape) for a in (*args, *outs))
    return pl.pallas_call(
        kernel,
        out_shape=outs,
        in_specs=places or [VMEM] * len(args),
        out_specs=out_places or [VMEM] * len(outs),
        scratch_shapes=scratch,
        cost_estimate=pl.CostEstimate(flops=size, bytes_accessed=size, transcendentals=0),
        compiler_params=pltpu.CompilerParams(vmem_limit_bytes=8 * 2**20),
    )(*args)


def total(terms):
    return functools.reduce(lambda a, b: a + b, terms)


def position():
    span_at, wall_at = lax.axis_index("span"), lax.axis_index("wall")
    odd = lax.rem(span_at, 2)
    plane_a = 3 - 3 * odd
    return odd == 0, plane_a, 3 - plane_a, 7 - 7 * wall_at


def inside():
    at, size = lax.axis_index("span"), lax.axis_size("span")
    return jnp.logical_and(at > 0, at < size - 1)


def mix(splat, which, values):
    return [total([splat[which, k, i] * values[k] for k in range(5)]) for i in range(5)]


def sweep(jinv, s, lanes, values):
    return [total([jinv[s, i, k, :, lanes] * values[k] for k in range(5)]) for i in range(5)]


def beyond_span(splat, halo, lanes, real=None):
    values = [halo[k, :, lanes] for k in range(5)]
    if real is not None:
        values = [jnp.where(real, v, 0.0) for v in values]
    return mix(splat, 1, values)


def wall_rows(splat, raw, out):
    for q in range(out.shape[-1] // LANES):
        lanes = slice(q * LANES, (q + 1) * LANES)
        mixed = mix(splat, 0, [raw[k, :, lanes] for k in range(5)])
        for i in range(5):
            out[4 * i : 4 * i + 4, lanes] = mixed[i][:4]


def for_lanes(body, length):
    @pl.loop(0, length // LANES)
    def _(q):
        body(pl.ds(pl.multiple_of(q * LANES, LANES), LANES))


def picked_sums(hot, rows):
    hot = hot.astype(jnp.bfloat16)
    high = rows.astype(jnp.bfloat16)
    rest = rows - high.astype(F32)
    middle = rest.astype(jnp.bfloat16)
    low = (rest - middle.astype(F32)).astype(jnp.bfloat16)
    return total([jnp.dot(hot, part, preferred_element_type=F32) for part in (low, middle, high)])


def hot_rows(owner, slot, tiles):
    ids = lax.broadcasted_iota(jnp.int32, (8, LANES), 1)
    hot = []
    for s in range(4):
        named = owner[s] * 4 + slot[s]
        hot += [jnp.where(named[:, q : q + 1] == ids, 1.0, 0.0) for q in range(tiles)]
    return jnp.concatenate(hot, axis=0)


def first_edge_kernel(rhs_in, jinv_in, edge_a, edge_b, rhs, jinv, sems):
    _, plane_a, plane_b, _ = position()
    outer = ((plane_b, edge_b), (plane_a, edge_a))
    copies = [
        pltpu.make_async_copy(source.at[plane], here.at[m], sems.at[n, m])
        for m, (plane, _) in enumerate(outer)
        for n, (source, here) in enumerate(((rhs_in, rhs), (jinv_in, jinv)))
    ]
    for copy in copies:
        copy.start()
    for m, (_, edge) in enumerate(outer):
        copies[2 * m].wait()
        copies[2 * m + 1].wait()

        def body(lanes, m=m, edge=edge):
            swept = sweep(jinv, m, lanes, [rhs[m, k, :, lanes] for k in range(5)])
            for k in range(5):
                edge[k, :, lanes] = swept[k]

        for_lanes(body, rhs.shape[-1])


def first_inner_kernel(
    wall_in, span_in, owner_in, slot_in, rhs_in, jinv_in, edge_b, edge_a,
    rhs, jinv, first, splat, onehot_t, edge_w,
    wall, span, owner, slot, raw, small_sems, sems,
):
    small = [
        pltpu.make_async_copy(source, here, small_sems.at[n])
        for n, (source, here) in enumerate(((wall_in, wall), (span_in, span), (owner_in, owner), (slot_in, slot)))
    ]
    small.append(pltpu.make_async_copy(rhs_in, rhs, small_sems.at[4]))
    slabs = {s: pltpu.make_async_copy(jinv_in.at[s], jinv.at[s], sems.at[s]) for s in (1, 2, 0, 3)}
    for copy in (*small, *slabs.values()):
        copy.start()
    even, _, _, row = position()
    for k in range(5):
        first[0, k] = jnp.where(even, edge_b[k], edge_a[k])
        first[3, k] = jnp.where(even, edge_a[k], edge_b[k])
    small[0].wait()
    small[1].wait()
    for which, coupling in enumerate((wall, span)):
        for k in range(5):
            for i in range(5):
                splat[which, k, i] = jnp.full((8, LANES), coupling[k, i], F32)
    small[2].wait()
    small[3].wait()
    onehot_t[...] = hot_rows(owner, slot, rhs.shape[-1] // LANES).T[: onehot_t.shape[0]]
    small[4].wait()
    for s in (1, 2):
        slabs[s].wait()

        def body(lanes, s=s):
            swept = sweep(jinv, s, lanes, [rhs[s, k, :, lanes] for k in range(5)])
            for k in range(5):
                first[s, k, :, lanes] = swept[k]

        for_lanes(body, rhs.shape[-1])
    for s in range(4):
        for k in range(5):
            raw[k, s, :] = first[s, k, row, :]
    wall_rows(splat, raw, edge_w)
    slabs[0].wait()
    slabs[3].wait()


def local_apply(splat, planes, jac, lanes, s):
    own = planes[s]
    rows = lax.broadcasted_iota(jnp.int32, own[0].shape, 0)
    near_wall, near_span = [], []
    for k in range(5):
        up = jnp.where(rows == 7, 0.0, pltpu.roll(own[k], 7, 0))
        down = jnp.where(rows == 0, 0.0, pltpu.roll(own[k], 1, 0))
        near_wall.append(up + down)
        near_span.append(total([planes[n][k] for n in (s - 1, s + 1) if 0 <= n < 4]))
    from_wall, from_span = mix(splat, 0, near_wall), mix(splat, 1, near_span)
    return [
        total([jac[s, k, i, :, lanes] * own[k] for k in range(5)]) - (from_wall[i] + from_span[i])
        for i in range(5)
    ]


def with_wall(rest, halo_w, s, lanes, row):
    rows = lax.broadcasted_iota(jnp.int32, (8, LANES), 0)
    return [
        rest[s, i, :, lanes] + jnp.where(rows == row, halo_w[4 * i + s, lanes][None, :], 0.0) for i in range(5)
    ]


def first_residual_kernel(splat, first, rhs, jac_in, rest, jac, sems):
    copies = [pltpu.make_async_copy(jac_in.at[s], jac.at[s], sems.at[s]) for s in range(4)]
    for copy in copies:
        copy.start()
    for s in range(4):

        def body(lanes, s=s):
            planes = [[first[n, k, :, lanes] for k in range(5)] if abs(n - s) < 2 else None for n in range(4)]
            applied = local_apply(splat, planes, jac, lanes, s)
            for k in range(5):
                rest[s, k, :, lanes] = rhs[s, k, :, lanes] - applied[k]

        copies[s].wait()
        for_lanes(body, rhs.shape[-1])


def second_local_kernel(first, rest, halo_w, jinv, inner):
    row = position()[3]

    def body(lanes):
        for s in range(4):
            swept = sweep(jinv, s, lanes, with_wall(rest, halo_w, s, lanes, row))
            for k in range(5):
                inner[s, k, :, lanes] = first[s, k, :, lanes] + swept[k]

    for_lanes(body, rest.shape[-1])


def second_edge_kernel(splat, inner, halo_b, halo_a, jinv, edge_a, edge_b, edge_w, raw):
    even, plane_a, plane_b, row = position()
    real = inside()

    def body(lanes):
        for plane, halo, edge, there in ((plane_a, halo_a, edge_a, None), (plane_b, halo_b, edge_b, real)):
            swept = sweep(jinv, plane, lanes, beyond_span(splat, halo, lanes, there))
            for k in range(5):
                edge[k, :, lanes] = inner[plane, k, :, lanes] + swept[k]

    for_lanes(body, inner.shape[-1])
    for k in range(5):
        for s in (1, 2):
            raw[k, s, :] = inner[s, k, row, :]
        a, b = edge_a[k, row, :], edge_b[k, row, :]
        raw[k, 0, :] = jnp.where(even, b, a)
        raw[k, 3, :] = jnp.where(even, a, b)
    wall_rows(splat, raw, edge_w)


def planes_of(even, inner, edge_a, edge_b, lanes):
    a = [edge_a[k, :, lanes] for k in range(5)]
    b = [edge_b[k, :, lanes] for k in range(5)]
    return [
        [jnp.where(even, b[k], a[k]) for k in range(5)],
        [inner[1, k, :, lanes] for k in range(5)],
        [inner[2, k, :, lanes] for k in range(5)],
        [jnp.where(even, a[k], b[k]) for k in range(5)],
    ]


def second_residual_kernel(splat, inner, edge_b, edge_a, rhs, jac, rest):
    even = position()[0]

    def body(lanes):
        planes = planes_of(even, inner, edge_a, edge_b, lanes)
        for s in range(4):
            applied = local_apply(splat, planes, jac, lanes, s)
            for k in range(5):
                rest[s, k, :, lanes] = rhs[s, k, :, lanes] - applied[k]

    for_lanes(body, rhs.shape[-1])


def defect_local_kernel(inner, edge_b, edge_a, rest, halo_w, jinv, onehot_t, partial, base_out, base, defect, sems):
    even, _, _, row = position()

    def body(lanes):
        planes = planes_of(even, inner, edge_a, edge_b, lanes)
        for s in range(4):
            known = with_wall(rest, halo_w, s, lanes, row)
            swept = sweep(jinv, s, lanes, known)
            for k in range(5):
                base[s, k, :, lanes] = planes[s][k] + swept[k]
                defect[s, k, :, lanes] = known[k]

    for_lanes(body, rest.shape[-1])
    store = pltpu.make_async_copy(base, base_out, sems.at[0])
    store.start()
    tiles = defect.shape[-1] // LANES
    for k in range(5):
        rows = jnp.concatenate(
            [defect[s, k, :, q * LANES : (q + 1) * LANES] for s in range(4) for q in range(tiles)], axis=0
        )
        partial[:, k * LANES : (k + 1) * LANES] = picked_sums(onehot_t[...], rows)
    store.wait()


def restrict_kernel(splat, inner, halo_b, halo_a, onehot_t, partial, late_out, late, sems):
    real = inside()
    at_a = 1 - lax.rem(lax.axis_index("span"), 2)
    tiles = halo_a.shape[-1] // LANES
    stores, parts = [], []
    for n, (halo, there, at) in enumerate(((halo_b, real, 1 - at_a), (halo_a, None, at_a))):
        for q in range(tiles):
            lanes = slice(q * LANES, (q + 1) * LANES)
            beyond = beyond_span(splat, halo, lanes, there)
            parts.append(beyond)
            for k in range(5):
                late[n, k, :, lanes] = beyond[k]
        stores.append(pltpu.make_async_copy(late.at[n], late_out.at[at], sems.at[n]))
        stores[-1].start()
    width = 8 * tiles
    even = at_a == 1
    low, high = onehot_t[:, :width], onehot_t[:, 3 * width :]
    hot = jnp.concatenate([jnp.where(even, low, high), jnp.where(even, high, low)], axis=1)
    slots = partial.shape[1]
    rows = jnp.concatenate([jnp.concatenate(part, axis=1) for part in parts], axis=0)
    sums = inner[...] + picked_sums(hot, rows)
    for p in range(partial.shape[0]):
        partial[p] = sums[p * slots : (p + 1) * slots]
    for store in stores:
        store.wait()


def sum_kernel(received, sums):
    sums[...] = total([received[p] for p in range(received.shape[0])])


def coarse_kernel(inv, own, other, out):
    first_group = lax.axis_index("wall") == 0
    groups = [
        [jnp.where(first_group, x[:, k * LANES : (k + 1) * LANES], y[:, k * LANES : (k + 1) * LANES]) for k in range(5)]
        for x, y in ((own, other), (other, own))
    ]
    for i in range(5):
        rows = inv[i]
        fix = total([rows[:, c * 5 + k : c * 5 + k + 1] * groups[c][k] for c in range(2) for k in range(5)])
        for p in range(out.shape[0]):
            out[p, :, i * LANES : (i + 1) * LANES] = fix


def prolong_kernel(splat, owner, slot, fixes, out, edge_a, edge_b, edge_w, fix, raw):
    _, plane_a, plane_b, row = position()
    tiles = out.shape[-1] // LANES
    owners, slots, _ = fixes.shape
    for p in range(owners):
        fix[p * slots : (p + 1) * slots, :] = fixes[p]
    hot = hot_rows(owner, slot, tiles)[:, : owners * slots]
    for k in range(5):
        rows = picked_sums(hot, fix[:, k * LANES : (k + 1) * LANES])
        for s in range(4):
            for q in range(tiles):
                at = (s * tiles + q) * 8
                out[s, k, :, q * LANES : (q + 1) * LANES] = rows[at : at + 8]
    for k in range(5):
        edge_a[k] = out[plane_a, k]
        edge_b[k] = out[plane_b, k]
        for s in range(4):
            raw[k, s, :] = out[s, k, row, :]
    wall_rows(splat, raw, edge_w)


def final_residual_kernel(splat, fix, jac, base_in, late_in, rest, base, late, sems):
    loads = [pltpu.make_async_copy(base_in, base, sems.at[0]), pltpu.make_async_copy(late_in, late, sems.at[1])]
    for load in loads:
        load.start()

    def body(lanes):
        planes = [[fix[n, k, :, lanes] for k in range(5)] for n in range(4)]
        for s in range(4):
            applied = local_apply(splat, planes, jac, lanes, s)
            for k in range(5):
                rest[s, k, :, lanes] = -applied[k]

    for_lanes(body, fix.shape[-1])
    for load in loads:
        load.wait()


def final_local_kernel(fix, rest, halo_w, jinv, base, late, inner):
    row = position()[3]

    def body(lanes):
        for s in range(4):
            known = with_wall(rest, halo_w, s, lanes, row)
            if s in (0, 3):
                known = [known[k] + late[s // 3, k, :, lanes] for k in range(5)]
            swept = sweep(jinv, s, lanes, known)
            for k in range(5):
                inner[s, k, :, lanes] = (base[s, k, :, lanes] + fix[s, k, :, lanes]) + swept[k]

    for_lanes(body, fix.shape[-1])


def final_edge_kernel(splat, inner, halo_b, halo_a, jinv, out, edges, sems):
    _, plane_a, plane_b, _ = position()
    real = inside()
    stores = [pltpu.make_async_copy(inner.at[pl.ds(1, 2)], out.at[pl.ds(1, 2)], sems.at[2])]
    stores[0].start()
    for n, (plane, halo, there) in enumerate(((plane_b, halo_b, real), (plane_a, halo_a, None))):

        def body(lanes, n=n, plane=plane, halo=halo, there=there):
            swept = sweep(jinv, plane, lanes, beyond_span(splat, halo, lanes, there))
            for k in range(5):
                edges[n, k, :, lanes] = inner[plane, k, :, lanes] + swept[k]

        for_lanes(body, inner.shape[-1])
        stores.append(pltpu.make_async_copy(edges.at[n], out.at[plane], sems.at[n]))
        stores[-1].start()
    for store in stores:
        store.wait()


def exchange(edge_a, edge_b, edge_w):
    size = lax.axis_size("span")
    even = [p for i in range(0, size, 2) for p in ((i, i + 1), (i + 1, i))]
    odd = [((i + 1) % size, (j + 1) % size) for i, j in even]
    halo_b = lax.ppermute(edge_b, "span", odd)
    halo_w = lax.ppermute(edge_w, "wall", [(0, 1), (1, 0)])
    halo_a = lax.ppermute(edge_a, "span", even)
    return halo_a, halo_b, halo_w


def local(rhs, jac, jac_inv, wall_coupling, span_coupling, block_owner, block_slot, coarse_inv):
    rhs = in_hbm(rhs.transpose(0, 2, 1, 3))
    jac_in = jac.transpose(0, 2, 3, 1, 4)
    jinv_in = jac_inv.transpose(0, 2, 3, 1, 4)
    inv = coarse_inv[0, 0].transpose(0, 2, 1)
    field, plane, edge = shaped(*rhs.shape), shaped(*rhs.shape[1:]), shaped(20, rhs.shape[-1])
    field_out = pltpu.HBM(rhs.shape, F32)
    matrices = shaped(*jac_in.shape)
    outer = pltpu.VMEM((2, *rhs.shape[1:]), F32)
    raw = pltpu.VMEM(rhs.shape[1:], F32)
    owners, slots = lax.axis_size("patch"), coarse_inv.shape[-1]
    aggregates, columns = owners * slots, 5 * LANES
    chunks = shaped(owners, slots, columns)

    rhs_in = rhs
    a, b = call(
        first_edge_kernel,
        [plane, plane],
        [rhs_in, in_hbm(jinv_in)],
        places=[HBM] * 2,
        scratch=[outer, pltpu.VMEM((2, *jinv_in.shape[1:]), F32), pltpu.SemaphoreType.DMA((2, 2))],
    )
    rhs, jinv, first, splat, onehot_t, w = call(
        first_inner_kernel,
        [field, matrices, field, shaped(2, 5, 5, 8, LANES), shaped(aggregates, block_owner.size), edge],
        [*(in_hbm(x) for x in (wall_coupling, span_coupling, block_owner, block_slot, rhs_in, jinv_in)), b, a],
        places=[HBM] * 6 + [VMEM] * 2,
        scratch=[
            pltpu.SMEM(wall_coupling.shape, F32),
            pltpu.SMEM(span_coupling.shape, F32),
            pltpu.VMEM(block_owner.shape, jnp.int32),
            pltpu.VMEM(block_owner.shape, jnp.int32),
            raw,
            pltpu.SemaphoreType.DMA((5,)),
            pltpu.SemaphoreType.DMA((4,)),
        ],
    )
    halo_a, halo_b, halo_w = exchange(a, b, w)
    rest, jac = call(
        first_residual_kernel,
        [field, matrices],
        [splat, first, rhs, in_hbm(jac_in)],
        places=[VMEM] * 3 + [HBM],
        scratch=[pltpu.SemaphoreType.DMA((4,))],
    )
    [inner] = call(second_local_kernel, [field], [first, rest, halo_w, jinv])
    a, b, w = call(
        second_edge_kernel, [plane, plane, edge], [splat, inner, halo_b, halo_a, jinv], scratch=[raw]
    )
    halo_a, halo_b, halo_w = exchange(a, b, w)
    [rest] = call(second_residual_kernel, [field], [splat, inner, b, a, rhs, jac])
    partial, base = call(
        defect_local_kernel,
        [shaped(aggregates, columns), field_out],
        [inner, b, a, rest, halo_w, jinv, onehot_t],
        out_places=[VMEM, HBM],
        scratch=[pltpu.VMEM(rhs.shape, F32), pltpu.VMEM(rhs.shape, F32), pltpu.SemaphoreType.DMA((1,))],
    )
    partial, late = call(
        restrict_kernel,
        [chunks, pltpu.HBM((2, *plane.shape), F32)],
        [splat, partial, halo_b, halo_a, onehot_t],
        out_places=[VMEM, HBM],
        scratch=[outer, pltpu.SemaphoreType.DMA((2,))],
    )
    received = lax.all_to_all(partial, "patch", split_axis=0, concat_axis=0, tiled=True)
    [mine] = call(sum_kernel, [shaped(slots, columns)], [received])
    theirs = lax.ppermute(mine, "wall", [(0, 1), (1, 0)])
    [reply] = call(coarse_kernel, [chunks], [inv, mine, theirs])
    fixes = lax.all_to_all(reply, "patch", split_axis=0, concat_axis=0, tiled=True)
    fix, a, b, w = call(
        prolong_kernel,
        [field, plane, plane, edge],
        [splat, block_owner, block_slot, fixes],
        scratch=[pltpu.VMEM((aggregates, columns), F32), raw],
    )
    halo_a, halo_b, halo_w = exchange(a, b, w)
    rest, base, late = call(
        final_residual_kernel,
        [field, field, shaped(2, *plane.shape)],
        [splat, fix, jac_in, in_hbm(base), in_hbm(late)],
        places=[VMEM] * 3 + [HBM] * 2,
        scratch=[pltpu.SemaphoreType.DMA((2,))],
    )
    [inner] = call(final_local_kernel, [field], [fix, rest, halo_w, jinv_in, base, late])
    [out] = call(
        final_edge_kernel,
        [field_out],
        [splat, inner, halo_b, halo_a, jinv_in],
        out_places=[HBM],
        scratch=[outer, pltpu.SemaphoreType.DMA((3,))],
    )
    return out.transpose(0, 2, 1, 3)


def solution(mesh):
    return jax.shard_map(
        local,
        mesh=mesh,
        in_specs=(
            P("span", "wall", None, "patch"),
            P("span", "wall", None, None, "patch"),
            P("span", "wall", None, None, "patch"),
            P(),
            P(),
            P("span", "wall", "patch"),
            P("span", "wall", "patch"),
            P("span", "wall", None, None, "patch"),
        ),
        out_specs=P("span", "wall", None, "patch"),
        check_vma=False,
    )
```

```python
import functools
import math

import jax
import jax.numpy as jnp
from jax import lax
from jax.experimental import pallas as pl
from jax.experimental.pallas import tpu as pltpu
from jax.sharding import PartitionSpec as P

LANES = 128
VMEM = pl.BlockSpec(memory_space=pltpu.VMEM)
SMEM = pl.BlockSpec(memory_space=pltpu.SMEM)
HBM = pl.BlockSpec(memory_space=pltpu.HBM)
F32 = jnp.float32


def shaped(*shape):
    return jax.ShapeDtypeStruct(shape, F32)


def in_hbm(array):
    return pltpu.with_memory_space_constraint(array, pltpu.HBM)


def call(kernel, outs, args, places=None, out_places=None, scratch=()):
    size = 2 * sum(math.prod(a.shape) for a in (*args, *outs))
    return pl.pallas_call(
        kernel,
        out_shape=outs,
        in_specs=places or [VMEM] * len(args),
        out_specs=out_places or [VMEM] * len(outs),
        scratch_shapes=scratch,
        cost_estimate=pl.CostEstimate(flops=size, bytes_accessed=size, transcendentals=0),
        compiler_params=pltpu.CompilerParams(vmem_limit_bytes=8 * 2**20),
    )(*args)


def total(terms):
    return functools.reduce(lambda a, b: a + b, terms)


def position():
    span_at, wall_at = lax.axis_index("span"), lax.axis_index("wall")
    odd = lax.rem(span_at, 2)
    plane_a = 3 - 3 * odd
    return odd == 0, plane_a, 3 - plane_a, 7 - 7 * wall_at


def inside():
    at, size = lax.axis_index("span"), lax.axis_size("span")
    return jnp.logical_and(at > 0, at < size - 1)


def mix(splat, which, values):
    return [total([splat[which, k, i] * values[k] for k in range(5)]) for i in range(5)]


def sweep(jinv, s, lanes, values):
    return [total([jinv[s, i, k, :, lanes] * values[k] for k in range(5)]) for i in range(5)]


def beyond_span(splat, halo, lanes, real=None):
    values = [halo[k, :, lanes] for k in range(5)]
    if real is not None:
        values = [jnp.where(real, v, 0.0) for v in values]
    return mix(splat, 1, values)


def wall_rows(splat, raw, out):
    for q in range(out.shape[-1] // LANES):
        lanes = slice(q * LANES, (q + 1) * LANES)
        mixed = mix(splat, 0, [raw[k, :, lanes] for k in range(5)])
        for i in range(5):
            out[4 * i : 4 * i + 4, lanes] = mixed[i][:4]


def for_lanes(body, length):
    @pl.loop(0, length // LANES)
    def _(q):
        body(pl.ds(pl.multiple_of(q * LANES, LANES), LANES))


def picked_sums(hot, rows):
    hot = hot.astype(jnp.bfloat16)
    high = rows.astype(jnp.bfloat16)
    rest = rows - high.astype(F32)
    middle = rest.astype(jnp.bfloat16)
    low = (rest - middle.astype(F32)).astype(jnp.bfloat16)
    return total([jnp.dot(hot, part, preferred_element_type=F32) for part in (low, middle, high)])


def hot_rows(owner, slot, tiles):
    ids = lax.broadcasted_iota(jnp.int32, (8, LANES), 1)
    hot = []
    for s in range(4):
        named = owner[s] * 4 + slot[s]
        hot += [jnp.where(named[:, q : q + 1] == ids, 1.0, 0.0) for q in range(tiles)]
    return jnp.concatenate(hot, axis=0)


def first_edge_kernel(rhs_in, jinv_in, edge_a, edge_b, rhs, jinv, sems):
    _, plane_a, plane_b, _ = position()
    outer = ((plane_b, edge_b), (plane_a, edge_a))
    copies = [
        pltpu.make_async_copy(source.at[plane], here.at[m], sems.at[n, m])
        for m, (plane, _) in enumerate(outer)
        for n, (source, here) in enumerate(((rhs_in, rhs), (jinv_in, jinv)))
    ]
    for copy in copies:
        copy.start()
    for m, (_, edge) in enumerate(outer):
        copies[2 * m].wait()
        copies[2 * m + 1].wait()

        def body(lanes, m=m, edge=edge):
            swept = sweep(jinv, m, lanes, [rhs[m, k, :, lanes] for k in range(5)])
            for k in range(5):
                edge[k, :, lanes] = swept[k]

        for_lanes(body, rhs.shape[-1])


def first_inner_kernel(
    wall_in, span_in, owner_in, slot_in, rhs_in, jinv_in, edge_b, edge_a,
    rhs, first, splat, onehot_t, edge_w,
    wall, span, owner, slot, raw, jinv, small_sems, sems,
):
    small = [
        pltpu.make_async_copy(source, here, small_sems.at[n])
        for n, (source, here) in enumerate(((wall_in, wall), (span_in, span), (owner_in, owner), (slot_in, slot)))
    ]
    small.append(pltpu.make_async_copy(rhs_in, rhs, small_sems.at[4]))
    slabs = [pltpu.make_async_copy(jinv_in.at[1 + m], jinv.at[m], sems.at[m]) for m in range(2)]
    for copy in small + slabs:
        copy.start()
    even, _, _, row = position()
    for k in range(5):
        first[0, k] = jnp.where(even, edge_b[k], edge_a[k])
        first[3, k] = jnp.where(even, edge_a[k], edge_b[k])
    small[0].wait()
    small[1].wait()
    for which, coupling in enumerate((wall, span)):
        for k in range(5):
            for i in range(5):
                splat[which, k, i] = jnp.full((8, LANES), coupling[k, i], F32)
    small[2].wait()
    small[3].wait()
    onehot_t[...] = hot_rows(owner, slot, rhs.shape[-1] // LANES).T[: onehot_t.shape[0]]
    small[4].wait()
    for s in (1, 2):
        slabs[s - 1].wait()

        def body(lanes, s=s):
            swept = sweep(jinv, s - 1, lanes, [rhs[s, k, :, lanes] for k in range(5)])
            for k in range(5):
                first[s, k, :, lanes] = swept[k]

        for_lanes(body, rhs.shape[-1])
    for s in range(4):
        for k in range(5):
            raw[k, s, :] = first[s, k, row, :]
    wall_rows(splat, raw, edge_w)


def local_apply(splat, planes, jac, lanes, s):
    own = planes[s]
    rows = lax.broadcasted_iota(jnp.int32, own[0].shape, 0)
    near_wall, near_span = [], []
    for k in range(5):
        up = jnp.where(rows == 7, 0.0, pltpu.roll(own[k], 7, 0))
        down = jnp.where(rows == 0, 0.0, pltpu.roll(own[k], 1, 0))
        near_wall.append(up + down)
        near_span.append(total([planes[n][k] for n in (s - 1, s + 1) if 0 <= n < 4]))
    from_wall, from_span = mix(splat, 0, near_wall), mix(splat, 1, near_span)
    return [
        total([jac[s, k, i, :, lanes] * own[k] for k in range(5)]) - (from_wall[i] + from_span[i])
        for i in range(5)
    ]


def with_wall(rest, halo_w, s, lanes, row):
    rows = lax.broadcasted_iota(jnp.int32, (8, LANES), 0)
    return [
        rest[s, i, :, lanes] + jnp.where(rows == row, halo_w[4 * i + s, lanes][None, :], 0.0) for i in range(5)
    ]


def first_residual_kernel(splat, first, rhs, jac, rest):
    def body(lanes):
        planes = [[first[n, k, :, lanes] for k in range(5)] for n in range(4)]
        for s in range(4):
            applied = local_apply(splat, planes, jac, lanes, s)
            for k in range(5):
                rest[s, k, :, lanes] = rhs[s, k, :, lanes] - applied[k]

    for_lanes(body, rhs.shape[-1])


def second_local_kernel(first, rest, halo_w, jinv, inner):
    row = position()[3]

    def body(lanes):
        for s in range(4):
            swept = sweep(jinv, s, lanes, with_wall(rest, halo_w, s, lanes, row))
            for k in range(5):
                inner[s, k, :, lanes] = first[s, k, :, lanes] + swept[k]

    for_lanes(body, rest.shape[-1])


def second_edge_kernel(splat, inner, halo_b, halo_a, jinv, edge_a, edge_b, edge_w, raw):
    even, plane_a, plane_b, row = position()
    real = inside()

    def body(lanes):
        for plane, halo, edge, there in ((plane_a, halo_a, edge_a, None), (plane_b, halo_b, edge_b, real)):
            swept = sweep(jinv, plane, lanes, beyond_span(splat, halo, lanes, there))
            for k in range(5):
                edge[k, :, lanes] = inner[plane, k, :, lanes] + swept[k]

    for_lanes(body, inner.shape[-1])
    for k in range(5):
        for s in (1, 2):
            raw[k, s, :] = inner[s, k, row, :]
        a, b = edge_a[k, row, :], edge_b[k, row, :]
        raw[k, 0, :] = jnp.where(even, b, a)
        raw[k, 3, :] = jnp.where(even, a, b)
    wall_rows(splat, raw, edge_w)


def planes_of(even, inner, edge_a, edge_b, lanes):
    a = [edge_a[k, :, lanes] for k in range(5)]
    b = [edge_b[k, :, lanes] for k in range(5)]
    return [
        [jnp.where(even, b[k], a[k]) for k in range(5)],
        [inner[1, k, :, lanes] for k in range(5)],
        [inner[2, k, :, lanes] for k in range(5)],
        [jnp.where(even, a[k], b[k]) for k in range(5)],
    ]


def second_residual_kernel(splat, inner, edge_b, edge_a, rhs, jac, rest):
    even = position()[0]

    def body(lanes):
        planes = planes_of(even, inner, edge_a, edge_b, lanes)
        for s in range(4):
            applied = local_apply(splat, planes, jac, lanes, s)
            for k in range(5):
                rest[s, k, :, lanes] = rhs[s, k, :, lanes] - applied[k]

    for_lanes(body, rhs.shape[-1])


def defect_local_kernel(inner, edge_b, edge_a, rest, halo_w, jinv, onehot_t, partial, base_out, base, defect, sems):
    even, _, _, row = position()

    def body(lanes):
        planes = planes_of(even, inner, edge_a, edge_b, lanes)
        for s in range(4):
            known = with_wall(rest, halo_w, s, lanes, row)
            swept = sweep(jinv, s, lanes, known)
            for k in range(5):
                base[s, k, :, lanes] = planes[s][k] + swept[k]
                defect[s, k, :, lanes] = known[k]

    for_lanes(body, rest.shape[-1])
    store = pltpu.make_async_copy(base, base_out, sems.at[0])
    store.start()
    tiles = defect.shape[-1] // LANES
    for k in range(5):
        rows = jnp.concatenate(
            [defect[s, k, :, q * LANES : (q + 1) * LANES] for s in range(4) for q in range(tiles)], axis=0
        )
        partial[:, k * LANES : (k + 1) * LANES] = picked_sums(onehot_t[...], rows)
    store.wait()


def restrict_kernel(splat, inner, halo_b, halo_a, onehot_t, partial, late_out, late, sems):
    real = inside()
    at_a = 1 - lax.rem(lax.axis_index("span"), 2)
    tiles = halo_a.shape[-1] // LANES
    stores, parts = [], []
    for n, (halo, there, at) in enumerate(((halo_b, real, 1 - at_a), (halo_a, None, at_a))):
        for q in range(tiles):
            lanes = slice(q * LANES, (q + 1) * LANES)
            beyond = beyond_span(splat, halo, lanes, there)
            parts.append(beyond)
            for k in range(5):
                late[n, k, :, lanes] = beyond[k]
        stores.append(pltpu.make_async_copy(late.at[n], late_out.at[at], sems.at[n]))
        stores[-1].start()
    width = 8 * tiles
    even = at_a == 1
    low, high = onehot_t[:, :width], onehot_t[:, 3 * width :]
    hot = jnp.concatenate([jnp.where(even, low, high), jnp.where(even, high, low)], axis=1)
    slots = partial.shape[1]
    rows = jnp.concatenate([jnp.concatenate(part, axis=1) for part in parts], axis=0)
    sums = inner[...] + picked_sums(hot, rows)
    for p in range(partial.shape[0]):
        partial[p] = sums[p * slots : (p + 1) * slots]
    for store in stores:
        store.wait()


def sum_kernel(received, sums):
    sums[...] = total([received[p] for p in range(received.shape[0])])


def coarse_kernel(inv, own, other, out):
    first_group = lax.axis_index("wall") == 0
    groups = [
        [jnp.where(first_group, x[:, k * LANES : (k + 1) * LANES], y[:, k * LANES : (k + 1) * LANES]) for k in range(5)]
        for x, y in ((own, other), (other, own))
    ]
    for i in range(5):
        rows = inv[i]
        fix = total([rows[:, c * 5 + k : c * 5 + k + 1] * groups[c][k] for c in range(2) for k in range(5)])
        for p in range(out.shape[0]):
            out[p, :, i * LANES : (i + 1) * LANES] = fix


def prolong_kernel(splat, owner, slot, fixes, out, edge_a, edge_b, edge_w, fix, raw):
    _, plane_a, plane_b, row = position()
    tiles = out.shape[-1] // LANES
    owners, slots, _ = fixes.shape
    for p in range(owners):
        fix[p * slots : (p + 1) * slots, :] = fixes[p]
    hot = hot_rows(owner, slot, tiles)[:, : owners * slots]
    for k in range(5):
        rows = picked_sums(hot, fix[:, k * LANES : (k + 1) * LANES])
        for s in range(4):
            for q in range(tiles):
                at = (s * tiles + q) * 8
                out[s, k, :, q * LANES : (q + 1) * LANES] = rows[at : at + 8]
    for k in range(5):
        edge_a[k] = out[plane_a, k]
        edge_b[k] = out[plane_b, k]
        for s in range(4):
            raw[k, s, :] = out[s, k, row, :]
    wall_rows(splat, raw, edge_w)


def final_residual_kernel(splat, fix, jac, base_in, late_in, rest, base, late, sems):
    loads = [pltpu.make_async_copy(base_in, base, sems.at[0]), pltpu.make_async_copy(late_in, late, sems.at[1])]
    for load in loads:
        load.start()

    def body(lanes):
        planes = [[fix[n, k, :, lanes] for k in range(5)] for n in range(4)]
        for s in range(4):
            applied = local_apply(splat, planes, jac, lanes, s)
            for k in range(5):
                rest[s, k, :, lanes] = -applied[k]

    for_lanes(body, fix.shape[-1])
    for load in loads:
        load.wait()


def final_local_kernel(fix, rest, halo_w, jinv, base, late, inner):
    row = position()[3]

    def body(lanes):
        for s in range(4):
            known = with_wall(rest, halo_w, s, lanes, row)
            if s in (0, 3):
                known = [known[k] + late[s // 3, k, :, lanes] for k in range(5)]
            swept = sweep(jinv, s, lanes, known)
            for k in range(5):
                inner[s, k, :, lanes] = (base[s, k, :, lanes] + fix[s, k, :, lanes]) + swept[k]

    for_lanes(body, fix.shape[-1])


def final_edge_kernel(splat, inner, halo_b, halo_a, jinv, out, edges, sems):
    _, plane_a, plane_b, _ = position()
    real = inside()
    stores = [pltpu.make_async_copy(inner.at[pl.ds(1, 2)], out.at[pl.ds(1, 2)], sems.at[2])]
    stores[0].start()
    for n, (plane, halo, there) in enumerate(((plane_b, halo_b, real), (plane_a, halo_a, None))):

        def body(lanes, n=n, plane=plane, halo=halo, there=there):
            swept = sweep(jinv, plane, lanes, beyond_span(splat, halo, lanes, there))
            for k in range(5):
                edges[n, k, :, lanes] = inner[plane, k, :, lanes] + swept[k]

        for_lanes(body, inner.shape[-1])
        stores.append(pltpu.make_async_copy(edges.at[n], out.at[plane], sems.at[n]))
        stores[-1].start()
    for store in stores:
        store.wait()


def exchange(edge_a, edge_b, edge_w):
    size = lax.axis_size("span")
    even = [p for i in range(0, size, 2) for p in ((i, i + 1), (i + 1, i))]
    odd = [((i + 1) % size, (j + 1) % size) for i, j in even]
    halo_b = lax.ppermute(edge_b, "span", odd)
    halo_w = lax.ppermute(edge_w, "wall", [(0, 1), (1, 0)])
    halo_a = lax.ppermute(edge_a, "span", even)
    return halo_a, halo_b, halo_w


def local(rhs, jac, jac_inv, wall_coupling, span_coupling, block_owner, block_slot, coarse_inv):
    rhs = in_hbm(rhs.transpose(0, 2, 1, 3))
    jac_in = jac.transpose(0, 2, 3, 1, 4)
    jinv_in = jac_inv.transpose(0, 2, 3, 1, 4)
    inv = coarse_inv[0, 0].transpose(0, 2, 1)
    field, plane, edge = shaped(*rhs.shape), shaped(*rhs.shape[1:]), shaped(20, rhs.shape[-1])
    field_out = pltpu.HBM(rhs.shape, F32)
    outer = pltpu.VMEM((2, *rhs.shape[1:]), F32)
    raw = pltpu.VMEM(rhs.shape[1:], F32)
    owners, slots = lax.axis_size("patch"), coarse_inv.shape[-1]
    aggregates, columns = owners * slots, 5 * LANES
    chunks = shaped(owners, slots, columns)

    rhs_in = rhs
    a, b = call(
        first_edge_kernel,
        [plane, plane],
        [rhs_in, in_hbm(jinv_in)],
        places=[HBM] * 2,
        scratch=[outer, pltpu.VMEM((2, *jinv_in.shape[1:]), F32), pltpu.SemaphoreType.DMA((2, 2))],
    )
    rhs, first, splat, onehot_t, w = call(
        first_inner_kernel,
        [field, field, shaped(2, 5, 5, 8, LANES), shaped(aggregates, block_owner.size), edge],
        [*(in_hbm(x) for x in (wall_coupling, span_coupling, block_owner, block_slot, rhs_in, jinv_in)), b, a],
        places=[HBM] * 6 + [VMEM] * 2,
        scratch=[
            pltpu.SMEM(wall_coupling.shape, F32),
            pltpu.SMEM(span_coupling.shape, F32),
            pltpu.VMEM(block_owner.shape, jnp.int32),
            pltpu.VMEM(block_owner.shape, jnp.int32),
            raw,
            pltpu.VMEM((2, *jinv_in.shape[1:]), F32),
            pltpu.SemaphoreType.DMA((5,)),
            pltpu.SemaphoreType.DMA((2,)),
        ],
    )
    halo_a, halo_b, halo_w = exchange(a, b, w)
    [rest] = call(first_residual_kernel, [field], [splat, first, rhs, jac_in])
    [inner] = call(second_local_kernel, [field], [first, rest, halo_w, jinv_in])
    a, b, w = call(
        second_edge_kernel, [plane, plane, edge], [splat, inner, halo_b, halo_a, jinv_in], scratch=[raw]
    )
    halo_a, halo_b, halo_w = exchange(a, b, w)
    [rest] = call(second_residual_kernel, [field], [splat, inner, b, a, rhs, jac_in])
    partial, base = call(
        defect_local_kernel,
        [shaped(aggregates, columns), field_out],
        [inner, b, a, rest, halo_w, jinv_in, onehot_t],
        out_places=[VMEM, HBM],
        scratch=[pltpu.VMEM(rhs.shape, F32), pltpu.VMEM(rhs.shape, F32), pltpu.SemaphoreType.DMA((1,))],
    )
    partial, late = call(
        restrict_kernel,
        [chunks, pltpu.HBM((2, *plane.shape), F32)],
        [splat, partial, halo_b, halo_a, onehot_t],
        out_places=[VMEM, HBM],
        scratch=[outer, pltpu.SemaphoreType.DMA((2,))],
    )
    received = lax.all_to_all(partial, "patch", split_axis=0, concat_axis=0, tiled=True)
    [mine] = call(sum_kernel, [shaped(slots, columns)], [received])
    theirs = lax.ppermute(mine, "wall", [(0, 1), (1, 0)])
    [reply] = call(coarse_kernel, [chunks], [inv, mine, theirs])
    fixes = lax.all_to_all(reply, "patch", split_axis=0, concat_axis=0, tiled=True)
    fix, a, b, w = call(
        prolong_kernel,
        [field, plane, plane, edge],
        [splat, block_owner, block_slot, fixes],
        scratch=[pltpu.VMEM((aggregates, columns), F32), raw],
    )
    halo_a, halo_b, halo_w = exchange(a, b, w)
    rest, base, late = call(
        final_residual_kernel,
        [field, field, shaped(2, *plane.shape)],
        [splat, fix, jac_in, in_hbm(base), in_hbm(late)],
        places=[VMEM] * 3 + [HBM] * 2,
        scratch=[pltpu.SemaphoreType.DMA((2,))],
    )
    [inner] = call(final_local_kernel, [field], [fix, rest, halo_w, jinv_in, base, late])
    [out] = call(
        final_edge_kernel,
        [field_out],
        [splat, inner, halo_b, halo_a, jinv_in],
        out_places=[HBM],
        scratch=[outer, pltpu.SemaphoreType.DMA((3,))],
    )
    return out.transpose(0, 2, 1, 3)


def solution(mesh):
    return jax.shard_map(
        local,
        mesh=mesh,
        in_specs=(
            P("span", "wall", None, "patch"),
            P("span", "wall", None, None, "patch"),
            P("span", "wall", None, None, "patch"),
            P(),
            P(),
            P("span", "wall", "patch"),
            P("span", "wall", "patch"),
            P("span", "wall", None, None, "patch"),
        ),
        out_specs=P("span", "wall", None, "patch"),
        check_vma=False,
    )
```

```python
import functools
import math

import jax
import jax.numpy as jnp
from jax import lax
from jax.experimental import pallas as pl
from jax.experimental.pallas import tpu as pltpu
from jax.sharding import PartitionSpec as P

LANES = 128
VMEM = pl.BlockSpec(memory_space=pltpu.VMEM)
SMEM = pl.BlockSpec(memory_space=pltpu.SMEM)
HBM = pl.BlockSpec(memory_space=pltpu.HBM)
F32 = jnp.float32


def shaped(*shape):
    return jax.ShapeDtypeStruct(shape, F32)


def in_hbm(array):
    return pltpu.with_memory_space_constraint(array, pltpu.HBM)


def call(kernel, outs, args, places=None, out_places=None, scratch=()):
    size = 2 * sum(math.prod(a.shape) for a in (*args, *outs))
    return pl.pallas_call(
        kernel,
        out_shape=outs,
        in_specs=places or [VMEM] * len(args),
        out_specs=out_places or [VMEM] * len(outs),
        scratch_shapes=scratch,
        cost_estimate=pl.CostEstimate(flops=size, bytes_accessed=size, transcendentals=0),
        compiler_params=pltpu.CompilerParams(vmem_limit_bytes=8 * 2**20),
    )(*args)


def total(terms):
    return functools.reduce(lambda a, b: a + b, terms)


def position():
    span_at, wall_at = lax.axis_index("span"), lax.axis_index("wall")
    odd = lax.rem(span_at, 2)
    plane_a = 3 - 3 * odd
    return odd == 0, plane_a, 3 - plane_a, 7 - 7 * wall_at


def inside():
    at, size = lax.axis_index("span"), lax.axis_size("span")
    return jnp.logical_and(at > 0, at < size - 1)


def mix(splat, which, values):
    return [total([splat[which, k, i] * values[k] for k in range(5)]) for i in range(5)]


def sweep(jinv, s, lanes, values):
    return [total([jinv[s, i, k, :, lanes] * values[k] for k in range(5)]) for i in range(5)]


def beyond_span(splat, halo, lanes, real=None):
    values = [halo[k, :, lanes] for k in range(5)]
    if real is not None:
        values = [jnp.where(real, v, 0.0) for v in values]
    return mix(splat, 1, values)


def wall_rows(splat, raw, out):
    for q in range(out.shape[-1] // LANES):
        lanes = slice(q * LANES, (q + 1) * LANES)
        mixed = mix(splat, 0, [raw[k, :, lanes] for k in range(5)])
        for i in range(5):
            out[4 * i : 4 * i + 4, lanes] = mixed[i][:4]


def for_lanes(body, length):
    @pl.loop(0, length // LANES)
    def _(q):
        body(pl.ds(pl.multiple_of(q * LANES, LANES), LANES))


def picked_sums(hot, rows):
    hot = hot.astype(jnp.bfloat16)
    high = rows.astype(jnp.bfloat16)
    rest = rows - high.astype(F32)
    middle = rest.astype(jnp.bfloat16)
    low = (rest - middle.astype(F32)).astype(jnp.bfloat16)
    return total([jnp.dot(hot, part, preferred_element_type=F32) for part in (low, middle, high)])


def hot_rows(owner, slot, tiles):
    ids = lax.broadcasted_iota(jnp.int32, (8, LANES), 1)
    hot = []
    for s in range(4):
        named = owner[s] * 4 + slot[s]
        hot += [jnp.where(named[:, q : q + 1] == ids, 1.0, 0.0) for q in range(tiles)]
    return jnp.concatenate(hot, axis=0)


def first_edge_kernel(
    wall_in, span_in, owner_in, slot_in, rhs_in, jinv_in,
    edge_b, edge_a, splat, onehot_t,
    wall, span, owner, slot, rhs, jinv, small_sems, sems,
):
    _, plane_a, plane_b, _ = position()
    outer = ((plane_b, edge_b), (plane_a, edge_a))
    small = [
        pltpu.make_async_copy(source, here, small_sems.at[n])
        for n, (source, here) in enumerate(((wall_in, wall), (span_in, span), (owner_in, owner), (slot_in, slot)))
    ]
    copies = [
        pltpu.make_async_copy(source.at[plane], here.at[m], sems.at[n, m])
        for m, (plane, _) in enumerate(outer)
        for n, (source, here) in enumerate(((rhs_in, rhs), (jinv_in, jinv)))
    ]
    for copy in small + copies:
        copy.start()
    small[0].wait()
    small[1].wait()
    for which, coupling in enumerate((wall, span)):
        for k in range(5):
            for i in range(5):
                splat[which, k, i] = jnp.full((8, LANES), coupling[k, i], F32)
    small[2].wait()
    small[3].wait()
    onehot_t[...] = hot_rows(owner, slot, rhs.shape[-1] // LANES).T[: onehot_t.shape[0]]
    for m, (_, edge) in enumerate(outer):
        copies[2 * m].wait()
        copies[2 * m + 1].wait()

        def body(lanes, m=m, edge=edge):
            swept = sweep(jinv, m, lanes, [rhs[m, k, :, lanes] for k in range(5)])
            for k in range(5):
                edge[k, :, lanes] = swept[k]

        for_lanes(body, rhs.shape[-1])


def first_inner_kernel(splat, edge_b, edge_a, rhs_in, jinv_in, rhs, first, edge_w, raw, jinv, sems):
    whole = pltpu.make_async_copy(rhs_in, rhs, sems.at[2])
    slabs = [pltpu.make_async_copy(jinv_in.at[1 + m], jinv.at[m], sems.at[m]) for m in range(2)]
    for copy in (whole, *slabs):
        copy.start()
    even, _, _, row = position()
    for k in range(5):
        first[0, k] = jnp.where(even, edge_b[k], edge_a[k])
        first[3, k] = jnp.where(even, edge_a[k], edge_b[k])
    whole.wait()
    for s in (1, 2):
        slabs[s - 1].wait()

        def body(lanes, s=s):
            swept = sweep(jinv, s - 1, lanes, [rhs[s, k, :, lanes] for k in range(5)])
            for k in range(5):
                first[s, k, :, lanes] = swept[k]

        for_lanes(body, rhs.shape[-1])
    for s in range(4):
        for k in range(5):
            raw[k, s, :] = first[s, k, row, :]
    wall_rows(splat, raw, edge_w)


def local_apply(splat, planes, jac, lanes, s):
    own = planes[s]
    rows = lax.broadcasted_iota(jnp.int32, own[0].shape, 0)
    near_wall, near_span = [], []
    for k in range(5):
        up = jnp.where(rows == 7, 0.0, pltpu.roll(own[k], 7, 0))
        down = jnp.where(rows == 0, 0.0, pltpu.roll(own[k], 1, 0))
        near_wall.append(up + down)
        near_span.append(total([planes[n][k] for n in (s - 1, s + 1) if 0 <= n < 4]))
    from_wall, from_span = mix(splat, 0, near_wall), mix(splat, 1, near_span)
    return [
        total([jac[s, k, i, :, lanes] * own[k] for k in range(5)]) - (from_wall[i] + from_span[i])
        for i in range(5)
    ]


def with_wall(rest, halo_w, s, lanes, row):
    rows = lax.broadcasted_iota(jnp.int32, (8, LANES), 0)
    return [
        rest[s, i, :, lanes] + jnp.where(rows == row, halo_w[4 * i + s, lanes][None, :], 0.0) for i in range(5)
    ]


def first_residual_kernel(splat, first, rhs, jac, rest):
    def body(lanes):
        planes = [[first[n, k, :, lanes] for k in range(5)] for n in range(4)]
        for s in range(4):
            applied = local_apply(splat, planes, jac, lanes, s)
            for k in range(5):
                rest[s, k, :, lanes] = rhs[s, k, :, lanes] - applied[k]

    for_lanes(body, rhs.shape[-1])


def second_local_kernel(first, rest, halo_w, jinv, inner):
    row = position()[3]

    def body(lanes):
        for s in range(4):
            swept = sweep(jinv, s, lanes, with_wall(rest, halo_w, s, lanes, row))
            for k in range(5):
                inner[s, k, :, lanes] = first[s, k, :, lanes] + swept[k]

    for_lanes(body, rest.shape[-1])


def second_edge_kernel(splat, inner, halo_b, halo_a, jinv, edge_a, edge_b, edge_w, raw):
    even, plane_a, plane_b, row = position()
    real = inside()

    def body(lanes):
        for plane, halo, edge, there in ((plane_a, halo_a, edge_a, None), (plane_b, halo_b, edge_b, real)):
            swept = sweep(jinv, plane, lanes, beyond_span(splat, halo, lanes, there))
            for k in range(5):
                edge[k, :, lanes] = inner[plane, k, :, lanes] + swept[k]

    for_lanes(body, inner.shape[-1])
    for k in range(5):
        for s in (1, 2):
            raw[k, s, :] = inner[s, k, row, :]
        a, b = edge_a[k, row, :], edge_b[k, row, :]
        raw[k, 0, :] = jnp.where(even, b, a)
        raw[k, 3, :] = jnp.where(even, a, b)
    wall_rows(splat, raw, edge_w)


def planes_of(even, inner, edge_a, edge_b, lanes):
    a = [edge_a[k, :, lanes] for k in range(5)]
    b = [edge_b[k, :, lanes] for k in range(5)]
    return [
        [jnp.where(even, b[k], a[k]) for k in range(5)],
        [inner[1, k, :, lanes] for k in range(5)],
        [inner[2, k, :, lanes] for k in range(5)],
        [jnp.where(even, a[k], b[k]) for k in range(5)],
    ]


def second_residual_kernel(splat, inner, edge_b, edge_a, rhs, jac, rest):
    even = position()[0]

    def body(lanes):
        planes = planes_of(even, inner, edge_a, edge_b, lanes)
        for s in range(4):
            applied = local_apply(splat, planes, jac, lanes, s)
            for k in range(5):
                rest[s, k, :, lanes] = rhs[s, k, :, lanes] - applied[k]

    for_lanes(body, rhs.shape[-1])


def defect_local_kernel(inner, edge_b, edge_a, rest, halo_w, jinv, onehot_t, partial, base_out, base, defect, sems):
    even, _, _, row = position()

    def body(lanes):
        planes = planes_of(even, inner, edge_a, edge_b, lanes)
        for s in range(4):
            known = with_wall(rest, halo_w, s, lanes, row)
            swept = sweep(jinv, s, lanes, known)
            for k in range(5):
                base[s, k, :, lanes] = planes[s][k] + swept[k]
                defect[s, k, :, lanes] = known[k]

    for_lanes(body, rest.shape[-1])
    store = pltpu.make_async_copy(base, base_out, sems.at[0])
    store.start()
    tiles = defect.shape[-1] // LANES
    for k in range(5):
        rows = jnp.concatenate(
            [defect[s, k, :, q * LANES : (q + 1) * LANES] for s in range(4) for q in range(tiles)], axis=0
        )
        partial[:, k * LANES : (k + 1) * LANES] = picked_sums(onehot_t[...], rows)
    store.wait()


def restrict_kernel(splat, inner, halo_b, halo_a, onehot_t, partial, late_out, sems):
    real = inside()
    at_a = 1 - lax.rem(lax.axis_index("span"), 2)
    stores = [
        pltpu.make_async_copy(halo_b, late_out.at[1 - at_a], sems.at[0]),
        pltpu.make_async_copy(halo_a, late_out.at[at_a], sems.at[1]),
    ]
    for store in stores:
        store.start()
    tiles = halo_a.shape[-1] // LANES
    parts = []
    for halo, there in ((halo_b, real), (halo_a, None)):
        for q in range(tiles):
            parts.append(beyond_span(splat, halo, slice(q * LANES, (q + 1) * LANES), there))
    width = 8 * tiles
    even = at_a == 1
    low, high = onehot_t[:, :width], onehot_t[:, 3 * width :]
    hot = jnp.concatenate([jnp.where(even, low, high), jnp.where(even, high, low)], axis=1)
    slots = partial.shape[1]
    rows = jnp.concatenate([jnp.concatenate(part, axis=1) for part in parts], axis=0)
    sums = inner[...] + picked_sums(hot, rows)
    for p in range(partial.shape[0]):
        partial[p] = sums[p * slots : (p + 1) * slots]
    for store in stores:
        store.wait()


def sum_kernel(received, sums):
    sums[...] = total([received[p] for p in range(received.shape[0])])


def coarse_kernel(inv, own, other, out):
    first_group = lax.axis_index("wall") == 0
    groups = [
        [jnp.where(first_group, x[:, k * LANES : (k + 1) * LANES], y[:, k * LANES : (k + 1) * LANES]) for k in range(5)]
        for x, y in ((own, other), (other, own))
    ]
    for i in range(5):
        rows = inv[i]
        fix = total([rows[:, c * 5 + k : c * 5 + k + 1] * groups[c][k] for c in range(2) for k in range(5)])
        for p in range(out.shape[0]):
            out[p, :, i * LANES : (i + 1) * LANES] = fix


def prolong_kernel(splat, owner, slot, fixes, out, edge_a, edge_b, edge_w, fix, raw):
    _, plane_a, plane_b, row = position()
    tiles = out.shape[-1] // LANES
    owners, slots, _ = fixes.shape
    for p in range(owners):
        fix[p * slots : (p + 1) * slots, :] = fixes[p]
    hot = hot_rows(owner, slot, tiles)[:, : owners * slots]
    for k in range(5):
        rows = picked_sums(hot, fix[:, k * LANES : (k + 1) * LANES])
        for s in range(4):
            for q in range(tiles):
                at = (s * tiles + q) * 8
                out[s, k, :, q * LANES : (q + 1) * LANES] = rows[at : at + 8]
    for k in range(5):
        edge_a[k] = out[plane_a, k]
        edge_b[k] = out[plane_b, k]
        for s in range(4):
            raw[k, s, :] = out[s, k, row, :]
    wall_rows(splat, raw, edge_w)


def final_residual_kernel(splat, fix, jac, base_in, late_in, rest, base, late, sems):
    loads = [pltpu.make_async_copy(base_in, base, sems.at[0]), pltpu.make_async_copy(late_in, late, sems.at[1])]
    for load in loads:
        load.start()

    def body(lanes):
        planes = [[fix[n, k, :, lanes] for k in range(5)] for n in range(4)]
        for s in range(4):
            applied = local_apply(splat, planes, jac, lanes, s)
            for k in range(5):
                rest[s, k, :, lanes] = -applied[k]

    for_lanes(body, fix.shape[-1])
    for load in loads:
        load.wait()


def final_local_kernel(splat, fix, rest, halo_w, jinv, base, late, inner):
    row = position()[3]
    at, size = lax.axis_index("span"), lax.axis_size("span")
    there = {0: at > 0, 3: at < size - 1}

    def body(lanes):
        for s in range(4):
            known = with_wall(rest, halo_w, s, lanes, row)
            if s in (0, 3):
                beyond = beyond_span(splat, late.at[s // 3], lanes, there[s])
                known = [known[k] + beyond[k] for k in range(5)]
            swept = sweep(jinv, s, lanes, known)
            for k in range(5):
                inner[s, k, :, lanes] = (base[s, k, :, lanes] + fix[s, k, :, lanes]) + swept[k]

    for_lanes(body, fix.shape[-1])


def final_edge_kernel(splat, inner, halo_b, halo_a, jinv, out, edges, sems):
    _, plane_a, plane_b, _ = position()
    real = inside()
    stores = [pltpu.make_async_copy(inner.at[pl.ds(1, 2)], out.at[pl.ds(1, 2)], sems.at[2])]
    stores[0].start()
    for n, (plane, halo, there) in enumerate(((plane_b, halo_b, real), (plane_a, halo_a, None))):

        def body(lanes, n=n, plane=plane, halo=halo, there=there):
            swept = sweep(jinv, plane, lanes, beyond_span(splat, halo, lanes, there))
            for k in range(5):
                edges[n, k, :, lanes] = inner[plane, k, :, lanes] + swept[k]

        for_lanes(body, inner.shape[-1])
        stores.append(pltpu.make_async_copy(edges.at[n], out.at[plane], sems.at[n]))
        stores[-1].start()
    for store in stores:
        store.wait()


def exchange(edge_a, edge_b, edge_w):
    size = lax.axis_size("span")
    even = [p for i in range(0, size, 2) for p in ((i, i + 1), (i + 1, i))]
    odd = [((i + 1) % size, (j + 1) % size) for i, j in even]
    halo_b = lax.ppermute(edge_b, "span", odd)
    halo_w = lax.ppermute(edge_w, "wall", [(0, 1), (1, 0)])
    halo_a = lax.ppermute(edge_a, "span", even)
    return halo_a, halo_b, halo_w


def local(rhs, jac, jac_inv, wall_coupling, span_coupling, block_owner, block_slot, coarse_inv):
    rhs = in_hbm(rhs.transpose(0, 2, 1, 3))
    jac_in = jac.transpose(0, 2, 3, 1, 4)
    jinv_in = jac_inv.transpose(0, 2, 3, 1, 4)
    inv = coarse_inv[0, 0].transpose(0, 2, 1)
    field, plane, edge = shaped(*rhs.shape), shaped(*rhs.shape[1:]), shaped(20, rhs.shape[-1])
    field_out = pltpu.HBM(rhs.shape, F32)
    outer = pltpu.VMEM((2, *rhs.shape[1:]), F32)
    raw = pltpu.VMEM(rhs.shape[1:], F32)
    owners, slots = lax.axis_size("patch"), coarse_inv.shape[-1]
    aggregates, columns = owners * slots, 5 * LANES
    chunks = shaped(owners, slots, columns)

    rhs_in = rhs
    b, a, splat, onehot_t = call(
        first_edge_kernel,
        [plane, plane, shaped(2, 5, 5, 8, LANES), shaped(aggregates, block_owner.size)],
        [in_hbm(x) for x in (wall_coupling, span_coupling, block_owner, block_slot, rhs_in, jinv_in)],
        places=[HBM] * 6,
        scratch=[
            pltpu.SMEM(wall_coupling.shape, F32),
            pltpu.SMEM(span_coupling.shape, F32),
            pltpu.VMEM(block_owner.shape, jnp.int32),
            pltpu.VMEM(block_owner.shape, jnp.int32),
            outer,
            pltpu.VMEM((2, *jinv_in.shape[1:]), F32),
            pltpu.SemaphoreType.DMA((4,)),
            pltpu.SemaphoreType.DMA((2, 2)),
        ],
    )
    rhs, first, w = call(
        first_inner_kernel,
        [field, field, edge],
        [splat, b, a, rhs_in, in_hbm(jinv_in)],
        places=[VMEM] * 3 + [HBM] * 2,
        scratch=[raw, pltpu.VMEM((2, *jinv_in.shape[1:]), F32), pltpu.SemaphoreType.DMA((3,))],
    )
    halo_a, halo_b, halo_w = exchange(a, b, w)
    [rest] = call(first_residual_kernel, [field], [splat, first, rhs, jac_in])
    [inner] = call(second_local_kernel, [field], [first, rest, halo_w, jinv_in])
    a, b, w = call(
        second_edge_kernel, [plane, plane, edge], [splat, inner, halo_b, halo_a, jinv_in], scratch=[raw]
    )
    halo_a, halo_b, halo_w = exchange(a, b, w)
    [rest] = call(second_residual_kernel, [field], [splat, inner, b, a, rhs, jac_in])
    partial, base = call(
        defect_local_kernel,
        [shaped(aggregates, columns), field_out],
        [inner, b, a, rest, halo_w, jinv_in, onehot_t],
        out_places=[VMEM, HBM],
        scratch=[pltpu.VMEM(rhs.shape, F32), pltpu.VMEM(rhs.shape, F32), pltpu.SemaphoreType.DMA((1,))],
    )
    partial, late = call(
        restrict_kernel,
        [chunks, pltpu.HBM((2, *plane.shape), F32)],
        [splat, partial, halo_b, halo_a, onehot_t],
        out_places=[VMEM, HBM],
        scratch=[pltpu.SemaphoreType.DMA((2,))],
    )
    received = lax.all_to_all(partial, "patch", split_axis=0, concat_axis=0, tiled=True)
    [mine] = call(sum_kernel, [shaped(slots, columns)], [received])
    theirs = lax.ppermute(mine, "wall", [(0, 1), (1, 0)])
    [reply] = call(coarse_kernel, [chunks], [inv, mine, theirs])
    fixes = lax.all_to_all(reply, "patch", split_axis=0, concat_axis=0, tiled=True)
    fix, a, b, w = call(
        prolong_kernel,
        [field, plane, plane, edge],
        [splat, block_owner, block_slot, fixes],
        scratch=[pltpu.VMEM((aggregates, columns), F32), raw],
    )
    halo_a, halo_b, halo_w = exchange(a, b, w)
    rest, base, late = call(
        final_residual_kernel,
        [field, field, shaped(2, *plane.shape)],
        [splat, fix, jac_in, in_hbm(base), in_hbm(late)],
        places=[VMEM] * 3 + [HBM] * 2,
        scratch=[pltpu.SemaphoreType.DMA((2,))],
    )
    [inner] = call(final_local_kernel, [field], [splat, fix, rest, halo_w, jinv_in, base, late])
    [out] = call(
        final_edge_kernel,
        [field_out],
        [splat, inner, halo_b, halo_a, jinv_in],
        out_places=[HBM],
        scratch=[outer, pltpu.SemaphoreType.DMA((3,))],
    )
    return out.transpose(0, 2, 1, 3)


def solution(mesh):
    return jax.shard_map(
        local,
        mesh=mesh,
        in_specs=(
            P("span", "wall", None, "patch"),
            P("span", "wall", None, None, "patch"),
            P("span", "wall", None, None, "patch"),
            P(),
            P(),
            P("span", "wall", "patch"),
            P("span", "wall", "patch"),
            P("span", "wall", None, None, "patch"),
        ),
        out_specs=P("span", "wall", None, "patch"),
        check_vma=False,
    )
```

```python
import functools
import math

import jax
import jax.numpy as jnp
from jax import lax
from jax.experimental import pallas as pl
from jax.experimental.pallas import tpu as pltpu
from jax.sharding import PartitionSpec as P

LANES = 128
VMEM = pl.BlockSpec(memory_space=pltpu.VMEM)
SMEM = pl.BlockSpec(memory_space=pltpu.SMEM)
HBM = pl.BlockSpec(memory_space=pltpu.HBM)
F32 = jnp.float32


def shaped(*shape):
    return jax.ShapeDtypeStruct(shape, F32)


def in_hbm(array):
    return pltpu.with_memory_space_constraint(array, pltpu.HBM)


def call(kernel, outs, args, places=None, out_places=None, scratch=()):
    size = 2 * sum(math.prod(a.shape) for a in (*args, *outs))
    return pl.pallas_call(
        kernel,
        out_shape=outs,
        in_specs=places or [VMEM] * len(args),
        out_specs=out_places or [VMEM] * len(outs),
        scratch_shapes=scratch,
        cost_estimate=pl.CostEstimate(flops=size, bytes_accessed=size, transcendentals=0),
        compiler_params=pltpu.CompilerParams(vmem_limit_bytes=8 * 2**20),
    )(*args)


def total(terms):
    return functools.reduce(lambda a, b: a + b, terms)


def position():
    span_at, wall_at = lax.axis_index("span"), lax.axis_index("wall")
    odd = lax.rem(span_at, 2)
    plane_a = 3 - 3 * odd
    return odd == 0, plane_a, 3 - plane_a, 7 - 7 * wall_at


def inside():
    at, size = lax.axis_index("span"), lax.axis_size("span")
    return jnp.logical_and(at > 0, at < size - 1)


def mix(splat, which, values):
    return [total([splat[which, k, i] * values[k] for k in range(5)]) for i in range(5)]


def sweep(jinv, s, lanes, values):
    return [total([jinv[s, i, k, :, lanes] * values[k] for k in range(5)]) for i in range(5)]


def beyond_span(splat, halo, lanes, real=None):
    values = [halo[k, :, lanes] for k in range(5)]
    if real is not None:
        values = [jnp.where(real, v, 0.0) for v in values]
    return mix(splat, 1, values)


def wall_rows(splat, raw, out):
    for q in range(out.shape[-1] // LANES):
        lanes = slice(q * LANES, (q + 1) * LANES)
        mixed = mix(splat, 0, [raw[k, :, lanes] for k in range(5)])
        for i in range(5):
            out[4 * i : 4 * i + 4, lanes] = mixed[i][:4]


def for_lanes(body, length):
    @pl.loop(0, length // LANES)
    def _(q):
        body(pl.ds(pl.multiple_of(q * LANES, LANES), LANES))


def picked_sums(hot, rows):
    hot = hot.astype(jnp.bfloat16)
    high = rows.astype(jnp.bfloat16)
    rest = rows - high.astype(F32)
    middle = rest.astype(jnp.bfloat16)
    low = (rest - middle.astype(F32)).astype(jnp.bfloat16)
    return total([jnp.dot(hot, part, preferred_element_type=F32) for part in (low, middle, high)])


def hot_rows(owner, slot, tiles, cells=range(4)):
    ids = lax.broadcasted_iota(jnp.int32, (8, LANES), 1)
    hot = []
    for s in cells:
        named = owner[s] * 4 + slot[s]
        hot += [jnp.where(named[:, q : q + 1] == ids, 1.0, 0.0) for q in range(tiles)]
    return jnp.concatenate(hot, axis=0)


def first_edge_kernel(
    wall_in, span_in, owner_in, slot_in, rhs_in, jinv_in,
    edge_b, edge_a, splat, onehot_t,
    wall, span, owner, slot, rhs, jinv, small_sems, sems,
):
    _, plane_a, plane_b, _ = position()
    outer = ((plane_b, edge_b), (plane_a, edge_a))
    small = [
        pltpu.make_async_copy(source, here, small_sems.at[n])
        for n, (source, here) in enumerate(((wall_in, wall), (span_in, span), (owner_in, owner), (slot_in, slot)))
    ]
    copies = [
        pltpu.make_async_copy(source.at[plane], here.at[m], sems.at[n, m])
        for m, (plane, _) in enumerate(outer)
        for n, (source, here) in enumerate(((rhs_in, rhs), (jinv_in, jinv)))
    ]
    for copy in small + copies:
        copy.start()
    small[0].wait()
    small[1].wait()
    for which, coupling in enumerate((wall, span)):
        for k in range(5):
            for i in range(5):
                splat[which, k, i] = jnp.full((8, LANES), coupling[k, i], F32)
    small[2].wait()
    small[3].wait()
    onehot_t[...] = hot_rows(owner, slot, rhs.shape[-1] // LANES).T[: onehot_t.shape[0]]
    for m, (_, edge) in enumerate(outer):
        copies[2 * m].wait()
        copies[2 * m + 1].wait()

        def body(lanes, m=m, edge=edge):
            swept = sweep(jinv, m, lanes, [rhs[m, k, :, lanes] for k in range(5)])
            for k in range(5):
                edge[k, :, lanes] = swept[k]

        for_lanes(body, rhs.shape[-1])


def first_inner_kernel(splat, edge_b, edge_a, rhs_in, jinv_in, rhs, first, edge_w, raw, jinv, sems):
    whole = pltpu.make_async_copy(rhs_in, rhs, sems.at[2])
    slabs = [pltpu.make_async_copy(jinv_in.at[1 + m], jinv.at[m], sems.at[m]) for m in range(2)]
    for copy in (whole, *slabs):
        copy.start()
    even, _, _, row = position()
    for k in range(5):
        first[0, k] = jnp.where(even, edge_b[k], edge_a[k])
        first[3, k] = jnp.where(even, edge_a[k], edge_b[k])
    whole.wait()
    for s in (1, 2):
        slabs[s - 1].wait()

        def body(lanes, s=s):
            swept = sweep(jinv, s - 1, lanes, [rhs[s, k, :, lanes] for k in range(5)])
            for k in range(5):
                first[s, k, :, lanes] = swept[k]

        for_lanes(body, rhs.shape[-1])
    for s in range(4):
        for k in range(5):
            raw[k, s, :] = first[s, k, row, :]
    wall_rows(splat, raw, edge_w)


def local_apply(splat, planes, jac, lanes, s):
    own = planes[s]
    rows = lax.broadcasted_iota(jnp.int32, own[0].shape, 0)
    near_wall, near_span = [], []
    for k in range(5):
        up = jnp.where(rows == 7, 0.0, pltpu.roll(own[k], 7, 0))
        down = jnp.where(rows == 0, 0.0, pltpu.roll(own[k], 1, 0))
        near_wall.append(up + down)
        near_span.append(total([planes[n][k] for n in (s - 1, s + 1) if 0 <= n < 4]))
    from_wall, from_span = mix(splat, 0, near_wall), mix(splat, 1, near_span)
    return [
        total([jac[s, k, i, :, lanes] * own[k] for k in range(5)]) - (from_wall[i] + from_span[i])
        for i in range(5)
    ]


def with_wall(rest, halo_w, s, lanes, row):
    rows = lax.broadcasted_iota(jnp.int32, (8, LANES), 0)
    return [
        rest[s, i, :, lanes] + jnp.where(rows == row, halo_w[4 * i + s, lanes][None, :], 0.0) for i in range(5)
    ]


def first_residual_kernel(splat, first, rhs, jac, rest):
    def body(lanes):
        planes = [[first[n, k, :, lanes] for k in range(5)] for n in range(4)]
        for s in range(4):
            applied = local_apply(splat, planes, jac, lanes, s)
            for k in range(5):
                rest[s, k, :, lanes] = rhs[s, k, :, lanes] - applied[k]

    for_lanes(body, rhs.shape[-1])


def second_local_kernel(first, rest, halo_w, jinv, inner):
    row = position()[3]

    def body(lanes):
        for s in range(4):
            swept = sweep(jinv, s, lanes, with_wall(rest, halo_w, s, lanes, row))
            for k in range(5):
                inner[s, k, :, lanes] = first[s, k, :, lanes] + swept[k]

    for_lanes(body, rest.shape[-1])


def second_edge_kernel(splat, inner, halo_b, halo_a, jinv, edge_b, edge_a):
    _, plane_a, plane_b, _ = position()
    real = inside()

    def body(lanes):
        for plane, halo, edge, there in ((plane_b, halo_b, edge_b, real), (plane_a, halo_a, edge_a, None)):
            swept = sweep(jinv, plane, lanes, beyond_span(splat, halo, lanes, there))
            for k in range(5):
                edge[k, :, lanes] = inner[plane, k, :, lanes] + swept[k]

    for_lanes(body, inner.shape[-1])


def second_wall_kernel(splat, inner, edge_b, edge_a, edge_w, raw):
    even, _, _, row = position()
    for k in range(5):
        for s in (1, 2):
            raw[k, s, :] = inner[s, k, row, :]
        a, b = edge_a[k, row, :], edge_b[k, row, :]
        raw[k, 0, :] = jnp.where(even, b, a)
        raw[k, 3, :] = jnp.where(even, a, b)
    wall_rows(splat, raw, edge_w)


def planes_of(even, inner, edge_a, edge_b, lanes):
    a = [edge_a[k, :, lanes] for k in range(5)]
    b = [edge_b[k, :, lanes] for k in range(5)]
    return [
        [jnp.where(even, b[k], a[k]) for k in range(5)],
        [inner[1, k, :, lanes] for k in range(5)],
        [inner[2, k, :, lanes] for k in range(5)],
        [jnp.where(even, a[k], b[k]) for k in range(5)],
    ]


def second_residual_kernel(splat, inner, edge_b, edge_a, rhs, jac, rest):
    even = position()[0]

    def body(lanes):
        planes = planes_of(even, inner, edge_a, edge_b, lanes)
        for s in range(4):
            applied = local_apply(splat, planes, jac, lanes, s)
            for k in range(5):
                rest[s, k, :, lanes] = rhs[s, k, :, lanes] - applied[k]

    for_lanes(body, rhs.shape[-1])


def defect_local_kernel(inner, edge_b, edge_a, rest, halo_w, jinv, onehot_t, partial, base_out, base, defect, sems):
    even, _, _, row = position()

    def body(lanes):
        planes = planes_of(even, inner, edge_a, edge_b, lanes)
        for s in range(4):
            known = with_wall(rest, halo_w, s, lanes, row)
            swept = sweep(jinv, s, lanes, known)
            for k in range(5):
                base[s, k, :, lanes] = planes[s][k] + swept[k]
                defect[s, k, :, lanes] = known[k]

    for_lanes(body, rest.shape[-1])
    store = pltpu.make_async_copy(base, base_out, sems.at[0])
    store.start()
    tiles = defect.shape[-1] // LANES
    for k in range(5):
        rows = jnp.concatenate(
            [defect[s, k, :, q * LANES : (q + 1) * LANES] for s in range(4) for q in range(tiles)], axis=0
        )
        partial[:, k * LANES : (k + 1) * LANES] = picked_sums(onehot_t[...], rows)
    store.wait()


def restrict_kernel(splat, inner, halo_b, halo_a, onehot_t, partial, late_out, sems):
    real = inside()
    at_a = 1 - lax.rem(lax.axis_index("span"), 2)
    stores = [
        pltpu.make_async_copy(halo_b, late_out.at[1 - at_a], sems.at[0]),
        pltpu.make_async_copy(halo_a, late_out.at[at_a], sems.at[1]),
    ]
    for store in stores:
        store.start()
    tiles = halo_a.shape[-1] // LANES
    parts = []
    for halo, there in ((halo_b, real), (halo_a, None)):
        for q in range(tiles):
            parts.append(beyond_span(splat, halo, slice(q * LANES, (q + 1) * LANES), there))
    width = 8 * tiles
    even = at_a == 1
    low, high = onehot_t[:, :width], onehot_t[:, 3 * width :]
    hot = jnp.concatenate([jnp.where(even, low, high), jnp.where(even, high, low)], axis=1)
    slots = partial.shape[1]
    rows = jnp.concatenate([jnp.concatenate(part, axis=1) for part in parts], axis=0)
    sums = inner[...] + picked_sums(hot, rows)
    for p in range(partial.shape[0]):
        partial[p] = sums[p * slots : (p + 1) * slots]
    for store in stores:
        store.wait()


def sum_kernel(received, sums):
    sums[...] = total([received[p] for p in range(received.shape[0])])


def coarse_kernel(inv, own, other, out):
    first_group = lax.axis_index("wall") == 0
    groups = [
        [jnp.where(first_group, x[:, k * LANES : (k + 1) * LANES], y[:, k * LANES : (k + 1) * LANES]) for k in range(5)]
        for x, y in ((own, other), (other, own))
    ]
    for i in range(5):
        rows = inv[i]
        fix = total([rows[:, c * 5 + k : c * 5 + k + 1] * groups[c][k] for c in range(2) for k in range(5)])
        for p in range(out.shape[0]):
            out[p, :, i * LANES : (i + 1) * LANES] = fix


def prolonged(owner, slot, fixes, fix, tiles, cells):
    owners, slots, _ = fixes.shape
    for p in range(owners):
        fix[p * slots : (p + 1) * slots, :] = fixes[p]
    hot = hot_rows(owner, slot, tiles, cells)[:, : owners * slots]
    rows = [picked_sums(hot, fix[:, k * LANES : (k + 1) * LANES]) for k in range(5)]
    return lambda k, n, q: rows[k][(n * tiles + q) * 8 : (n * tiles + q) * 8 + 8]


def prolong_edge_kernel(owner, slot, fixes, edge_b, edge_a, fix):
    even = position()[0]
    tiles = edge_a.shape[-1] // LANES
    tile = prolonged(owner, slot, fixes, fix, tiles, (0, 3))
    for k in range(5):
        for q in range(tiles):
            lanes = slice(q * LANES, (q + 1) * LANES)
            low, high = tile(k, 0, q), tile(k, 1, q)
            edge_b[k, :, lanes] = jnp.where(even, low, high)
            edge_a[k, :, lanes] = jnp.where(even, high, low)


def prolong_inner_kernel(splat, owner, slot, fixes, edge_b, edge_a, out, edge_w, fix, raw):
    even, _, _, row = position()
    tiles = out.shape[-1] // LANES
    tile = prolonged(owner, slot, fixes, fix, tiles, (1, 2))
    for k in range(5):
        out[0, k] = jnp.where(even, edge_b[k], edge_a[k])
        out[3, k] = jnp.where(even, edge_a[k], edge_b[k])
        for n in range(2):
            for q in range(tiles):
                out[1 + n, k, :, q * LANES : (q + 1) * LANES] = tile(k, n, q)
    for k in range(5):
        for s in range(4):
            raw[k, s, :] = out[s, k, row, :]
    wall_rows(splat, raw, edge_w)


def final_residual_kernel(splat, fix, jac, base_in, late_in, rest, base, late, sems):
    loads = [pltpu.make_async_copy(base_in, base, sems.at[0]), pltpu.make_async_copy(late_in, late, sems.at[1])]
    for load in loads:
        load.start()

    def body(lanes):
        planes = [[fix[n, k, :, lanes] for k in range(5)] for n in range(4)]
        for s in range(4):
            applied = local_apply(splat, planes, jac, lanes, s)
            for k in range(5):
                rest[s, k, :, lanes] = -applied[k]

    for_lanes(body, fix.shape[-1])
    for load in loads:
        load.wait()


def final_local_kernel(splat, fix, rest, halo_w, jinv, base, late, inner):
    row = position()[3]
    at, size = lax.axis_index("span"), lax.axis_size("span")
    there = {0: at > 0, 3: at < size - 1}

    def body(lanes):
        for s in range(4):
            known = with_wall(rest, halo_w, s, lanes, row)
            if s in (0, 3):
                beyond = beyond_span(splat, late.at[s // 3], lanes, there[s])
                known = [known[k] + beyond[k] for k in range(5)]
            swept = sweep(jinv, s, lanes, known)
            for k in range(5):
                inner[s, k, :, lanes] = (base[s, k, :, lanes] + fix[s, k, :, lanes]) + swept[k]

    for_lanes(body, fix.shape[-1])


def final_edge_kernel(splat, inner, halo_b, halo_a, jinv, out, edges, sems):
    _, plane_a, plane_b, _ = position()
    real = inside()
    stores = [pltpu.make_async_copy(inner.at[pl.ds(1, 2)], out.at[pl.ds(1, 2)], sems.at[2])]
    stores[0].start()
    for n, (plane, halo, there) in enumerate(((plane_b, halo_b, real), (plane_a, halo_a, None))):

        def body(lanes, n=n, plane=plane, halo=halo, there=there):
            swept = sweep(jinv, plane, lanes, beyond_span(splat, halo, lanes, there))
            for k in range(5):
                edges[n, k, :, lanes] = inner[plane, k, :, lanes] + swept[k]

        for_lanes(body, inner.shape[-1])
        stores.append(pltpu.make_async_copy(edges.at[n], out.at[plane], sems.at[n]))
        stores[-1].start()
    for store in stores:
        store.wait()


def exchange(edge_a, edge_b, edge_w):
    size = lax.axis_size("span")
    even = [p for i in range(0, size, 2) for p in ((i, i + 1), (i + 1, i))]
    odd = [((i + 1) % size, (j + 1) % size) for i, j in even]
    halo_b = lax.ppermute(edge_b, "span", odd)
    halo_w = lax.ppermute(edge_w, "wall", [(0, 1), (1, 0)])
    halo_a = lax.ppermute(edge_a, "span", even)
    return halo_a, halo_b, halo_w


def local(rhs, jac, jac_inv, wall_coupling, span_coupling, block_owner, block_slot, coarse_inv):
    rhs = in_hbm(rhs.transpose(0, 2, 1, 3))
    jac_in = jac.transpose(0, 2, 3, 1, 4)
    jinv_in = jac_inv.transpose(0, 2, 3, 1, 4)
    inv = coarse_inv[0, 0].transpose(0, 2, 1)
    field, plane, edge = shaped(*rhs.shape), shaped(*rhs.shape[1:]), shaped(20, rhs.shape[-1])
    field_out = pltpu.HBM(rhs.shape, F32)
    outer = pltpu.VMEM((2, *rhs.shape[1:]), F32)
    raw = pltpu.VMEM(rhs.shape[1:], F32)
    owners, slots = lax.axis_size("patch"), coarse_inv.shape[-1]
    aggregates, columns = owners * slots, 5 * LANES
    chunks = shaped(owners, slots, columns)

    rhs_in = rhs
    b, a, splat, onehot_t = call(
        first_edge_kernel,
        [plane, plane, shaped(2, 5, 5, 8, LANES), shaped(aggregates, block_owner.size)],
        [in_hbm(x) for x in (wall_coupling, span_coupling, block_owner, block_slot, rhs_in, jinv_in)],
        places=[HBM] * 6,
        scratch=[
            pltpu.SMEM(wall_coupling.shape, F32),
            pltpu.SMEM(span_coupling.shape, F32),
            pltpu.VMEM(block_owner.shape, jnp.int32),
            pltpu.VMEM(block_owner.shape, jnp.int32),
            outer,
            pltpu.VMEM((2, *jinv_in.shape[1:]), F32),
            pltpu.SemaphoreType.DMA((4,)),
            pltpu.SemaphoreType.DMA((2, 2)),
        ],
    )
    rhs, first, w = call(
        first_inner_kernel,
        [field, field, edge],
        [splat, b, a, rhs_in, in_hbm(jinv_in)],
        places=[VMEM] * 3 + [HBM] * 2,
        scratch=[raw, pltpu.VMEM((2, *jinv_in.shape[1:]), F32), pltpu.SemaphoreType.DMA((3,))],
    )
    halo_a, halo_b, halo_w = exchange(a, b, w)
    [rest] = call(first_residual_kernel, [field], [splat, first, rhs, jac_in])
    [inner] = call(second_local_kernel, [field], [first, rest, halo_w, jinv_in])
    b, a = call(second_edge_kernel, [plane, plane], [splat, inner, halo_b, halo_a, jinv_in])
    [w] = call(second_wall_kernel, [edge], [splat, inner, b, a], scratch=[raw])
    halo_a, halo_b, halo_w = exchange(a, b, w)
    [rest] = call(second_residual_kernel, [field], [splat, inner, b, a, rhs, jac_in])
    partial, base = call(
        defect_local_kernel,
        [shaped(aggregates, columns), field_out],
        [inner, b, a, rest, halo_w, jinv_in, onehot_t],
        out_places=[VMEM, HBM],
        scratch=[pltpu.VMEM(rhs.shape, F32), pltpu.VMEM(rhs.shape, F32), pltpu.SemaphoreType.DMA((1,))],
    )
    partial, late = call(
        restrict_kernel,
        [chunks, pltpu.HBM((2, *plane.shape), F32)],
        [splat, partial, halo_b, halo_a, onehot_t],
        out_places=[VMEM, HBM],
        scratch=[pltpu.SemaphoreType.DMA((2,))],
    )
    received = lax.all_to_all(partial, "patch", split_axis=0, concat_axis=0, tiled=True)
    [mine] = call(sum_kernel, [shaped(slots, columns)], [received])
    theirs = lax.ppermute(mine, "wall", [(0, 1), (1, 0)])
    [reply] = call(coarse_kernel, [chunks], [inv, mine, theirs])
    fixes = lax.all_to_all(reply, "patch", split_axis=0, concat_axis=0, tiled=True)
    held = pltpu.VMEM((aggregates, columns), F32)
    b, a = call(prolong_edge_kernel, [plane, plane], [block_owner, block_slot, fixes], scratch=[held])
    fix, w = call(
        prolong_inner_kernel, [field, edge], [splat, block_owner, block_slot, fixes, b, a], scratch=[held, raw]
    )
    halo_a, halo_b, halo_w = exchange(a, b, w)
    rest, base, late = call(
        final_residual_kernel,
        [field, field, shaped(2, *plane.shape)],
        [splat, fix, jac_in, in_hbm(base), in_hbm(late)],
        places=[VMEM] * 3 + [HBM] * 2,
        scratch=[pltpu.SemaphoreType.DMA((2,))],
    )
    [inner] = call(final_local_kernel, [field], [splat, fix, rest, halo_w, jinv_in, base, late])
    [out] = call(
        final_edge_kernel,
        [field_out],
        [splat, inner, halo_b, halo_a, jinv_in],
        out_places=[HBM],
        scratch=[outer, pltpu.SemaphoreType.DMA((3,))],
    )
    return out.transpose(0, 2, 1, 3)


def solution(mesh):
    return jax.shard_map(
        local,
        mesh=mesh,
        in_specs=(
            P("span", "wall", None, "patch"),
            P("span", "wall", None, None, "patch"),
            P("span", "wall", None, None, "patch"),
            P(),
            P(),
            P("span", "wall", "patch"),
            P("span", "wall", "patch"),
            P("span", "wall", None, None, "patch"),
        ),
        out_specs=P("span", "wall", None, "patch"),
        check_vma=False,
    )
```

```python
import functools
import math

import jax
import jax.numpy as jnp
from jax import lax
from jax.experimental import pallas as pl
from jax.experimental.pallas import tpu as pltpu
from jax.sharding import PartitionSpec as P

LANES = 128
VMEM = pl.BlockSpec(memory_space=pltpu.VMEM)
SMEM = pl.BlockSpec(memory_space=pltpu.SMEM)
HBM = pl.BlockSpec(memory_space=pltpu.HBM)
F32 = jnp.float32


def shaped(*shape):
    return jax.ShapeDtypeStruct(shape, F32)


def in_hbm(array):
    return pltpu.with_memory_space_constraint(array, pltpu.HBM)


def call(kernel, outs, args, places=None, out_places=None, scratch=(), aliases=None):
    size = 2 * sum(math.prod(a.shape) for a in (*args, *outs))
    return pl.pallas_call(
        kernel,
        out_shape=outs,
        in_specs=places or [VMEM] * len(args),
        out_specs=out_places or [VMEM] * len(outs),
        scratch_shapes=scratch,
        input_output_aliases=aliases or {},
        cost_estimate=pl.CostEstimate(flops=size, bytes_accessed=size, transcendentals=0),
        compiler_params=pltpu.CompilerParams(vmem_limit_bytes=8 * 2**20),
    )(*args)


def total(terms):
    return functools.reduce(lambda a, b: a + b, terms)


def position():
    span_at, wall_at = lax.axis_index("span"), lax.axis_index("wall")
    odd = lax.rem(span_at, 2)
    plane_a = 3 - 3 * odd
    return odd == 0, plane_a, 3 - plane_a, 7 - 7 * wall_at


def inside():
    at, size = lax.axis_index("span"), lax.axis_size("span")
    return jnp.logical_and(at > 0, at < size - 1)


def mix(splat, which, values):
    return [total([splat[which, k, i] * values[k] for k in range(5)]) for i in range(5)]


def sweep(jinv, s, lanes, values):
    return [total([jinv[s, i, k, :, lanes] * values[k] for k in range(5)]) for i in range(5)]


def beyond_span(splat, halo, lanes, real=None):
    values = [halo[k, :, lanes] for k in range(5)]
    if real is not None:
        values = [jnp.where(real, v, 0.0) for v in values]
    return mix(splat, 1, values)


def wall_rows(splat, raw, out):
    for q in range(out.shape[-1] // LANES):
        lanes = slice(q * LANES, (q + 1) * LANES)
        mixed = mix(splat, 0, [raw[k, :, lanes] for k in range(5)])
        for i in range(5):
            out[4 * i : 4 * i + 4, lanes] = mixed[i][:4]


def for_lanes(body, length):
    @pl.loop(0, length // LANES)
    def _(q):
        body(pl.ds(pl.multiple_of(q * LANES, LANES), LANES))


def picked_sums(hot, rows):
    hot = hot.astype(jnp.bfloat16)
    high = rows.astype(jnp.bfloat16)
    rest = rows - high.astype(F32)
    middle = rest.astype(jnp.bfloat16)
    low = (rest - middle.astype(F32)).astype(jnp.bfloat16)
    return total([jnp.dot(hot, part, preferred_element_type=F32) for part in (low, middle, high)])


def hot_rows(owner, slot, tiles, cells=range(4)):
    ids = lax.broadcasted_iota(jnp.int32, (8, LANES), 1)
    hot = []
    for s in cells:
        named = owner[s] * 4 + slot[s]
        hot += [jnp.where(named[:, q : q + 1] == ids, 1.0, 0.0) for q in range(tiles)]
    return jnp.concatenate(hot, axis=0)


def first_edge_kernel(
    wall_in, span_in, owner_in, slot_in, rhs_in, jinv_in,
    edge_b, edge_a, splat, onehot_t,
    wall, span, owner, slot, rhs, jinv, small_sems, sems,
):
    _, plane_a, plane_b, _ = position()
    outer = ((plane_b, edge_b), (plane_a, edge_a))
    small = [
        pltpu.make_async_copy(source, here, small_sems.at[n])
        for n, (source, here) in enumerate(((wall_in, wall), (span_in, span), (owner_in, owner), (slot_in, slot)))
    ]
    copies = [
        pltpu.make_async_copy(source.at[plane], here.at[m], sems.at[n, m])
        for m, (plane, _) in enumerate(outer)
        for n, (source, here) in enumerate(((rhs_in, rhs), (jinv_in, jinv)))
    ]
    for copy in small + copies:
        copy.start()
    small[0].wait()
    small[1].wait()
    for which, coupling in enumerate((wall, span)):
        for k in range(5):
            for i in range(5):
                splat[which, k, i] = jnp.full((8, LANES), coupling[k, i], F32)
    small[2].wait()
    small[3].wait()
    onehot_t[...] = hot_rows(owner, slot, rhs.shape[-1] // LANES).T[: onehot_t.shape[0]]
    for m, (_, edge) in enumerate(outer):
        copies[2 * m].wait()
        copies[2 * m + 1].wait()

        def body(lanes, m=m, edge=edge):
            swept = sweep(jinv, m, lanes, [rhs[m, k, :, lanes] for k in range(5)])
            for k in range(5):
                edge[k, :, lanes] = swept[k]

        for_lanes(body, rhs.shape[-1])


def first_inner_kernel(splat, edge_b, edge_a, rhs_in, jinv_in, rhs, first, edge_w, raw, jinv, sems):
    whole = pltpu.make_async_copy(rhs_in, rhs, sems.at[2])
    slabs = [pltpu.make_async_copy(jinv_in.at[1 + m], jinv.at[m], sems.at[m]) for m in range(2)]
    for copy in (whole, *slabs):
        copy.start()
    even, _, _, row = position()
    for k in range(5):
        first[0, k] = jnp.where(even, edge_b[k], edge_a[k])
        first[3, k] = jnp.where(even, edge_a[k], edge_b[k])
    whole.wait()
    for s in (1, 2):
        slabs[s - 1].wait()

        def body(lanes, s=s):
            swept = sweep(jinv, s - 1, lanes, [rhs[s, k, :, lanes] for k in range(5)])
            for k in range(5):
                first[s, k, :, lanes] = swept[k]

        for_lanes(body, rhs.shape[-1])
    for s in range(4):
        for k in range(5):
            raw[k, s, :] = first[s, k, row, :]
    wall_rows(splat, raw, edge_w)


def local_apply(splat, planes, jac, lanes, s):
    own = planes[s]
    rows = lax.broadcasted_iota(jnp.int32, own[0].shape, 0)
    near_wall, near_span = [], []
    for k in range(5):
        up = jnp.where(rows == 7, 0.0, pltpu.roll(own[k], 7, 0))
        down = jnp.where(rows == 0, 0.0, pltpu.roll(own[k], 1, 0))
        near_wall.append(up + down)
        near_span.append(total([planes[n][k] for n in (s - 1, s + 1) if 0 <= n < 4]))
    from_wall, from_span = mix(splat, 0, near_wall), mix(splat, 1, near_span)
    return [
        total([jac[s, k, i, :, lanes] * own[k] for k in range(5)]) - (from_wall[i] + from_span[i])
        for i in range(5)
    ]


def with_wall(rest, halo_w, s, lanes, row):
    rows = lax.broadcasted_iota(jnp.int32, (8, LANES), 0)
    return [
        rest[s, i, :, lanes] + jnp.where(rows == row, halo_w[4 * i + s, lanes][None, :], 0.0) for i in range(5)
    ]


def first_residual_kernel(splat, first, rhs, jac, rest):
    def body(lanes):
        planes = [[first[n, k, :, lanes] for k in range(5)] for n in range(4)]
        for s in range(4):
            applied = local_apply(splat, planes, jac, lanes, s)
            for k in range(5):
                rest[s, k, :, lanes] = rhs[s, k, :, lanes] - applied[k]

    for_lanes(body, rhs.shape[-1])


def second_local_kernel(first, rest, halo_w, jinv, inner):
    row = position()[3]

    def body(lanes):
        for s in range(4):
            swept = sweep(jinv, s, lanes, with_wall(rest, halo_w, s, lanes, row))
            for k in range(5):
                inner[s, k, :, lanes] = first[s, k, :, lanes] + swept[k]

    for_lanes(body, rest.shape[-1])


def second_edge_kernel(splat, inner, halo_b, halo_a, jinv, edge_b, edge_a):
    _, plane_a, plane_b, _ = position()
    real = inside()

    def body(lanes):
        for plane, halo, edge, there in ((plane_b, halo_b, edge_b, real), (plane_a, halo_a, edge_a, None)):
            swept = sweep(jinv, plane, lanes, beyond_span(splat, halo, lanes, there))
            for k in range(5):
                edge[k, :, lanes] = inner[plane, k, :, lanes] + swept[k]

    for_lanes(body, inner.shape[-1])


def second_wall_kernel(splat, inner, edge_b, edge_a, edge_w, raw):
    even, _, _, row = position()
    for k in range(5):
        for s in (1, 2):
            raw[k, s, :] = inner[s, k, row, :]
        a, b = edge_a[k, row, :], edge_b[k, row, :]
        raw[k, 0, :] = jnp.where(even, b, a)
        raw[k, 3, :] = jnp.where(even, a, b)
    wall_rows(splat, raw, edge_w)


def planes_of(even, inner, edge_a, edge_b, lanes):
    a = [edge_a[k, :, lanes] for k in range(5)]
    b = [edge_b[k, :, lanes] for k in range(5)]
    return [
        [jnp.where(even, b[k], a[k]) for k in range(5)],
        [inner[1, k, :, lanes] for k in range(5)],
        [inner[2, k, :, lanes] for k in range(5)],
        [jnp.where(even, a[k], b[k]) for k in range(5)],
    ]


def second_residual_kernel(splat, inner, edge_b, edge_a, rhs, jac, rest):
    even = position()[0]

    def body(lanes):
        planes = planes_of(even, inner, edge_a, edge_b, lanes)
        for s in range(4):
            applied = local_apply(splat, planes, jac, lanes, s)
            for k in range(5):
                rest[s, k, :, lanes] = rhs[s, k, :, lanes] - applied[k]

    for_lanes(body, rhs.shape[-1])


def defect_local_kernel(inner, edge_b, edge_a, rest, halo_w, jinv, onehot_t, partial, base_out, base, defect, sems):
    even, _, _, row = position()

    def body(lanes):
        planes = planes_of(even, inner, edge_a, edge_b, lanes)
        for s in range(4):
            known = with_wall(rest, halo_w, s, lanes, row)
            swept = sweep(jinv, s, lanes, known)
            for k in range(5):
                base[s, k, :, lanes] = planes[s][k] + swept[k]
                defect[s, k, :, lanes] = known[k]

    for_lanes(body, rest.shape[-1])
    store = pltpu.make_async_copy(base, base_out, sems.at[0])
    store.start()
    tiles = defect.shape[-1] // LANES
    for k in range(5):
        rows = jnp.concatenate(
            [defect[s, k, :, q * LANES : (q + 1) * LANES] for s in range(4) for q in range(tiles)], axis=0
        )
        partial[:, k * LANES : (k + 1) * LANES] = picked_sums(onehot_t[...], rows)
    store.wait()


def restrict_kernel(splat, inner, halo_b, halo_a, onehot_t, partial, late_out, sems):
    real = inside()
    at_a = 1 - lax.rem(lax.axis_index("span"), 2)
    stores = [
        pltpu.make_async_copy(halo_b, late_out.at[1 - at_a], sems.at[0]),
        pltpu.make_async_copy(halo_a, late_out.at[at_a], sems.at[1]),
    ]
    for store in stores:
        store.start()
    tiles = halo_a.shape[-1] // LANES
    parts = []
    for halo, there in ((halo_b, real), (halo_a, None)):
        for q in range(tiles):
            parts.append(beyond_span(splat, halo, slice(q * LANES, (q + 1) * LANES), there))
    width = 8 * tiles
    even = at_a == 1
    low, high = onehot_t[:, :width], onehot_t[:, 3 * width :]
    hot = jnp.concatenate([jnp.where(even, low, high), jnp.where(even, high, low)], axis=1)
    slots = partial.shape[1]
    rows = jnp.concatenate([jnp.concatenate(part, axis=1) for part in parts], axis=0)
    sums = inner[...] + picked_sums(hot, rows)
    for p in range(partial.shape[0]):
        partial[p] = sums[p * slots : (p + 1) * slots]
    for store in stores:
        store.wait()


def sum_kernel(received, sums):
    sums[...] = total([received[p] for p in range(received.shape[0])])


def coarse_kernel(inv, own, other, out):
    first_group = lax.axis_index("wall") == 0
    groups = [
        [jnp.where(first_group, x[:, k * LANES : (k + 1) * LANES], y[:, k * LANES : (k + 1) * LANES]) for k in range(5)]
        for x, y in ((own, other), (other, own))
    ]
    for i in range(5):
        rows = inv[i]
        fix = total([rows[:, c * 5 + k : c * 5 + k + 1] * groups[c][k] for c in range(2) for k in range(5)])
        for p in range(out.shape[0]):
            out[p, :, i * LANES : (i + 1) * LANES] = fix


def prolonged(owner, slot, fixes, fix, tiles, cells):
    owners, slots, _ = fixes.shape
    for p in range(owners):
        fix[p * slots : (p + 1) * slots, :] = fixes[p]
    hot = hot_rows(owner, slot, tiles, cells)[:, : owners * slots]
    rows = [picked_sums(hot, fix[:, k * LANES : (k + 1) * LANES]) for k in range(5)]
    return lambda k, n, q: rows[k][(n * tiles + q) * 8 : (n * tiles + q) * 8 + 8]


def prolong_edge_kernel(owner, slot, fixes, edge_b, edge_a, fix):
    even = position()[0]
    tiles = edge_a.shape[-1] // LANES
    tile = prolonged(owner, slot, fixes, fix, tiles, (0, 3))
    for k in range(5):
        for q in range(tiles):
            lanes = slice(q * LANES, (q + 1) * LANES)
            low, high = tile(k, 0, q), tile(k, 1, q)
            edge_b[k, :, lanes] = jnp.where(even, low, high)
            edge_a[k, :, lanes] = jnp.where(even, high, low)


def prolong_inner_kernel(splat, owner, slot, fixes, edge_b, edge_a, out, edge_w, fix, raw):
    even, _, _, row = position()
    tiles = out.shape[-1] // LANES
    tile = prolonged(owner, slot, fixes, fix, tiles, (1, 2))
    for k in range(5):
        out[0, k] = jnp.where(even, edge_b[k], edge_a[k])
        out[3, k] = jnp.where(even, edge_a[k], edge_b[k])
        for n in range(2):
            for q in range(tiles):
                out[1 + n, k, :, q * LANES : (q + 1) * LANES] = tile(k, n, q)
    for k in range(5):
        for s in range(4):
            raw[k, s, :] = out[s, k, row, :]
    wall_rows(splat, raw, edge_w)


def final_residual_kernel(splat, fix, jac, base_in, late_in, rest, base, late, sems):
    loads = [pltpu.make_async_copy(base_in, base, sems.at[0]), pltpu.make_async_copy(late_in, late, sems.at[1])]
    for load in loads:
        load.start()

    def body(lanes):
        planes = [[fix[n, k, :, lanes] for k in range(5)] for n in range(4)]
        for s in range(4):
            applied = local_apply(splat, planes, jac, lanes, s)
            for k in range(5):
                rest[s, k, :, lanes] = -applied[k]

    for_lanes(body, fix.shape[-1])
    for load in loads:
        load.wait()


def final_local_kernel(splat, fix, rest, halo_w, jinv, base, late, inner, out, sems):
    row = position()[3]
    at, size = lax.axis_index("span"), lax.axis_size("span")
    there = {0: at > 0, 3: at < size - 1}
    store = pltpu.make_async_copy(inner.at[pl.ds(1, 2)], out.at[pl.ds(1, 2)], sems.at[0])
    for cells in ((1, 2), (0, 3)):

        def body(lanes, cells=cells):
            for s in cells:
                known = with_wall(rest, halo_w, s, lanes, row)
                if s in there:
                    beyond = beyond_span(splat, late.at[s // 3], lanes, there[s])
                    known = [known[k] + beyond[k] for k in range(5)]
                swept = sweep(jinv, s, lanes, known)
                for k in range(5):
                    inner[s, k, :, lanes] = (base[s, k, :, lanes] + fix[s, k, :, lanes]) + swept[k]

        for_lanes(body, fix.shape[-1])
        if cells == (1, 2):
            store.start()
    store.wait()


def final_edge_kernel(splat, inner, halo_b, halo_a, jinv, out_had, out, edges, sems):
    del out_had
    _, plane_a, plane_b, _ = position()
    real = inside()
    stores = []
    for n, (plane, halo, there) in enumerate(((plane_b, halo_b, real), (plane_a, halo_a, None))):

        def body(lanes, n=n, plane=plane, halo=halo, there=there):
            swept = sweep(jinv, plane, lanes, beyond_span(splat, halo, lanes, there))
            for k in range(5):
                edges[n, k, :, lanes] = inner[plane, k, :, lanes] + swept[k]

        for_lanes(body, inner.shape[-1])
        stores.append(pltpu.make_async_copy(edges.at[n], out.at[plane], sems.at[n]))
        stores[-1].start()
    for store in stores:
        store.wait()


def exchange(edge_a, edge_b, edge_w):
    size = lax.axis_size("span")
    even = [p for i in range(0, size, 2) for p in ((i, i + 1), (i + 1, i))]
    odd = [((i + 1) % size, (j + 1) % size) for i, j in even]
    halo_b = lax.ppermute(edge_b, "span", odd)
    halo_w = lax.ppermute(edge_w, "wall", [(0, 1), (1, 0)])
    halo_a = lax.ppermute(edge_a, "span", even)
    return halo_a, halo_b, halo_w


def local(rhs, jac, jac_inv, wall_coupling, span_coupling, block_owner, block_slot, coarse_inv):
    rhs = in_hbm(rhs.transpose(0, 2, 1, 3))
    jac_in = jac.transpose(0, 2, 3, 1, 4)
    jinv_in = jac_inv.transpose(0, 2, 3, 1, 4)
    inv = coarse_inv[0, 0].transpose(0, 2, 1)
    field, plane, edge = shaped(*rhs.shape), shaped(*rhs.shape[1:]), shaped(20, rhs.shape[-1])
    field_out = pltpu.HBM(rhs.shape, F32)
    outer = pltpu.VMEM((2, *rhs.shape[1:]), F32)
    raw = pltpu.VMEM(rhs.shape[1:], F32)
    owners, slots = lax.axis_size("patch"), coarse_inv.shape[-1]
    aggregates, columns = owners * slots, 5 * LANES
    chunks = shaped(owners, slots, columns)

    rhs_in = rhs
    b, a, splat, onehot_t = call(
        first_edge_kernel,
        [plane, plane, shaped(2, 5, 5, 8, LANES), shaped(aggregates, block_owner.size)],
        [in_hbm(x) for x in (wall_coupling, span_coupling, block_owner, block_slot, rhs_in, jinv_in)],
        places=[HBM] * 6,
        scratch=[
            pltpu.SMEM(wall_coupling.shape, F32),
            pltpu.SMEM(span_coupling.shape, F32),
            pltpu.VMEM(block_owner.shape, jnp.int32),
            pltpu.VMEM(block_owner.shape, jnp.int32),
            outer,
            pltpu.VMEM((2, *jinv_in.shape[1:]), F32),
            pltpu.SemaphoreType.DMA((4,)),
            pltpu.SemaphoreType.DMA((2, 2)),
        ],
    )
    rhs, first, w = call(
        first_inner_kernel,
        [field, field, edge],
        [splat, b, a, rhs_in, in_hbm(jinv_in)],
        places=[VMEM] * 3 + [HBM] * 2,
        scratch=[raw, pltpu.VMEM((2, *jinv_in.shape[1:]), F32), pltpu.SemaphoreType.DMA((3,))],
    )
    halo_a, halo_b, halo_w = exchange(a, b, w)
    [rest] = call(first_residual_kernel, [field], [splat, first, rhs, jac_in])
    [inner] = call(second_local_kernel, [field], [first, rest, halo_w, jinv_in])
    b, a = call(second_edge_kernel, [plane, plane], [splat, inner, halo_b, halo_a, jinv_in])
    [w] = call(second_wall_kernel, [edge], [splat, inner, b, a], scratch=[raw])
    halo_a, halo_b, halo_w = exchange(a, b, w)
    [rest] = call(second_residual_kernel, [field], [splat, inner, b, a, rhs, jac_in])
    partial, base = call(
        defect_local_kernel,
        [shaped(aggregates, columns), field_out],
        [inner, b, a, rest, halo_w, jinv_in, onehot_t],
        out_places=[VMEM, HBM],
        scratch=[pltpu.VMEM(rhs.shape, F32), pltpu.VMEM(rhs.shape, F32), pltpu.SemaphoreType.DMA((1,))],
    )
    partial, late = call(
        restrict_kernel,
        [chunks, pltpu.HBM((2, *plane.shape), F32)],
        [splat, partial, halo_b, halo_a, onehot_t],
        out_places=[VMEM, HBM],
        scratch=[pltpu.SemaphoreType.DMA((2,))],
    )
    received = lax.all_to_all(partial, "patch", split_axis=0, concat_axis=0, tiled=True)
    [mine] = call(sum_kernel, [shaped(slots, columns)], [received])
    theirs = lax.ppermute(mine, "wall", [(0, 1), (1, 0)])
    [reply] = call(coarse_kernel, [chunks], [inv, mine, theirs])
    fixes = lax.all_to_all(reply, "patch", split_axis=0, concat_axis=0, tiled=True)
    held = pltpu.VMEM((aggregates, columns), F32)
    b, a = call(prolong_edge_kernel, [plane, plane], [block_owner, block_slot, fixes], scratch=[held])
    fix, w = call(
        prolong_inner_kernel, [field, edge], [splat, block_owner, block_slot, fixes, b, a], scratch=[held, raw]
    )
    halo_a, halo_b, halo_w = exchange(a, b, w)
    rest, base, late = call(
        final_residual_kernel,
        [field, field, shaped(2, *plane.shape)],
        [splat, fix, jac_in, in_hbm(base), in_hbm(late)],
        places=[VMEM] * 3 + [HBM] * 2,
        scratch=[pltpu.SemaphoreType.DMA((2,))],
    )
    inner, out = call(
        final_local_kernel,
        [field, field_out],
        [splat, fix, rest, halo_w, jinv_in, base, late],
        out_places=[VMEM, HBM],
        scratch=[pltpu.SemaphoreType.DMA((1,))],
    )
    [out] = call(
        final_edge_kernel,
        [field_out],
        [splat, inner, halo_b, halo_a, jinv_in, in_hbm(out)],
        places=[VMEM] * 5 + [HBM],
        out_places=[HBM],
        scratch=[outer, pltpu.SemaphoreType.DMA((2,))],
        aliases={5: 0},
    )
    return out.transpose(0, 2, 1, 3)


def solution(mesh):
    return jax.shard_map(
        local,
        mesh=mesh,
        in_specs=(
            P("span", "wall", None, "patch"),
            P("span", "wall", None, None, "patch"),
            P("span", "wall", None, None, "patch"),
            P(),
            P(),
            P("span", "wall", "patch"),
            P("span", "wall", "patch"),
            P("span", "wall", None, None, "patch"),
        ),
        out_specs=P("span", "wall", None, "patch"),
        check_vma=False,
    )
```

```python
import functools
import math

import jax
import jax.numpy as jnp
from jax import lax
from jax.experimental import pallas as pl
from jax.experimental.pallas import tpu as pltpu
from jax.sharding import PartitionSpec as P

LANES = 128
VMEM = pl.BlockSpec(memory_space=pltpu.VMEM)
SMEM = pl.BlockSpec(memory_space=pltpu.SMEM)
HBM = pl.BlockSpec(memory_space=pltpu.HBM)
F32 = jnp.float32


def shaped(*shape):
    return jax.ShapeDtypeStruct(shape, F32)


def in_hbm(array):
    return pltpu.with_memory_space_constraint(array, pltpu.HBM)


def call(kernel, outs, args, places=None, out_places=None, scratch=(), aliases=None):
    size = 2 * sum(math.prod(a.shape) for a in (*args, *outs))
    return pl.pallas_call(
        kernel,
        out_shape=outs,
        in_specs=places or [VMEM] * len(args),
        out_specs=out_places or [VMEM] * len(outs),
        scratch_shapes=scratch,
        input_output_aliases=aliases or {},
        cost_estimate=pl.CostEstimate(flops=size, bytes_accessed=size, transcendentals=0),
        compiler_params=pltpu.CompilerParams(vmem_limit_bytes=8 * 2**20),
    )(*args)


def total(terms):
    return functools.reduce(lambda a, b: a + b, terms)


def position():
    span_at, wall_at = lax.axis_index("span"), lax.axis_index("wall")
    odd = lax.rem(span_at, 2)
    plane_a = 3 - 3 * odd
    return odd == 0, plane_a, 3 - plane_a, 7 - 7 * wall_at


def inside():
    at, size = lax.axis_index("span"), lax.axis_size("span")
    return jnp.logical_and(at > 0, at < size - 1)


def mix(splat, which, values):
    return [total([splat[which, k, i] * values[k] for k in range(5)]) for i in range(5)]


def sweep(jinv, s, lanes, values):
    return [total([jinv[s, i, k, :, lanes] * values[k] for k in range(5)]) for i in range(5)]


def beyond_span(splat, halo, lanes, real=None):
    values = [halo[k, :, lanes] for k in range(5)]
    if real is not None:
        values = [jnp.where(real, v, 0.0) for v in values]
    return mix(splat, 1, values)


def wall_rows(splat, raw, out):
    for q in range(out.shape[-1] // LANES):
        lanes = slice(q * LANES, (q + 1) * LANES)
        mixed = mix(splat, 0, [raw[k, :, lanes] for k in range(5)])
        for i in range(5):
            out[4 * i : 4 * i + 4, lanes] = mixed[i][:4]


def for_lanes(body, length):
    @pl.loop(0, length // LANES)
    def _(q):
        body(pl.ds(pl.multiple_of(q * LANES, LANES), LANES))


def picked_sums(hot, rows):
    hot = hot.astype(jnp.bfloat16)
    high = rows.astype(jnp.bfloat16)
    rest = rows - high.astype(F32)
    middle = rest.astype(jnp.bfloat16)
    low = (rest - middle.astype(F32)).astype(jnp.bfloat16)
    return total([jnp.dot(hot, part, preferred_element_type=F32) for part in (low, middle, high)])


def hot_rows(owner, slot, tiles, cells=range(4)):
    ids = lax.broadcasted_iota(jnp.int32, (8, LANES), 1)
    hot = []
    for s in cells:
        named = owner[s] * 4 + slot[s]
        hot += [jnp.where(named[:, q : q + 1] == ids, 1.0, 0.0) for q in range(tiles)]
    return jnp.concatenate(hot, axis=0)


def first_edge_kernel(
    wall_in, span_in, owner_in, slot_in, rhs_in, jinv_in,
    edge_b, edge_a, splat, onehot_t,
    wall, span, owner, slot, rhs, jinv, small_sems, sems,
):
    _, plane_a, plane_b, _ = position()
    outer = ((plane_b, edge_b), (plane_a, edge_a))
    small = [
        pltpu.make_async_copy(source, here, small_sems.at[n])
        for n, (source, here) in enumerate(((wall_in, wall), (span_in, span), (owner_in, owner), (slot_in, slot)))
    ]
    copies = [
        pltpu.make_async_copy(source.at[plane], here.at[m], sems.at[n, m])
        for m, (plane, _) in enumerate(outer)
        for n, (source, here) in enumerate(((rhs_in, rhs), (jinv_in, jinv)))
    ]
    for copy in small + copies:
        copy.start()
    small[0].wait()
    small[1].wait()
    for which, coupling in enumerate((wall, span)):
        for k in range(5):
            for i in range(5):
                splat[which, k, i] = jnp.full((8, LANES), coupling[k, i], F32)
    small[2].wait()
    small[3].wait()
    onehot_t[...] = hot_rows(owner, slot, rhs.shape[-1] // LANES).T[: onehot_t.shape[0]]
    for m, (_, edge) in enumerate(outer):
        copies[2 * m].wait()
        copies[2 * m + 1].wait()

        def body(lanes, m=m, edge=edge):
            swept = sweep(jinv, m, lanes, [rhs[m, k, :, lanes] for k in range(5)])
            for k in range(5):
                edge[k, :, lanes] = swept[k]

        for_lanes(body, rhs.shape[-1])


def first_inner_kernel(splat, edge_b, edge_a, rhs_in, jinv_in, rhs, first, edge_w, raw, jinv, sems):
    slabs = [pltpu.make_async_copy(jinv_in.at[1 + m], jinv.at[m], sems.at[m]) for m in range(2)]
    sides = [pltpu.make_async_copy(rhs_in.at[s], rhs.at[s], sems.at[2 + s]) for s in range(4)]
    for copy in (sides[1], slabs[0], sides[2], slabs[1], sides[0], sides[3]):
        copy.start()
    even, _, _, row = position()
    for k in range(5):
        first[0, k] = jnp.where(even, edge_b[k], edge_a[k])
        first[3, k] = jnp.where(even, edge_a[k], edge_b[k])
    for s in (1, 2):
        sides[s].wait()
        slabs[s - 1].wait()

        def body(lanes, s=s):
            swept = sweep(jinv, s - 1, lanes, [rhs[s, k, :, lanes] for k in range(5)])
            for k in range(5):
                first[s, k, :, lanes] = swept[k]

        for_lanes(body, rhs.shape[-1])
    for s in range(4):
        for k in range(5):
            raw[k, s, :] = first[s, k, row, :]
    wall_rows(splat, raw, edge_w)
    sides[0].wait()
    sides[3].wait()


def local_apply(splat, planes, jac, lanes, s):
    own = planes[s]
    rows = lax.broadcasted_iota(jnp.int32, own[0].shape, 0)
    near_wall, near_span = [], []
    for k in range(5):
        up = jnp.where(rows == 7, 0.0, pltpu.roll(own[k], 7, 0))
        down = jnp.where(rows == 0, 0.0, pltpu.roll(own[k], 1, 0))
        near_wall.append(up + down)
        near_span.append(total([planes[n][k] for n in (s - 1, s + 1) if 0 <= n < 4]))
    from_wall, from_span = mix(splat, 0, near_wall), mix(splat, 1, near_span)
    return [
        total([jac[s, k, i, :, lanes] * own[k] for k in range(5)]) - (from_wall[i] + from_span[i])
        for i in range(5)
    ]


def with_wall(rest, halo_w, s, lanes, row):
    rows = lax.broadcasted_iota(jnp.int32, (8, LANES), 0)
    return [
        rest[s, i, :, lanes] + jnp.where(rows == row, halo_w[4 * i + s, lanes][None, :], 0.0) for i in range(5)
    ]


def first_residual_kernel(splat, first, rhs, jac, rest):
    def body(lanes):
        planes = [[first[n, k, :, lanes] for k in range(5)] for n in range(4)]
        for s in range(4):
            applied = local_apply(splat, planes, jac, lanes, s)
            for k in range(5):
                rest[s, k, :, lanes] = rhs[s, k, :, lanes] - applied[k]

    for_lanes(body, rhs.shape[-1])


def second_local_kernel(first, rest, halo_w, jinv, inner):
    row = position()[3]

    def body(lanes):
        for s in range(4):
            swept = sweep(jinv, s, lanes, with_wall(rest, halo_w, s, lanes, row))
            for k in range(5):
                inner[s, k, :, lanes] = first[s, k, :, lanes] + swept[k]

    for_lanes(body, rest.shape[-1])


def second_edge_kernel(splat, inner, halo_b, halo_a, jinv, edge_b, edge_a):
    _, plane_a, plane_b, _ = position()
    real = inside()

    def body(lanes):
        for plane, halo, edge, there in ((plane_b, halo_b, edge_b, real), (plane_a, halo_a, edge_a, None)):
            swept = sweep(jinv, plane, lanes, beyond_span(splat, halo, lanes, there))
            for k in range(5):
                edge[k, :, lanes] = inner[plane, k, :, lanes] + swept[k]

    for_lanes(body, inner.shape[-1])


def second_wall_kernel(splat, inner, edge_b, edge_a, edge_w, raw):
    even, _, _, row = position()
    for k in range(5):
        for s in (1, 2):
            raw[k, s, :] = inner[s, k, row, :]
        a, b = edge_a[k, row, :], edge_b[k, row, :]
        raw[k, 0, :] = jnp.where(even, b, a)
        raw[k, 3, :] = jnp.where(even, a, b)
    wall_rows(splat, raw, edge_w)


def planes_of(even, inner, edge_a, edge_b, lanes):
    a = [edge_a[k, :, lanes] for k in range(5)]
    b = [edge_b[k, :, lanes] for k in range(5)]
    return [
        [jnp.where(even, b[k], a[k]) for k in range(5)],
        [inner[1, k, :, lanes] for k in range(5)],
        [inner[2, k, :, lanes] for k in range(5)],
        [jnp.where(even, a[k], b[k]) for k in range(5)],
    ]


def second_residual_kernel(splat, inner, edge_b, edge_a, rhs, jac, rest):
    even = position()[0]

    def body(lanes):
        planes = planes_of(even, inner, edge_a, edge_b, lanes)
        for s in range(4):
            applied = local_apply(splat, planes, jac, lanes, s)
            for k in range(5):
                rest[s, k, :, lanes] = rhs[s, k, :, lanes] - applied[k]

    for_lanes(body, rhs.shape[-1])


def defect_local_kernel(inner, edge_b, edge_a, rest, halo_w, jinv, onehot_t, partial, base_out, base, defect, sems):
    even, _, _, row = position()

    def body(lanes):
        planes = planes_of(even, inner, edge_a, edge_b, lanes)
        for s in range(4):
            known = with_wall(rest, halo_w, s, lanes, row)
            swept = sweep(jinv, s, lanes, known)
            for k in range(5):
                base[s, k, :, lanes] = planes[s][k] + swept[k]
                defect[s, k, :, lanes] = known[k]

    for_lanes(body, rest.shape[-1])
    store = pltpu.make_async_copy(base, base_out, sems.at[0])
    store.start()
    tiles = defect.shape[-1] // LANES
    for k in range(5):
        rows = jnp.concatenate(
            [defect[s, k, :, q * LANES : (q + 1) * LANES] for s in range(4) for q in range(tiles)], axis=0
        )
        partial[:, k * LANES : (k + 1) * LANES] = picked_sums(onehot_t[...], rows)
    store.wait()


def restrict_kernel(splat, inner, halo_b, halo_a, onehot_t, partial, late_out, sems):
    real = inside()
    at_a = 1 - lax.rem(lax.axis_index("span"), 2)
    stores = [
        pltpu.make_async_copy(halo_b, late_out.at[1 - at_a], sems.at[0]),
        pltpu.make_async_copy(halo_a, late_out.at[at_a], sems.at[1]),
    ]
    for store in stores:
        store.start()
    tiles = halo_a.shape[-1] // LANES
    parts = []
    for halo, there in ((halo_b, real), (halo_a, None)):
        for q in range(tiles):
            parts.append(beyond_span(splat, halo, slice(q * LANES, (q + 1) * LANES), there))
    width = 8 * tiles
    even = at_a == 1
    low, high = onehot_t[:, :width], onehot_t[:, 3 * width :]
    hot = jnp.concatenate([jnp.where(even, low, high), jnp.where(even, high, low)], axis=1)
    slots = partial.shape[1]
    rows = jnp.concatenate([jnp.concatenate(part, axis=1) for part in parts], axis=0)
    sums = inner[...] + picked_sums(hot, rows)
    for p in range(partial.shape[0]):
        partial[p] = sums[p * slots : (p + 1) * slots]
    for store in stores:
        store.wait()


def sum_kernel(received, sums):
    sums[...] = total([received[p] for p in range(received.shape[0])])


def coarse_kernel(inv, own, other, out):
    first_group = lax.axis_index("wall") == 0
    groups = [
        [jnp.where(first_group, x[:, k * LANES : (k + 1) * LANES], y[:, k * LANES : (k + 1) * LANES]) for k in range(5)]
        for x, y in ((own, other), (other, own))
    ]
    for i in range(5):
        rows = inv[i]
        fix = total([rows[:, c * 5 + k : c * 5 + k + 1] * groups[c][k] for c in range(2) for k in range(5)])
        for p in range(out.shape[0]):
            out[p, :, i * LANES : (i + 1) * LANES] = fix


def prolonged(owner, slot, fixes, fix, tiles, cells):
    owners, slots, _ = fixes.shape
    for p in range(owners):
        fix[p * slots : (p + 1) * slots, :] = fixes[p]
    hot = hot_rows(owner, slot, tiles, cells)[:, : owners * slots]
    rows = [picked_sums(hot, fix[:, k * LANES : (k + 1) * LANES]) for k in range(5)]
    return lambda k, n, q: rows[k][(n * tiles + q) * 8 : (n * tiles + q) * 8 + 8]


def prolong_edge_kernel(owner, slot, fixes, edge_b, edge_a, fix):
    even = position()[0]
    tiles = edge_a.shape[-1] // LANES
    tile = prolonged(owner, slot, fixes, fix, tiles, (0, 3))
    for k in range(5):
        for q in range(tiles):
            lanes = slice(q * LANES, (q + 1) * LANES)
            low, high = tile(k, 0, q), tile(k, 1, q)
            edge_b[k, :, lanes] = jnp.where(even, low, high)
            edge_a[k, :, lanes] = jnp.where(even, high, low)


def prolong_inner_kernel(splat, owner, slot, fixes, edge_b, edge_a, out, edge_w, fix, raw):
    even, _, _, row = position()
    tiles = out.shape[-1] // LANES
    tile = prolonged(owner, slot, fixes, fix, tiles, (1, 2))
    for k in range(5):
        out[0, k] = jnp.where(even, edge_b[k], edge_a[k])
        out[3, k] = jnp.where(even, edge_a[k], edge_b[k])
        for n in range(2):
            for q in range(tiles):
                out[1 + n, k, :, q * LANES : (q + 1) * LANES] = tile(k, n, q)
    for k in range(5):
        for s in range(4):
            raw[k, s, :] = out[s, k, row, :]
    wall_rows(splat, raw, edge_w)


def final_residual_kernel(splat, fix, jac, base_in, late_in, rest, base, late, sems):
    loads = [pltpu.make_async_copy(base_in, base, sems.at[0]), pltpu.make_async_copy(late_in, late, sems.at[1])]
    for load in loads:
        load.start()

    def body(lanes):
        planes = [[fix[n, k, :, lanes] for k in range(5)] for n in range(4)]
        for s in range(4):
            applied = local_apply(splat, planes, jac, lanes, s)
            for k in range(5):
                rest[s, k, :, lanes] = -applied[k]

    for_lanes(body, fix.shape[-1])
    for load in loads:
        load.wait()


def final_local_kernel(splat, fix, rest, halo_w, jinv, base, late, inner, out, sems):
    row = position()[3]
    at, size = lax.axis_index("span"), lax.axis_size("span")
    there = {0: at > 0, 3: at < size - 1}
    store = pltpu.make_async_copy(inner.at[pl.ds(1, 2)], out.at[pl.ds(1, 2)], sems.at[0])
    for cells in ((1, 2), (0, 3)):

        def body(lanes, cells=cells):
            for s in cells:
                known = with_wall(rest, halo_w, s, lanes, row)
                if s in there:
                    beyond = beyond_span(splat, late.at[s // 3], lanes, there[s])
                    known = [known[k] + beyond[k] for k in range(5)]
                swept = sweep(jinv, s, lanes, known)
                for k in range(5):
                    inner[s, k, :, lanes] = (base[s, k, :, lanes] + fix[s, k, :, lanes]) + swept[k]

        for_lanes(body, fix.shape[-1])
        if cells == (1, 2):
            store.start()
    store.wait()


def final_edge_kernel(splat, inner, halo_b, halo_a, jinv, out_had, out, edges, sems):
    del out_had
    _, plane_a, plane_b, _ = position()
    real = inside()
    stores = []
    for n, (plane, halo, there) in enumerate(((plane_b, halo_b, real), (plane_a, halo_a, None))):

        def body(lanes, n=n, plane=plane, halo=halo, there=there):
            swept = sweep(jinv, plane, lanes, beyond_span(splat, halo, lanes, there))
            for k in range(5):
                edges[n, k, :, lanes] = inner[plane, k, :, lanes] + swept[k]

        for_lanes(body, inner.shape[-1])
        stores.append(pltpu.make_async_copy(edges.at[n], out.at[plane], sems.at[n]))
        stores[-1].start()
    for store in stores:
        store.wait()


def exchange(edge_a, edge_b, edge_w):
    size = lax.axis_size("span")
    even = [p for i in range(0, size, 2) for p in ((i, i + 1), (i + 1, i))]
    odd = [((i + 1) % size, (j + 1) % size) for i, j in even]
    halo_b = lax.ppermute(edge_b, "span", odd)
    halo_w = lax.ppermute(edge_w, "wall", [(0, 1), (1, 0)])
    halo_a = lax.ppermute(edge_a, "span", even)
    return halo_a, halo_b, halo_w


def local(rhs, jac, jac_inv, wall_coupling, span_coupling, block_owner, block_slot, coarse_inv):
    rhs = in_hbm(rhs.transpose(0, 2, 1, 3))
    jac_in = jac.transpose(0, 2, 3, 1, 4)
    jinv_in = jac_inv.transpose(0, 2, 3, 1, 4)
    inv = coarse_inv[0, 0].transpose(0, 2, 1)
    field, plane, edge = shaped(*rhs.shape), shaped(*rhs.shape[1:]), shaped(20, rhs.shape[-1])
    field_out = pltpu.HBM(rhs.shape, F32)
    outer = pltpu.VMEM((2, *rhs.shape[1:]), F32)
    raw = pltpu.VMEM(rhs.shape[1:], F32)
    owners, slots = lax.axis_size("patch"), coarse_inv.shape[-1]
    aggregates, columns = owners * slots, 5 * LANES
    chunks = shaped(owners, slots, columns)

    rhs_in = rhs
    b, a, splat, onehot_t = call(
        first_edge_kernel,
        [plane, plane, shaped(2, 5, 5, 8, LANES), shaped(aggregates, block_owner.size)],
        [in_hbm(x) for x in (wall_coupling, span_coupling, block_owner, block_slot, rhs_in, jinv_in)],
        places=[HBM] * 6,
        scratch=[
            pltpu.SMEM(wall_coupling.shape, F32),
            pltpu.SMEM(span_coupling.shape, F32),
            pltpu.VMEM(block_owner.shape, jnp.int32),
            pltpu.VMEM(block_owner.shape, jnp.int32),
            outer,
            pltpu.VMEM((2, *jinv_in.shape[1:]), F32),
            pltpu.SemaphoreType.DMA((4,)),
            pltpu.SemaphoreType.DMA((2, 2)),
        ],
    )
    rhs, first, w = call(
        first_inner_kernel,
        [field, field, edge],
        [splat, b, a, rhs_in, in_hbm(jinv_in)],
        places=[VMEM] * 3 + [HBM] * 2,
        scratch=[raw, pltpu.VMEM((2, *jinv_in.shape[1:]), F32), pltpu.SemaphoreType.DMA((6,))],
    )
    halo_a, halo_b, halo_w = exchange(a, b, w)
    [rest] = call(first_residual_kernel, [field], [splat, first, rhs, jac_in])
    [inner] = call(second_local_kernel, [field], [first, rest, halo_w, jinv_in])
    b, a = call(second_edge_kernel, [plane, plane], [splat, inner, halo_b, halo_a, jinv_in])
    [w] = call(second_wall_kernel, [edge], [splat, inner, b, a], scratch=[raw])
    halo_a, halo_b, halo_w = exchange(a, b, w)
    [rest] = call(second_residual_kernel, [field], [splat, inner, b, a, rhs, jac_in])
    partial, base = call(
        defect_local_kernel,
        [shaped(aggregates, columns), field_out],
        [inner, b, a, rest, halo_w, jinv_in, onehot_t],
        out_places=[VMEM, HBM],
        scratch=[pltpu.VMEM(rhs.shape, F32), pltpu.VMEM(rhs.shape, F32), pltpu.SemaphoreType.DMA((1,))],
    )
    partial, late = call(
        restrict_kernel,
        [chunks, pltpu.HBM((2, *plane.shape), F32)],
        [splat, partial, halo_b, halo_a, onehot_t],
        out_places=[VMEM, HBM],
        scratch=[pltpu.SemaphoreType.DMA((2,))],
    )
    received = lax.all_to_all(partial, "patch", split_axis=0, concat_axis=0, tiled=True)
    [mine] = call(sum_kernel, [shaped(slots, columns)], [received])
    theirs = lax.ppermute(mine, "wall", [(0, 1), (1, 0)])
    [reply] = call(coarse_kernel, [chunks], [inv, mine, theirs])
    fixes = lax.all_to_all(reply, "patch", split_axis=0, concat_axis=0, tiled=True)
    held = pltpu.VMEM((aggregates, columns), F32)
    b, a = call(prolong_edge_kernel, [plane, plane], [block_owner, block_slot, fixes], scratch=[held])
    fix, w = call(
        prolong_inner_kernel, [field, edge], [splat, block_owner, block_slot, fixes, b, a], scratch=[held, raw]
    )
    halo_a, halo_b, halo_w = exchange(a, b, w)
    rest, base, late = call(
        final_residual_kernel,
        [field, field, shaped(2, *plane.shape)],
        [splat, fix, jac_in, in_hbm(base), in_hbm(late)],
        places=[VMEM] * 3 + [HBM] * 2,
        scratch=[pltpu.SemaphoreType.DMA((2,))],
    )
    inner, out = call(
        final_local_kernel,
        [field, field_out],
        [splat, fix, rest, halo_w, jinv_in, base, late],
        out_places=[VMEM, HBM],
        scratch=[pltpu.SemaphoreType.DMA((1,))],
    )
    [out] = call(
        final_edge_kernel,
        [field_out],
        [splat, inner, halo_b, halo_a, jinv_in, in_hbm(out)],
        places=[VMEM] * 5 + [HBM],
        out_places=[HBM],
        scratch=[outer, pltpu.SemaphoreType.DMA((2,))],
        aliases={5: 0},
    )
    return out.transpose(0, 2, 1, 3)


def solution(mesh):
    return jax.shard_map(
        local,
        mesh=mesh,
        in_specs=(
            P("span", "wall", None, "patch"),
            P("span", "wall", None, None, "patch"),
            P("span", "wall", None, None, "patch"),
            P(),
            P(),
            P("span", "wall", "patch"),
            P("span", "wall", "patch"),
            P("span", "wall", None, None, "patch"),
        ),
        out_specs=P("span", "wall", None, "patch"),
        check_vma=False,
    )
```
